32 devices in a mesh: dp: 8 (over y, x, core), tensor: 4 (over z).
Axes of the slice: x: 2, y: 2, z: 4, core: 2. Of those that a mesh axis runs over, the one named last changes fastest.
Arguments:
- tokens: bfloat16 [16384, 2048], P(('dp', 'tensor')), may hold values from -6 to 6
- upstream: bfloat16 [16384, 2048], P(('dp', 'tensor')), may hold values from -8 to 8
- lengths: int32 [8, 3], P('dp'), may hold values from 1 to 1024, 1792 in all within a row
- permutation: int32 [8, 2048], P('dp'), may hold values from 0 to 2047, each once within a row
- w_query: bfloat16 [2048, 2048], P('dp', 'tensor'), may hold values from -2 to 2
- w_key: bfloat16 [2048, 2048], P('dp', 'tensor'), may hold values from -2 to 2
- w_value: bfloat16 [2048, 2048], P('dp', 'tensor'), may hold values from -0.125 to 0.125
- w_out: bfloat16 [2048, 2048], P('tensor', 'dp'), may hold values from -2 to 2
- w_gate: bfloat16 [2048, 8192], P('dp', 'tensor'), may hold values from -0.125 to 0.125
- w_up: bfloat16 [2048, 8192], P('dp', 'tensor'), may hold values from -0.125 to 0.125
- w_down: bfloat16 [8192, 2048], P('tensor', 'dp'), may hold values from -2 to 2
- q_gain: float32 [2048], replicated, may hold values from 0.25 to 1.75
- k_gain: float32 [2048], replicated, may hold values from 0.25 to 1.75
- attn_gain: float32 [2048], replicated, may hold values from 0.25 to 1.75
- ffn_gain: float32 [2048], replicated, may hold values from 0.25 to 1.75
Outputs:
- layer_out: bfloat16 [16384, 2048], P(('dp', 'tensor'))
- tokens_grad: bfloat16 [16384, 2048], P(('dp', 'tensor'))
- w_query_grad: float32 [2048, 2048], P('dp', 'tensor')
- w_key_grad: float32 [2048, 2048], P('dp', 'tensor')
- w_value_grad: float32 [2048, 2048], P('dp', 'tensor')
- w_out_grad: float32 [2048, 2048], P('tensor', 'dp')
- w_gate_grad: float32 [2048, 8192], P('dp', 'tensor')
- w_up_grad: float32 [2048, 8192], P('dp', 'tensor')
- w_down_grad: float32 [8192, 2048], P('tensor', 'dp')
- q_gain_grad: float32 [2048], replicated
- k_gain_grad: float32 [2048], replicated
- attn_gain_grad: float32 [2048], replicated
- ffn_gain_grad: float32 [2048], replicated
The draws below stay inside these ranges and needn't reach their ends.
Inputs may be any that keep to these rules, and one draw needn't show every extreme that they name: Each group's row of lengths sums to 1792, and its longest sequence has 1024 tokens. `permutation`: each group's row holds every slot number once.
All inputs are finite; a program needn't handle non-finite values.
Results may differ from the reference program's by a relative error of at most 0.019.
The reference program's roundings to bfloat16 on the way count: a program that leaves them out, or rounds other values in their place, can miss the bound.
Values may be sent and summed in bfloat16 or wider, within the bound.
A program may use at most 320 MiB of HBM per device.

```python
import math
import jax
import jax.numpy as jnp
import numpy as np
from jax import lax

D = 2048
HEADS = 16
HDIM = 128
FF = 8192
TOK_GROUP = 2048
SEQS = 3
BLOCK = 512
MOST = 1024
FILLED = 1792
TOKENS = 16384
N_DP = 8


def scaled_matrix(key, row_count, col_count, fan_in):
    base_key, column_key = jax.random.split(key)
    column_place = jnp.arange(col_count, dtype=jnp.float32) / col_count
    spread = jax.random.uniform(column_key, (col_count,), jnp.float32)
    base_draw = jnp.clip(jax.random.normal(base_key, (row_count, col_count), jnp.float32), -4.0, 4.0)
    rising = jnp.power(3.0, column_place - 0.5)
    column_scale = rising * jnp.power(10.0, spread - 0.5) / 1.6
    return base_draw * column_scale[None, :] / jnp.sqrt(jnp.float32(fan_in))


def draw_w_query(key, part):
    return scaled_matrix(jax.random.fold_in(key, 11), D, D, D).astype(jnp.bfloat16)


def draw_w_key(key, part):
    return scaled_matrix(jax.random.fold_in(key, 12), D, D, D).astype(jnp.bfloat16)


def draw_w_out(key, part):
    return scaled_matrix(jax.random.fold_in(key, 13), D, D, D).astype(jnp.bfloat16)


def draw_w_down(key, part):
    return scaled_matrix(jax.random.fold_in(key, 14), FF, D, FF).astype(jnp.bfloat16)


def draw_upstream(key, part):
    base_key = jax.random.fold_in(jax.random.fold_in(key, 15), 0)
    row_place = jnp.arange(TOKENS, dtype=jnp.float32) / TOKENS
    base_draw = jnp.clip(jax.random.normal(base_key, (TOKENS, D), jnp.float32), -4.0, 4.0)
    rising = jnp.power(3.0, row_place - 0.5)
    return (base_draw * rising[:, None]).astype(jnp.bfloat16)


def block_scale(own_key, shape, pieces, low, top_value):
    gain = 1.0
    for dim, shards_of in pieces:
        heights = jax.random.uniform(jax.random.fold_in(jax.random.fold_in(own_key, 6), dim), (shards_of,), jnp.float32, low / len(pieces), top_value / len(pieces))
        gain = gain * jnp.repeat(jnp.exp(heights), shape[dim] // shards_of).reshape((-1,) + (1,) * (len(shape) - 1 - dim))
    return gain


def profile(amount, total, bound, lean):
    portions = [(1 << 20) // math.isqrt(standing ** lean) + 1 for standing in range(2, amount + 1)]
    spare, counts = total - bound - (amount - 1), [1] * (amount - 1)
    while spare > 0:
        movable = [i for i in range(amount - 1) if counts[i] < bound]
        whole, budget = sum([portions[i] for i in movable]), spare
        for i in movable:
            extra = min(bound - counts[i], max(1, budget * portions[i] // whole), spare)
            counts[i] = counts[i] + extra
            spare = spare - extra
    return np.array([bound] + counts)


def uneven(rng, count, total, most, skew):
    if count == 2:
        one = jax.random.randint(rng, (), max(1, total - most), min(most, total - 1) + 1)
        return jnp.stack([one, total - one])
    tallies = jnp.asarray(profile(count, total, most, skew), jnp.int32)
    couples = (count - 1) // 2
    giver, taker = tallies[1:1 + 2 * couples:2], tallies[2:2 + 2 * couples:2]
    room = jnp.minimum(giver - 1, most - taker)
    shifted = jax.random.randint(jax.random.fold_in(rng, 1), (couples,), 0, 1 << 20) % (room + 1)
    tallies = tallies.at[1:1 + 2 * couples:2].set(giver - shifted).at[2:2 + 2 * couples:2].set(taker + shifted)
    return tallies[jax.random.permutation(jax.random.fold_in(rng, 2), count)]


def gaussian(key, shape, scale, most, cuts=(), kind=jnp.bfloat16):
    result = scale * jax.random.normal(key, shape, jnp.float32)
    if cuts:
        result = result * block_scale(key, shape, cuts, -0.22, 0.18)
    return jnp.clip(result, -most, most).astype(kind)


def setup_inputs(seed: int = 0) -> dict:
    splits = jax.random.split(jax.random.key(seed), 16)
    tokens = gaussian(splits[0], (TOKENS, D), 1.0, 6.0, ((0, 32),))
    upstream = draw_upstream(jax.random.fold_in(splits[15], 71), 0)
    lengths = jax.vmap(lambda own: uneven(own, SEQS, FILLED, MOST, 1))(jax.random.split(splits[2], N_DP)).reshape((N_DP, SEQS)).astype(jnp.int32)
    permutation = jax.vmap(lambda own: jax.random.permutation(own, TOK_GROUP))(jax.random.split(splits[3], N_DP)).reshape((N_DP, TOK_GROUP)).astype(jnp.int32)
    w_query = draw_w_query(jax.random.fold_in(splits[15], 71), 0)
    w_key = draw_w_key(jax.random.fold_in(splits[15], 71), 0)
    w_value = gaussian(splits[6], (D, D), D ** -0.5, 0.125, ((0, 8), (1, 4)))
    w_out = draw_w_out(jax.random.fold_in(splits[15], 71), 0)
    w_gate = gaussian(splits[8], (D, FF), D ** -0.5, 0.125, ((0, 8), (1, 4)))
    w_up = gaussian(splits[9], (D, FF), D ** -0.5, 0.125, ((0, 8), (1, 4)))
    w_down = draw_w_down(jax.random.fold_in(splits[15], 71), 0)
    q_gain = jnp.clip(1.0 + 0.15 * jax.random.normal(splits[11], (D,), jnp.float32), 0.25, 1.75)
    k_gain = jnp.clip(1.0 + 0.15 * jax.random.normal(splits[12], (D,), jnp.float32), 0.25, 1.75)
    attn_gain = jnp.clip(1.0 + 0.15 * jax.random.normal(splits[13], (D,), jnp.float32), 0.25, 1.75)
    ffn_gain = jnp.clip(1.0 + 0.15 * jax.random.normal(splits[14], (D,), jnp.float32), 0.25, 1.75)
    return {"tokens": tokens, "upstream": upstream, "lengths": lengths, "permutation": permutation, "w_query": w_query, "w_key": w_key, "w_value": w_value, "w_out": w_out, "w_gate": w_gate, "w_up": w_up, "w_down": w_down, "q_gain": q_gain, "k_gain": k_gain, "attn_gain": attn_gain, "ffn_gain": ffn_gain}


epsilon = 1e-06
rope_base = 500000.0
masked_score = -1e+30

@jax.custom_vjp
def low(v):
    return lax.optimization_barrier(v.astype(jnp.bfloat16)).astype(jnp.float32)

@jax.custom_vjp
def low_back(v):
    return v

def low_keep(v):
    return (low(v), None)

def low_pass(kept, grad):
    return (grad,)

def back_keep(v):
    return (v, None)

def back_low(kept, grad):
    return (low(grad),)
low.defvjp(low_keep, low_pass)
low_back.defvjp(back_keep, back_low)

def matmul(left, right):
    return jnp.dot(left, right, precision=lax.Precision.HIGHEST, preferred_element_type=jnp.float32)

def rms_scale(values, gain_vec):
    return values * lax.rsqrt(lax.optimization_barrier(jnp.mean(values * values, axis=-1, keepdims=True)) + epsilon) * gain_vec

def layout(length_row):
    positions = jnp.arange(TOK_GROUP, dtype=jnp.int32)
    seq_ends = jnp.cumsum(length_row).astype(jnp.int32)
    seq_starts = (seq_ends - length_row).astype(jnp.int32)
    segment = lax.optimization_barrier(jnp.sum((positions[:, None] >= seq_ends[None, :]).astype(jnp.int32), axis=1)).astype(jnp.int32)
    chosen = segment[:, None] == jnp.arange(SEQS, dtype=jnp.int32)[None, :]
    offsets = lax.optimization_barrier(jnp.sum(jnp.where(chosen, seq_starts[None, :], 0), axis=1)).astype(jnp.int32)
    return (segment, positions - offsets)

def rotary_tables(position):
    half_dim = HDIM // 2
    exponents = jnp.arange(half_dim, dtype=jnp.float32) * (2.0 / HDIM)
    frequency = jnp.power(jnp.float32(rope_base), -exponents)
    angles = position.astype(jnp.float32)[:, None] * frequency[None, :]
    return (jnp.cos(angles), jnp.sin(angles))

def rotate(values, cosine, sine_part):
    half_dim = HDIM // 2
    first_half = values[..., :half_dim]
    second_half = values[..., half_dim:]
    cos_rows = cosine[:, None, :]
    sin_rows = sine_part[:, None, :]
    return jnp.concatenate([first_half * cos_rows - second_half * sin_rows, second_half * cos_rows + first_half * sin_rows], axis=-1)

def allowed_block(segment, first_row, block_rows):
    query_seg = lax.dynamic_slice_in_dim(segment, first_row, block_rows)
    query_pos = first_row + jnp.arange(block_rows, dtype=jnp.int32)
    key_pos = jnp.arange(segment.shape[0], dtype=jnp.int32)
    same_seq = (query_seg[:, None] == segment[None, :]) & (query_seg[:, None] < SEQS) & (key_pos[None, :] <= query_pos[:, None])
    return same_seq | (key_pos[None, :] == query_pos[:, None])

def attend(q_b, k_b, v_b, segment):
    score_scale = 1.0 / float(HDIM) ** 0.5

    def one_block(block_index):
        first_row = (block_index * BLOCK).astype(jnp.int32)
        queries = lax.dynamic_slice_in_dim(q_b, first_row, BLOCK, 0)
        raw_scores = jnp.einsum('qhd,khd->hqk', queries, k_b, precision=lax.Precision.HIGHEST) * score_scale
        scores = low_back(raw_scores)
        allowed = allowed_block(segment, first_row, BLOCK)
        masked = jnp.where(allowed[None], scores, masked_score)
        row_peak = lax.optimization_barrier(jnp.max(masked, axis=-1, keepdims=True))
        exponent = jnp.exp(masked - row_peak)
        probs_f = exponent / lax.optimization_barrier(jnp.sum(exponent, axis=-1, keepdims=True))
        return jnp.einsum('hqk,khd->qhd', low(probs_f), v_b, precision=lax.Precision.HIGHEST)
    blocks = lax.map(jax.checkpoint(one_block), jnp.arange(TOK_GROUP // BLOCK, dtype=jnp.int32))
    return blocks.reshape(TOK_GROUP, HEADS * HDIM)

def group_layer(tokens_group, length_row, perm_row, params):
    w_query, w_key, w_value, w_out, w_gate, w_up, w_down, q_gain, k_gain, attn_gain, ffn_gain = params
    segment, position = layout(length_row)
    cosine, sine_part = rotary_tables(position)
    inverse = jnp.zeros((TOK_GROUP,), jnp.int32).at[perm_row].set(jnp.arange(TOK_GROUP, dtype=jnp.int32))
    q_raw = low_back(matmul(tokens_group, w_query))
    k_raw = low_back(matmul(tokens_group, w_key))
    v_raw = low_back(matmul(tokens_group, w_value))
    q_norm = rms_scale(q_raw, q_gain)
    k_norm = rms_scale(k_raw, k_gain)
    q_rot = rotate(q_norm[perm_row].reshape(TOK_GROUP, HEADS, HDIM), cosine, sine_part)
    k_rot = rotate(k_norm[perm_row].reshape(TOK_GROUP, HEADS, HDIM), cosine, sine_part)
    v_b = low(v_raw[perm_row]).reshape(TOK_GROUP, HEADS, HDIM)
    attn_f = low_back(attend(low(q_rot), low(k_rot), v_b, segment))
    attn_given = low(attn_f)[inverse]
    attn_out = low_back(matmul(attn_given, w_out))
    resid = tokens_group + rms_scale(attn_out, attn_gain)
    resid_b = low(resid)
    gate = low_back(matmul(resid_b, w_gate))
    up_part = low_back(matmul(resid_b, w_up))
    hidden_b = low(jax.nn.silu(gate) * up_part)
    mlp_out = low_back(matmul(hidden_b, w_down))
    return resid + rms_scale(mlp_out, ffn_gain)

def reference(tokens, upstream, lengths, permutation, w_query, w_key, w_value, w_out, w_gate, w_up, w_down, q_gain, k_gain, attn_gain, ffn_gain):
    params = (w_query.astype(jnp.float32), w_key.astype(jnp.float32), w_value.astype(jnp.float32), w_out.astype(jnp.float32), w_gate.astype(jnp.float32), w_up.astype(jnp.float32), w_down.astype(jnp.float32), q_gain.astype(jnp.float32), k_gain.astype(jnp.float32), attn_gain.astype(jnp.float32), ffn_gain.astype(jnp.float32))
    tokens_f = tokens.astype(jnp.float32).reshape(N_DP, TOK_GROUP, D)

    def forward(tokens_all, weight_set):

        def one_group(group_in):
            return group_layer(group_in[0], group_in[1], group_in[2], weight_set)
        return lax.map(jax.checkpoint(one_group), (tokens_all, lengths, permutation))
    layer_all, pullback = jax.vjp(forward, tokens_f, params)
    tokens_grad, grad_set = pullback(upstream.astype(jnp.float32).reshape(N_DP, TOK_GROUP, D))
    return (layer_all.reshape(TOKENS, D).astype(jnp.bfloat16), tokens_grad.reshape(TOKENS, D).astype(jnp.bfloat16), grad_set[0], grad_set[1], grad_set[2], grad_set[3], grad_set[4], grad_set[5], grad_set[6], grad_set[7], grad_set[8], grad_set[9], grad_set[10])
```

```python
import math

import jax
import jax.numpy as jnp
from jax import lax
from jax.sharding import Mesh, PartitionSpec as P

D = 2048
HDIM = 128

epsilon = 1e-06
rope_base = 500000.0
masked_score = -1e30

SWAP = [(0, 1), (1, 0)]
TURN = [(0, 0), (1, 2), (2, 1), (3, 3)]
CYCLE = [(0, 1), (1, 3), (3, 2), (2, 0)]
CYCLE_BACK = [(d, s) for s, d in CYCLE]
DP = ("a", "b", "core")
TENSOR = ("th", "tl")
RANK = ("core", "tl")


def swap(value, axis):
    return lax.ppermute(value, axis, SWAP)


def turn(value):
    return lax.ppermute(value, ("core", "th"), TURN)


def small_grid():
    return lax.axis_size("a") == 2 and lax.axis_size("tl") == 2


def part(value, dim, index, count):
    size = value.shape[dim] // count
    return lax.slice_in_dim(value, index * size, (index + 1) * size, axis=dim)


def gather_weight(shard, dim):
    first = turn(shard)
    second = lax.ppermute(shard, ("core", "th"), CYCLE)
    if not small_grid():
        upper = lax.axis_index("th") == 0
        pair = jnp.concatenate(
            [jnp.where(upper, first, second), jnp.where(upper, second, first)], axis=dim
        )
        return lax.all_gather(pair, ("a", "b"), axis=dim, tiled=True)
    first_b, first_a = swap(first, "b"), swap(first, "a")
    second_b, second_a = swap(second, "b"), swap(second, "a")
    first_d, second_d = swap(first_b, "a"), swap(second_a, "b")
    return jnp.concatenate(
        [first, second, first_b, second_b, first_a, second_a, first_d, second_d], axis=dim
    )


def scatter_weight(total, dim):
    total = total.astype(jnp.bfloat16)

    def add(left, right):
        return (left.astype(jnp.float32) + right.astype(jnp.float32)).astype(jnp.bfloat16)

    if not small_grid():
        pair = lax.psum_scatter(total, ("a", "b"), scatter_dimension=dim, tiled=True)
        upper = lax.axis_index("th") == 0
        low_part, high_part = part(pair, dim, 0, 2), part(pair, dim, 1, 2)
        first = jnp.where(upper, low_part, high_part)
        second = jnp.where(upper, high_part, low_part)
    else:
        blocks = [part(total, dim, index, 8) for index in range(8)]
        first, second, first_b, second_b, first_a, second_a, first_d, second_d = blocks
        first_b = add(first_b, swap(first_d, "a"))
        second_a = add(second_a, swap(second_d, "b"))
        first = (
            first.astype(jnp.float32)
            + swap(first_b, "b").astype(jnp.float32)
            + swap(first_a, "a").astype(jnp.float32)
        ).astype(jnp.bfloat16)
        second = (
            second.astype(jnp.float32)
            + swap(second_b, "b").astype(jnp.float32)
            + swap(second_a, "a").astype(jnp.float32)
        ).astype(jnp.bfloat16)
    return turn(first).astype(jnp.float32) + lax.ppermute(
        second, ("core", "th"), CYCLE_BACK
    ).astype(jnp.float32)


def swap_features(value):
    if not small_grid():
        return value
    size = value.shape[-1] // 8
    mask = 4 * lax.axis_index("a") + 2 * lax.axis_index("b") + lax.axis_index("th")
    return jnp.concatenate(
        [
            lax.dynamic_slice_in_dim(value, (index ^ mask) * size, size, axis=value.ndim - 1)
            for index in range(8)
        ],
        axis=value.ndim - 1,
    )


def row_place(row, own_rows):
    if not small_grid():
        return row
    mask = 2 * lax.axis_index("core") + lax.axis_index("tl")
    block = (row // own_rows) ^ mask
    block = (block // 2) + 2 * (block % 2)
    return block * own_rows + row % own_rows


def gather_rows(value):
    if not small_grid():
        return [lax.all_gather(value, RANK, axis=0, tiled=True)]
    far = swap(value, "tl")
    near_peer = swap(value, "core")
    far_peer = swap(far, "core")
    return [
        jnp.concatenate([value, near_peer], axis=0),
        jnp.concatenate([far, far_peer], axis=0),
    ]


def scatter_rows(pieces):
    if not small_grid():
        return lax.psum_scatter(
            pieces[0].astype(jnp.bfloat16), RANK, scatter_dimension=0, tiled=True
        ).astype(jnp.float32)
    near, far = pieces
    rows = near.shape[0] // 2
    far_peer = swap(far[rows:].astype(jnp.bfloat16), "core")
    far_sum = (far[:rows] + far_peer.astype(jnp.float32)).astype(jnp.bfloat16)
    from_far = swap(far_sum, "tl")
    near_peer = swap(near[rows:].astype(jnp.bfloat16), "core")
    return near[:rows] + near_peer.astype(jnp.float32) + from_far.astype(jnp.float32)


def sum_over(value, axes):
    for axis in axes:
        if lax.axis_size(axis) == 2:
            value = value + swap(value, axis)
        else:
            value = lax.psum(value, axis)
    return value


def layout(length_row, group_rows):
    count = length_row.shape[0]
    positions = jnp.arange(group_rows, dtype=jnp.int32)
    start = jnp.int32(0)
    segment = jnp.zeros((group_rows,), jnp.int32)
    offset = jnp.zeros((group_rows,), jnp.int32)
    for index in range(count):
        end = start + length_row[index]
        inside = (positions >= start) & (positions < end)
        offset = jnp.where(inside, start, offset)
        segment = segment + (positions >= end).astype(jnp.int32)
        start = end
    return (segment, positions - offset)


def rotary_tables(position):
    half_dim = HDIM // 2
    exponents = jnp.arange(half_dim, dtype=jnp.float32) * (2.0 / HDIM)
    frequency = jnp.power(jnp.float32(rope_base), -exponents)
    angles = position.astype(jnp.float32)[:, None] * frequency[None, :]
    return (jnp.cos(angles), jnp.sin(angles))


def rotate(values, cosine, sine_part):
    half_dim = HDIM // 2
    first_half = values[..., :half_dim]
    second_half = values[..., half_dim:]
    cos_rows = cosine[:, None, :]
    sin_rows = sine_part[:, None, :]
    return jnp.concatenate(
        [
            first_half * cos_rows - second_half * sin_rows,
            second_half * cos_rows + first_half * sin_rows,
        ],
        axis=-1,
    )


def allowed_block(segment, first_row, block_rows, seq_count):
    query_seg = lax.dynamic_slice_in_dim(segment, first_row, block_rows)
    query_pos = first_row + jnp.arange(block_rows, dtype=jnp.int32)
    key_pos = jnp.arange(segment.shape[0], dtype=jnp.int32)
    same_seq = (
        (query_seg[:, None] == segment[None, :])
        & (query_seg[:, None] < seq_count)
        & (key_pos[None, :] <= query_pos[:, None])
    )
    return same_seq | (key_pos[None, :] == query_pos[:, None])


def dot(left, right):
    return jnp.dot(left, right, preferred_element_type=jnp.float32)


def contract_rows(left, right):
    return lax.dot_general(
        left, right, (((0,), (0,)), ((), ())), preferred_element_type=jnp.float32
    )


def contract_cols(left, right):
    return lax.dot_general(
        left, right, (((1,), (1,)), ((), ())), preferred_element_type=jnp.float32
    )


def rms_back(values, rstd, gain_vec, grad):
    scaled = grad * gain_vec
    row_dots = jnp.sum(values * scaled, axis=1, keepdims=True)
    return rstd * scaled - values * (rstd * rstd * rstd) * row_dots / D


def per_device(
    tokens,
    upstream,
    lengths,
    permutation,
    w_query,
    w_key,
    w_value,
    w_out,
    w_gate,
    w_up,
    w_down,
    q_gain,
    k_gain,
    attn_gain,
    ffn_gain,
):
    rank = lax.axis_index("core") * lax.axis_size("tl") + lax.axis_index("tl")
    own_rows = tokens.shape[0]
    group_rows = own_rows * 2 * lax.axis_size("tl")
    local_width = w_query.shape[1]
    local_heads = local_width // HDIM
    score_scale = 1.0 / math.sqrt(HDIM)
    block_rows = min(512, group_rows)
    block_count = group_rows // block_rows
    seq_count = lengths.shape[1]

    own_group = lax.axis_index("core") == lax.axis_index("th")
    length_row = jnp.where(own_group, lengths, swap(lengths, "core"))[0]
    perm_row = jnp.where(own_group, permutation, swap(permutation, "core"))[0]

    tokens = swap_features(turn(tokens))
    qkv_full = gather_weight(jnp.concatenate([w_query, w_key, w_value], axis=1), 0)
    tokens_all = jnp.concatenate(gather_rows(tokens), axis=0)
    out_full = gather_weight(w_out, 1)
    gate_full = gather_weight(w_gate, 0)
    up_full = gather_weight(w_up, 0)
    down_full = gather_weight(w_down, 1)
    upstream = swap_features(turn(upstream))
    attn_gain = swap_features(attn_gain)
    ffn_gain = swap_features(ffn_gain)

    perm_row = row_place(perm_row, own_rows)
    slots = jnp.arange(group_rows, dtype=jnp.int32)
    inverse = jnp.zeros((group_rows,), jnp.int32).at[perm_row].set(slots)
    segment, position = layout(length_row, group_rows)
    cosine, sine_part = rotary_tables(position)

    packed = tokens_all[perm_row]
    projected = dot(packed, qkv_full)
    q_raw = projected[:, :local_width]
    k_raw = projected[:, local_width : 2 * local_width]
    v_raw = projected[:, 2 * local_width :]
    squares = sum_over(
        jnp.stack([jnp.sum(q_raw * q_raw, axis=1), jnp.sum(k_raw * k_raw, axis=1)]), RANK
    )
    rstd_q = lax.rsqrt(squares[0] / D + epsilon)[:, None]
    rstd_k = lax.rsqrt(squares[1] / D + epsilon)[:, None]
    gain_q = lax.dynamic_slice_in_dim(q_gain, rank * local_width, local_width)
    gain_k = lax.dynamic_slice_in_dim(k_gain, rank * local_width, local_width)
    q_norm = q_raw * rstd_q * gain_q
    k_norm = k_raw * rstd_k * gain_k
    q_b = rotate(q_norm.reshape(group_rows, local_heads, HDIM), cosine, sine_part).astype(
        jnp.bfloat16
    )
    k_b = rotate(k_norm.reshape(group_rows, local_heads, HDIM), cosine, sine_part).astype(
        jnp.bfloat16
    )
    v_b = v_raw.astype(jnp.bfloat16).reshape(group_rows, local_heads, HDIM)

    def forward_block(block_index):
        first_row = block_index * block_rows
        queries = lax.dynamic_slice_in_dim(q_b, first_row, block_rows, 0)
        scores = (
            jnp.einsum("qhd,khd->hqk", queries, k_b, preferred_element_type=jnp.float32)
            * score_scale
        )
        allowed = allowed_block(segment, first_row, block_rows, seq_count)
        masked = jnp.where(allowed[None], scores, masked_score)
        row_peak = jnp.max(masked, axis=-1, keepdims=True)
        exponent = jnp.exp(masked - row_peak)
        totals = jnp.sum(exponent, axis=-1, keepdims=True)
        probs_b = (exponent / totals).astype(jnp.bfloat16)
        attn_block = jnp.einsum("hqk,khd->qhd", probs_b, v_b, preferred_element_type=jnp.float32)
        return (attn_block.astype(jnp.bfloat16), (row_peak + jnp.log(totals))[..., 0])

    attn_blocks, log_totals = lax.map(forward_block, jnp.arange(block_count, dtype=jnp.int32))
    attn_given = attn_blocks.reshape(group_rows, local_width)[inverse]

    def pieces_of(value):
        if not small_grid():
            return [value]
        return [part(value, 0, 0, 2), part(value, 0, 1, 2)]

    attn_out = scatter_rows([dot(piece, out_full) for piece in pieces_of(attn_given)])
    rstd_a = lax.rsqrt(jnp.mean(attn_out * attn_out, axis=1, keepdims=True) + epsilon)
    resid = tokens.astype(jnp.float32) + attn_out * rstd_a * attn_gain
    resid_pieces = gather_rows(resid.astype(jnp.bfloat16))
    gates, ups, hiddens, sums = [], [], [], []
    for piece in resid_pieces:
        gate = dot(piece, gate_full)
        up_part = dot(piece, up_full)
        hidden_b = (gate * jax.nn.sigmoid(gate) * up_part).astype(jnp.bfloat16)
        gates.append(gate)
        ups.append(up_part)
        hiddens.append(hidden_b)
        sums.append(dot(hidden_b, down_full))
    mlp_out = scatter_rows(sums)
    rstd_m = lax.rsqrt(jnp.mean(mlp_out * mlp_out, axis=1, keepdims=True) + epsilon)
    normed_m = mlp_out * rstd_m
    layer_out = turn(swap_features((resid + normed_m * ffn_gain).astype(jnp.bfloat16)))

    grad_f = upstream.astype(jnp.float32)
    ffn_gain_part = jnp.sum(grad_f * normed_m, axis=0)
    d_mlp_b = rms_back(mlp_out, rstd_m, ffn_gain, grad_f).astype(jnp.bfloat16)
    d_mlp_pieces = gather_rows(d_mlp_b)
    d_gates, d_ups, sums = [], [], []
    for gate, up_part, d_mlp in zip(gates, ups, d_mlp_pieces):
        gate_sigmoid = jax.nn.sigmoid(gate)
        d_hidden = contract_cols(d_mlp, down_full)
        d_gate_b = (
            d_hidden * up_part * gate_sigmoid * (1.0 + gate * (1.0 - gate_sigmoid))
        ).astype(jnp.bfloat16)
        d_up_b = (d_hidden * gate * gate_sigmoid).astype(jnp.bfloat16)
        d_gates.append(d_gate_b)
        d_ups.append(d_up_b)
        sums.append(contract_cols(d_gate_b, gate_full) + contract_cols(d_up_b, up_full))
    d_resid = grad_f + scatter_rows(sums)

    def rows(pieces):
        return jnp.concatenate(pieces, axis=0)

    down_shard = scatter_weight(contract_rows(rows(hiddens), rows(d_mlp_pieces)), 1)
    gate_shard = scatter_weight(contract_rows(rows(resid_pieces), rows(d_gates)), 0)
    up_shard = scatter_weight(contract_rows(rows(resid_pieces), rows(d_ups)), 0)

    attn_gain_part = jnp.sum(d_resid * attn_out * rstd_a, axis=0)
    d_attn_b = rms_back(attn_out, rstd_a, attn_gain, d_resid).astype(jnp.bfloat16)
    d_attn_pieces = gather_rows(d_attn_b)
    d_attn_all = rows(d_attn_pieces)
    out_shard = scatter_weight(contract_rows(attn_given, d_attn_all), 1)
    d_given_b = rows([contract_cols(piece, out_full).astype(jnp.bfloat16) for piece in d_attn_pieces])
    d_packed = d_given_b[perm_row].reshape(group_rows, local_heads, HDIM)

    def backward_block(carried, block_in):
        key_acc, value_acc = carried
        block_index, log_rows = block_in
        first_row = block_index * block_rows
        queries = lax.dynamic_slice_in_dim(q_b, first_row, block_rows, 0)
        grad_rows = lax.dynamic_slice_in_dim(d_packed, first_row, block_rows, 0)
        scores = (
            jnp.einsum("qhd,khd->hqk", queries, k_b, preferred_element_type=jnp.float32)
            * score_scale
        )
        allowed = allowed_block(segment, first_row, block_rows, seq_count)
        probs_f = jnp.where(allowed[None], jnp.exp(scores - log_rows[..., None]), 0.0)
        probs_b = probs_f.astype(jnp.bfloat16)
        d_probs = jnp.einsum("qhd,khd->hqk", grad_rows, v_b, preferred_element_type=jnp.float32)
        row_delta = jnp.sum(probs_f * d_probs, axis=-1, keepdims=True)
        d_scores_b = (probs_f * (d_probs - row_delta)).astype(jnp.bfloat16)
        d_query = (
            jnp.einsum("hqk,khd->qhd", d_scores_b, k_b, preferred_element_type=jnp.float32)
            * score_scale
        )
        key_acc = (
            key_acc
            + jnp.einsum("hqk,qhd->khd", d_scores_b, queries, preferred_element_type=jnp.float32)
            * score_scale
        )
        value_acc = value_acc + jnp.einsum(
            "hqk,qhd->khd", probs_b, grad_rows, preferred_element_type=jnp.float32
        )
        return ((key_acc, value_acc), d_query)

    zero_acc = jnp.zeros((group_rows, local_heads, HDIM), jnp.float32)
    (d_key_rot, d_value), d_query_blocks = lax.scan(
        backward_block, (zero_acc, zero_acc), (jnp.arange(block_count, dtype=jnp.int32), log_totals)
    )
    d_query_rot = d_query_blocks.reshape(group_rows, local_heads, HDIM)
    d_q_norm = rotate(d_query_rot, cosine, -sine_part).reshape(group_rows, local_width)
    d_k_norm = rotate(d_key_rot, cosine, -sine_part).reshape(group_rows, local_width)
    d_v = d_value.reshape(group_rows, local_width)
    dots = sum_over(
        jnp.stack(
            [
                jnp.sum(q_raw * gain_q * d_q_norm, axis=1),
                jnp.sum(k_raw * gain_k * d_k_norm, axis=1),
            ]
        ),
        RANK,
    )
    d_q_raw = rstd_q * gain_q * d_q_norm - q_raw * (rstd_q * rstd_q * rstd_q) * dots[0][:, None] / D
    d_k_raw = rstd_k * gain_k * d_k_norm - k_raw * (rstd_k * rstd_k * rstd_k) * dots[1][:, None] / D
    q_gain_part = jnp.sum(d_q_norm * q_raw * rstd_q, axis=0)
    k_gain_part = jnp.sum(d_k_norm * k_raw * rstd_k, axis=0)
    d_qkv_b = jnp.concatenate([d_q_raw, d_k_raw, d_v], axis=1).astype(jnp.bfloat16)
    d_qkv_given = d_qkv_b[inverse]
    input_grad = scatter_rows(
        [contract_cols(piece, qkv_full) for piece in pieces_of(d_qkv_given)]
    )
    qkv_shard = scatter_weight(contract_rows(packed, d_qkv_b), 0)
    tokens_grad = turn(swap_features((d_resid + input_grad).astype(jnp.bfloat16)))

    def placed(part_sum):
        return lax.dynamic_update_slice_in_dim(
            jnp.zeros((D,), jnp.float32), part_sum, rank * local_width, 0
        )

    gain_grads = sum_over(
        jnp.stack(
            [
                placed(q_gain_part),
                placed(k_gain_part),
                swap_features(attn_gain_part),
                swap_features(ffn_gain_part),
            ]
        ),
        DP + TENSOR,
    )
    return (
        layer_out,
        tokens_grad,
        qkv_shard[:, :local_width],
        qkv_shard[:, local_width : 2 * local_width],
        qkv_shard[:, 2 * local_width :],
        out_shard,
        gate_shard,
        up_shard,
        down_shard,
        gain_grads[0],
        gain_grads[1],
        gain_grads[2],
        gain_grads[3],
    )


def solution(mesh):
    dp, tensor = mesh.shape["dp"], mesh.shape["tensor"]
    fine = Mesh(mesh.devices.reshape(dp // 4, 2, 2, 2, tensor // 2), DP + TENSOR)
    rows, weight, weight_out = P(DP + TENSOR, None), P(DP, TENSOR), P(TENSOR, DP)
    return jax.shard_map(
        per_device,
        mesh=fine,
        in_specs=(rows, rows, P(DP, None), P(DP, None))
        + (weight,) * 3
        + (weight_out, weight, weight, weight_out)
        + (P(),) * 4,
        out_specs=(rows, rows)
        + (weight,) * 3
        + (weight_out, weight, weight, weight_out)
        + (P(),) * 4,
        check_vma=False,
    )
```

```python
import functools
import math

import jax
import jax.numpy as jnp
from jax import lax
from jax.experimental import pallas as pl
from jax.experimental.pallas import tpu as pltpu
from jax.sharding import Mesh, PartitionSpec as P

D = 2048
HDIM = 128

epsilon = 1e-06
rope_base = 500000.0
masked_score = -1e30
BLOCK = 256
VMEM_BYTES = 48 * 1024 * 1024
MESH = pl.DeviceIdType.MESH

SWAP = [(0, 1), (1, 0)]
TURN = [(1, 2), (2, 1)]
CYCLE = [(0, 1), (1, 3), (3, 2), (2, 0)]
CYCLE_BACK = [(d, s) for s, d in CYCLE]
DP = ("a", "b", "core")
TENSOR = ("th", "tl")
RANK = ("core", "tl")


def swap(value, axis):
    return lax.ppermute(value, axis, SWAP)


def turn(value):
    stays = lax.axis_index("core") == lax.axis_index("th")
    return jnp.where(stays, value, lax.ppermute(value, ("core", "th"), TURN))


def small_grid():
    return lax.axis_size("a") == 2 and lax.axis_size("tl") == 2


def part(value, dim, index, count):
    size = value.shape[dim] // count
    return lax.slice_in_dim(value, index * size, (index + 1) * size, axis=dim)


def pieces_of_weight(shard):
    return turn(shard), lax.ppermute(shard, ("core", "th"), CYCLE)


def gather_weight(pieces):
    first, second = pieces
    upper = lax.axis_index("th") == 0
    pair = jnp.concatenate(
        [jnp.where(upper, first, second), jnp.where(upper, second, first)], axis=0
    )
    return lax.all_gather(pair, ("a", "b"), axis=0, tiled=True)


def finish_scatter(first, second):
    return turn(first).astype(jnp.float32) + lax.ppermute(
        second, ("core", "th"), CYCLE_BACK
    ).astype(jnp.float32)


def in_turn(low_part, high_part):
    upper = lax.axis_index("th") == 0
    return jnp.where(upper, low_part, high_part), jnp.where(upper, high_part, low_part)


def scatter_weight(total):
    pair = lax.psum_scatter(
        total.astype(jnp.bfloat16), ("a", "b"), scatter_dimension=0, tiled=True
    )
    return finish_scatter(*in_turn(part(pair, 0, 0, 2), part(pair, 0, 1, 2)))


def greet():
    a, b, core = lax.axis_index("a"), lax.axis_index("b"), lax.axis_index("core")
    th, tl = lax.axis_index("th"), lax.axis_index("tl")
    barrier = pltpu.get_barrier_semaphore()
    others = (
        {"a": 1 - a},
        {"b": 1 - b},
        {"core": 1 - core},
        {"tl": 1 - tl},
        {"th": 1 - th},
        {"core": 1 - core, "th": 1 - th},
    )
    for other in others:
        pl.semaphore_signal(barrier, inc=1, device_id=other, device_id_type=MESH)
    pl.semaphore_wait(barrier, len(others))


CHUNKS = 4


def entry_slots(plan):
    return 4 * CHUNKS + sum(3 * len(units) + 6 for units in plan)


def entry_kernel(plan, *refs):
    shard_count = sum(len(units) for units in plan)
    tokens, shards = refs[0], refs[1 : 1 + shard_count]
    tokens_all, fulls = refs[1 + shard_count], refs[2 + shard_count : -3]
    send, recv, local = refs[-3:]
    a, b, core = lax.axis_index("a"), lax.axis_index("b"), lax.axis_index("core")
    th, tl = lax.axis_index("th"), lax.axis_index("tl")
    stays = core == th
    greet()
    used = [0]

    def slots(count):
        used[0] += count
        return used[0] - count

    def remote(source, target, slot, to):
        return pltpu.make_async_remote_copy(
            src_ref=source,
            dst_ref=target,
            send_sem=send.at[slot],
            recv_sem=recv.at[slot],
            device_id=to,
            device_id_type=MESH,
        )

    def arrived(target, slot):
        remote(target, target, slot, {"core": 1 - core}).wait_recv()

    stages, taken = [], 0
    for full, units in zip(fulls, plan):
        stage = []
        for column in units:
            shard = shards[taken]
            base = slots(3)
            height, width = shard.shape

            def place(sub, full=full, column=column, height=height, width=width):
                row = pl.multiple_of((4 * a + 2 * b + sub) * height, height)
                return full.at[pl.ds(row, height), pl.ds(column, width)]

            stage.append((shard, place, base, taken))
            taken += 1
        stages.append(stage)

    def near_copy(shard, place, base):
        return remote(shard, place(core), base + 2, {"core": 1 - core})

    def far_copy(shard, place, base):
        return remote(shard, place(core), base + core, {"core": th, "th": 1 - th})

    def start_stage(stage):
        for shard, place, base, index in stage:
            far_copy(shard, place, base).start()

            @pl.when(stays)
            def _():
                pltpu.make_async_copy(shard, place(core), local.at[index]).start()

            @pl.when(jnp.logical_not(stays))
            def _():
                near_copy(shard, place, base).start()

    def finish_stage(stage):
        for shard, place, base, index in stage:

            @pl.when(stays)
            def _():
                pltpu.make_async_copy(shard, place(core), local.at[index]).wait()
                arrived(place(1 - core), base + 2)

            @pl.when(jnp.logical_not(stays))
            def _():
                arrived(place(0), base)
                arrived(place(1), base + 1)

    def piece(full, block_a, block_b, sub):
        height = full.shape[0] // 8
        row = pl.multiple_of((4 * block_a + 2 * block_b + sub) * height, height)
        return full.at[pl.ds(row, height), :]

    def ring(full, base):
        to_a, to_b = {"a": 1 - a}, {"b": 1 - b}
        return (
            [remote(piece(full, a, b, sub), piece(full, a, b, sub), base + sub, to_b) for sub in (0, 1)],
            [remote(piece(full, a, b, sub), piece(full, a, b, sub), base + 2 + sub, to_a) for sub in (0, 1)],
            remote(piece(full, a, 1 - b, 0), piece(full, a, 1 - b, 0), base + 4, to_a),
            remote(piece(full, 1 - a, b, 1), piece(full, 1 - a, b, 1), base + 5, to_b),
        )

    ring_base = [slots(6) for _ in fulls]

    def start_ring(index):
        over_b, over_a, _, _ = ring(fulls[index], ring_base[index])
        for copy in (over_b[0], over_a[1], over_b[1], over_a[0]):
            copy.start()

    def forward_ring(index):
        full, base = fulls[index], ring_base[index]
        arrived(piece(full, a, 1 - b, 0), base)
        ring(full, base)[2].start()
        arrived(piece(full, 1 - a, b, 1), base + 3)
        ring(full, base)[3].start()

    def finish_ring(index):
        full, base = fulls[index], ring_base[index]
        arrived(piece(full, a, 1 - b, 1), base + 1)
        arrived(piece(full, 1 - a, b, 0), base + 2)
        arrived(piece(full, 1 - a, 1 - b, 0), base + 4)
        arrived(piece(full, 1 - a, 1 - b, 1), base + 5)
        over_b, over_a, first, second = ring(full, base)
        for copy in (*over_b, *over_a, first, second):
            copy.wait_send()

    rows = tokens.shape[0]
    step = rows // CHUNKS
    row_base = slots(4 * CHUNKS)

    def rows_of(block_core, block_tl, chunk):
        row = pl.multiple_of((2 * block_core + block_tl) * rows + chunk * step, step)
        return tokens_all.at[pl.ds(row, step), :]

    def row_copies(chunk):
        slot = row_base + 4 * chunk
        own, other = rows_of(core, tl, chunk), rows_of(core, 1 - tl, chunk)
        return (
            remote(
                tokens.at[pl.ds(chunk * step, step), :],
                rows_of(th, tl, chunk),
                slot,
                {"core": th, "th": core},
            ),
            remote(own, own, slot + 1, {"tl": 1 - tl}),
            remote(own, own, slot + 2, {"core": 1 - core}),
            remote(other, other, slot + 3, {"core": 1 - core}),
        )

    def own_rows(chunk):
        return pltpu.make_async_copy(
            tokens.at[pl.ds(chunk * step, step), :],
            rows_of(core, tl, chunk),
            local.at[shard_count + chunk],
        )

    for chunk in range(CHUNKS):

        @pl.when(stays)
        def _():
            own_rows(chunk).start()

    start_stage(stages[0])
    start_stage(stages[1])
    finish_stage(stages[0])
    start_ring(0)
    for stage in stages[2:]:
        start_stage(stage)
    finish_stage(stages[1])
    start_ring(1)
    for chunk in range(CHUNKS):

        @pl.when(jnp.logical_not(stays))
        def _():
            row_copies(chunk)[0].start()

        @pl.when(stays)
        def _():
            own_rows(chunk).wait()
            row_copies(chunk)[1].start()
            row_copies(chunk)[2].start()

    forward_ring(0)
    forward_ring(1)
    for index in range(2, len(fulls)):
        finish_stage(stages[index])
        start_ring(index)
    for chunk in range(CHUNKS):

        @pl.when(jnp.logical_not(stays))
        def _():
            arrived(rows_of(core, tl, chunk), row_base + 4 * chunk)
            row_copies(chunk)[1].start()
            row_copies(chunk)[2].start()

        arrived(rows_of(core, 1 - tl, chunk), row_base + 4 * chunk + 1)
        row_copies(chunk)[3].start()
    for index in range(2, len(fulls)):
        forward_ring(index)
    for index in range(len(fulls)):
        finish_ring(index)
    for chunk in range(CHUNKS):
        arrived(rows_of(1 - core, tl, chunk), row_base + 4 * chunk + 2)
        arrived(rows_of(1 - core, 1 - tl, chunk), row_base + 4 * chunk + 3)

        @pl.when(jnp.logical_not(stays))
        def _():
            row_copies(chunk)[0].wait_send()

        for copy in row_copies(chunk)[1:]:
            copy.wait_send()
    for stage in stages:
        for shard, place, base, _ in stage:
            far_copy(shard, place, base).wait_send()

            @pl.when(jnp.logical_not(stays))
            def _():
                near_copy(shard, place, base).wait_send()


def leave_kernel(cuts, *refs):
    count = len(cuts)
    partial, resid, totals = refs[0], refs[1], refs[2 : 2 + count]
    outs = refs[2 + count : 2 + count + 1 + sum(len(cut) for cut in cuts)]
    rows_out, shard_outs = outs[0], outs[1:]
    scratch = refs[2 + count + len(outs) :]
    peer_far, peer_near, far_sum, from_far, done_rows = scratch[:5]
    boxes = [scratch[5 + 7 * index : 12 + 7 * index] for index in range(count)]
    send, recv, local = scratch[-3:]
    a, b, core = lax.axis_index("a"), lax.axis_index("b"), lax.axis_index("core")
    th, tl = lax.axis_index("th"), lax.axis_index("tl")
    stays = core == th
    to_a, to_b, to_core, to_tl = {"a": 1 - a}, {"b": 1 - b}, {"core": 1 - core}, {"tl": 1 - tl}
    greet()

    def remote(source, target, slot, to, send_slot=None):
        return pltpu.make_async_remote_copy(
            src_ref=source,
            dst_ref=target,
            send_sem=send.at[slot if send_slot is None else send_slot],
            recv_sem=recv.at[slot],
            device_id=to,
            device_id_type=MESH,
        )

    def arrived(target, slot):
        remote(target, target, slot, to_core).wait_recv()

    def add(target, target_row, height, *sources):
        step = 16

        def one(index, unused):
            value = None
            for source, first in sources:
                here = pl.ds(pl.multiple_of(first + index * step, step), step)
                term = source[here, :].astype(jnp.float32)
                value = term if value is None else value + term
            there = pl.ds(pl.multiple_of(target_row + index * step, step), step)
            target[there, :] = value.astype(target.dtype)
            return unused

        lax.fori_loop(0, height // step, one, 0)

    rows = resid.shape[0]
    step = rows // CHUNKS

    own, peer, far, peer_of_far = range(4)

    def row_of(block, chunk):
        return block * rows + chunk * step

    def at(ref, row):
        return ref.at[pl.ds(row, step), :]

    def row_copies(chunk):
        here = chunk * step
        return (
            remote(at(partial, row_of(peer_of_far, chunk)), at(peer_far, here), 4 * chunk, to_core),
            remote(at(partial, row_of(peer, chunk)), at(peer_near, here), 4 * chunk + 1, to_core),
            remote(at(far_sum, here), at(from_far, here), 4 * chunk + 2, to_tl),
            remote(at(done_rows, here), at(rows_out, here), 4 * chunk + 3, {"core": th, "th": core}),
        )

    def kept_rows(chunk):
        here = chunk * step
        return pltpu.make_async_copy(at(done_rows, here), at(rows_out, here), local.at[chunk])

    base = 4 * CHUNKS

    def piece(ref, block_a, block_b, sub):
        height = ref.shape[0] // 8
        return pl.multiple_of((4 * block_a + 2 * block_b + sub) * height, height), height

    def slice_of(ref, block_a, block_b, sub):
        row, height = piece(ref, block_a, block_b, sub)
        return ref.at[pl.ds(row, height), :]

    def copies(index):
        total = totals[index]
        over_a, over_b, send_b, send_a, from_b, from_a, _ = boxes[index]
        slot = base + 10 * index
        height = total.shape[0] // 8

        def half(ref, sub):
            return ref.at[pl.ds(sub * height, height), :]

        return (
            remote(slice_of(total, 1 - a, 1 - b, 0), over_a, slot, to_a),
            remote(slice_of(total, 1 - a, 1 - b, 1), over_b, slot + 1, to_b),
            remote(slice_of(total, a, 1 - b, 1), half(from_b, 1), slot + 2, to_b),
            remote(slice_of(total, 1 - a, b, 0), half(from_a, 0), slot + 3, to_a),
            remote(send_b, half(from_b, 0), slot + 4, to_b),
            remote(send_a, half(from_a, 1), slot + 5, to_a),
        )

    def last_copies(index):
        sums = boxes[index][6]
        slot = base + 10 * index + 6
        return (
            remote(sums.at[1 - core], sums.at[2], slot, to_core),
            remote(sums.at[0], sums.at[3], slot + 1, {"core": 0, "th": core}),
            remote(sums.at[1], sums.at[3], slot + 1, {"core": 1, "th": core}, slot + 2),
        )

    for index in range(count):
        for copy in copies(index)[:2]:
            copy.start()
    for chunk in range(CHUNKS):
        row_copies(chunk)[0].start()
    for index in range(count):
        for copy in copies(index)[2:4]:
            copy.start()
    for chunk in range(CHUNKS):
        row_copies(chunk)[1].start()
    for chunk in range(CHUNKS):
        arrived(at(peer_far, chunk * step), 4 * chunk)
        add(
            far_sum,
            chunk * step,
            step,
            (partial, row_of(far, chunk)),
            (peer_far, chunk * step),
        )
        row_copies(chunk)[2].start()
    for index in range(count):
        total = totals[index]
        over_a, over_b, send_b, send_a, _, _, _ = boxes[index]
        height = total.shape[0] // 8
        arrived(over_a, base + 10 * index)
        add(send_b, 0, height, (total, piece(total, a, 1 - b, 0)[0]), (over_a, 0))
        copies(index)[4].start()
        arrived(over_b, base + 10 * index + 1)
        add(send_a, 0, height, (total, piece(total, 1 - a, b, 1)[0]), (over_b, 0))
        copies(index)[5].start()
    for chunk in range(CHUNKS):
        here = chunk * step
        arrived(at(peer_near, here), 4 * chunk + 1)
        arrived(at(from_far, here), 4 * chunk + 2)
        add(
            done_rows,
            here,
            step,
            (partial, row_of(own, chunk)),
            (peer_near, here),
            (from_far, here),
            (resid, here),
        )

        @pl.when(stays)
        def _():
            kept_rows(chunk).start()

        @pl.when(jnp.logical_not(stays))
        def _():
            row_copies(chunk)[3].start()

    for index in range(count):
        total = totals[index]
        _, _, _, _, from_b, from_a, sums = boxes[index]
        height = total.shape[0] // 8
        slot = base + 10 * index
        for sub in (0, 1):
            arrived(from_b.at[pl.ds(sub * height, height), :], slot + (4 if sub == 0 else 2))
            arrived(from_a.at[pl.ds(sub * height, height), :], slot + (3 if sub == 0 else 5))
            add(
                sums.at[sub],
                0,
                height,
                (total, piece(total, a, b, sub)[0]),
                (from_b, sub * height),
                (from_a, sub * height),
            )
        near, zero, one = last_copies(index)

        @pl.when(stays)
        def _():
            near.start()

        @pl.when(jnp.logical_not(stays))
        def _():
            zero.start()
            one.start()

    taken = 0
    for index, cut in enumerate(cuts):
        total = totals[index]
        sums = boxes[index][6]
        slot = base + 10 * index + 6
        arrived(sums.at[3], slot + 1)

        @pl.when(jnp.logical_not(stays))
        def _():
            arrived(sums.at[2], slot)

        first = 0
        for end in cut:
            out = shard_outs[taken]
            taken += 1

            def one(step_index, unused, out=out, first=first, end=end, sums=sums):
                here = pl.ds(pl.multiple_of(step_index * 16, 16), 16)

                @pl.when(stays)
                def _():
                    out[here, :] = sums[core, here, first:end].astype(jnp.float32) + sums[
                        3, here, first:end
                    ].astype(jnp.float32)

                @pl.when(jnp.logical_not(stays))
                def _():
                    out[here, :] = sums[2, here, first:end].astype(jnp.float32) + sums[
                        3, here, first:end
                    ].astype(jnp.float32)

                return unused

            lax.fori_loop(0, out.shape[0] // 16, one, 0)
            first = end
    for chunk in range(CHUNKS):
        for copy in row_copies(chunk)[:3]:
            copy.wait_send()

        @pl.when(stays)
        def _():
            kept_rows(chunk).wait()

        @pl.when(jnp.logical_not(stays))
        def _():
            row_copies(chunk)[3].wait_send()
            arrived(at(rows_out, chunk * step), 4 * chunk + 3)

    for index in range(count):
        for copy in copies(index):
            copy.wait_send()
        near, zero, one = last_copies(index)

        @pl.when(stays)
        def _():
            near.wait_send()

        @pl.when(jnp.logical_not(stays))
        def _():
            zero.wait_send()
            one.wait_send()


def leave(partial, resid, totals):
    if not small_grid():
        summed, _ = scatter_rows([partial])
        shards = []
        for total, parts in totals:
            shard, first = scatter_weight(total), 0
            for width in parts:
                shards.append(shard[:, first : first + width])
                first += width
        return [turn((resid + summed).astype(jnp.bfloat16))] + shards
    rows, columns = resid.shape
    cuts, scratch, outs = [], [], [jax.ShapeDtypeStruct((rows, columns), jnp.bfloat16)]
    for total, parts in totals:
        height, width = total.shape[0] // 8, total.shape[1]
        cuts.append(tuple(sum(parts[: index + 1]) for index in range(len(parts))))
        outs += [jax.ShapeDtypeStruct((height, part_width), jnp.float32) for part_width in parts]
        for shape in [(height, width)] * 4 + [(2 * height, width)] * 2 + [(4, height, width)]:
            scratch.append(pltpu.VMEM(shape, jnp.bfloat16))
    slots = 4 * CHUNKS + 10 * len(totals)
    vmem = pl.BlockSpec(memory_space=pltpu.VMEM)
    return pl.pallas_call(
        functools.partial(leave_kernel, tuple(cuts)),
        in_specs=[vmem] * (2 + len(totals)),
        out_specs=[pl.BlockSpec(memory_space=pl.ANY)] + [vmem] * (len(outs) - 1),
        out_shape=outs,
        scratch_shapes=[pltpu.VMEM((rows, columns), jnp.bfloat16)] * 5
        + scratch
        + [
            pltpu.SemaphoreType.DMA((slots,)),
            pltpu.SemaphoreType.DMA((slots,)),
            pltpu.SemaphoreType.DMA((CHUNKS,)),
        ],
        compiler_params=pltpu.CompilerParams(
            collective_id=1, has_side_effects=True, vmem_limit_bytes=60 * 1024 * 1024
        ),
        cost_estimate=pl.CostEstimate(flops=0, bytes_accessed=1 << 27, transcendentals=0),
        name="leave",
    )(partial.astype(jnp.bfloat16), resid, *[total.astype(jnp.bfloat16) for total, _ in totals])


def enter(tokens, matrices):
    if not small_grid():
        own = turn(tokens)
        return [lax.all_gather(own, RANK, axis=0, tiled=True)] + [
            gather_weight(pieces_of_weight(jnp.concatenate(shards, axis=1))) for shards in matrices
        ]
    plan, outs = [], [jax.ShapeDtypeStruct((4 * tokens.shape[0], tokens.shape[1]), tokens.dtype)]
    for shards in matrices:
        columns = [0]
        for shard in shards:
            columns.append(columns[-1] + shard.shape[1])
        plan.append(tuple(columns[:-1]))
        outs.append(jax.ShapeDtypeStruct((8 * shards[0].shape[0], columns[-1]), tokens.dtype))
    flat = [shard for shards in matrices for shard in shards]
    slots = entry_slots(plan)
    anywhere = pl.BlockSpec(memory_space=pl.ANY)
    return pl.pallas_call(
        functools.partial(entry_kernel, tuple(plan)),
        in_specs=[anywhere] * (1 + len(flat)),
        out_specs=[anywhere] * len(outs),
        out_shape=outs,
        scratch_shapes=[
            pltpu.SemaphoreType.DMA((slots,)),
            pltpu.SemaphoreType.DMA((slots,)),
            pltpu.SemaphoreType.DMA((len(flat) + CHUNKS,)),
        ],
        compiler_params=pltpu.CompilerParams(collective_id=0, has_side_effects=True),
        cost_estimate=pl.CostEstimate(flops=0, bytes_accessed=1 << 27, transcendentals=0),
        name="enter",
    )(tokens, *flat)


def row_place(row, own_rows):
    if not small_grid():
        return row
    mask = 2 * lax.axis_index("core") + lax.axis_index("tl")
    block = (row // own_rows) ^ mask
    block = (block // 2) + 2 * (block % 2)
    return block * own_rows + row % own_rows


def gather_rows(value):
    if not small_grid():
        return [lax.all_gather(value, RANK, axis=0, tiled=True)]
    far = swap(value, "tl")
    near_peer = swap(value, "core")
    far_peer = swap(far, "core")
    return [
        jnp.concatenate([value, near_peer], axis=0),
        jnp.concatenate([far, far_peer], axis=0),
    ]


def scatter_rows(pieces, beside=()):
    if not small_grid():
        total = lax.psum_scatter(
            pieces[0].astype(jnp.bfloat16), RANK, scatter_dimension=0, tiled=True
        ).astype(jnp.float32)
        return total, beside
    near, far = pieces
    rows = near.shape[0] // 2
    far_peer = swap(far[rows:].astype(jnp.bfloat16), "core")
    far_sum = (far[:rows].astype(jnp.float32) + far_peer.astype(jnp.float32)).astype(jnp.bfloat16)
    from_far = swap(far_sum, "tl")
    near_peer = swap(near[rows:].astype(jnp.bfloat16), "core")
    from_far, beside = lax.optimization_barrier((from_far, beside))
    total = (
        near[:rows].astype(jnp.float32)
        + near_peer.astype(jnp.float32)
        + from_far.astype(jnp.float32)
    )
    return total, beside


def sum_over(value, axes):
    for axis in axes:
        if lax.axis_size(axis) == 2:
            value = value + swap(value, axis)
        else:
            value = lax.psum(value, axis)
    return value


def layout(length_row, group_rows):
    positions = jnp.arange(group_rows, dtype=jnp.int32)
    start = jnp.int32(0)
    offset = jnp.zeros((group_rows,), jnp.int32)
    starts = positions
    for index in range(length_row.shape[0]):
        end = start + length_row[index]
        inside = (positions >= start) & (positions < end)
        offset = jnp.where(inside, start, offset)
        starts = jnp.where(inside, start, starts)
        start = end
    return (positions - offset, starts)


def rotary_tables(position):
    half_dim = HDIM // 2
    exponents = jnp.arange(half_dim, dtype=jnp.float32) * (2.0 / HDIM)
    frequency = jnp.power(jnp.float32(rope_base), -exponents)
    angles = position.astype(jnp.float32)[:, None] * frequency[None, :]
    cosine, sine = jnp.cos(angles), jnp.sin(angles)
    return (
        jnp.concatenate([cosine, cosine], axis=1),
        jnp.concatenate([-sine, sine], axis=1),
    )


def columns_of(rows, index):
    chosen = (lax.broadcasted_iota(jnp.int32, (rows.shape[0], HDIM), 0) == index).astype(
        jnp.float32
    )
    return lax.dot_general(
        rows,
        chosen,
        (((0,), (0,)), ((), ())),
        precision=lax.Precision.HIGHEST,
        preferred_element_type=jnp.float32,
    )


def row_sums(values):
    ones = jnp.ones((8, values.shape[1]), jnp.float32)
    return lax.dot_general(
        ones,
        values,
        (((1,), (1,)), ((), ())),
        precision=lax.Precision.HIGHEST,
        preferred_element_type=jnp.float32,
    )[:1]


def rstd_of(squares, index):
    return lax.rsqrt(columns_of(squares, index) * (1.0 / D) + epsilon)


def prepare_kernel(raw, squares, gain_q, gain_k, cosine, sine, q_out, k_out, v_out):
    width = q_out.shape[1]
    table_c, table_s = cosine[...], sine[...]
    both = squares[...]
    for index, (gain, out) in enumerate(((gain_q, q_out), (gain_k, k_out))):
        rstd = rstd_of(both, index)
        for head in range(width // HDIM):
            cols = slice(head * HDIM, (head + 1) * HDIM)
            base = index * width + head * HDIM
            norm = raw[:, base : base + HDIM] * rstd * gain[:, cols]
            turned = norm * table_c + pltpu.roll(norm, HDIM // 2, 1) * table_s
            out[:, cols] = turned.astype(jnp.bfloat16)
    v_out[...] = raw[:, 2 * width :].astype(jnp.bfloat16)


def prepare(raw, squares, gain_q, gain_k, cosine, sine):
    rows, width = raw.shape[0], raw.shape[1] // 3
    whole = pl.BlockSpec((1, width), lambda i: (0, 0))
    table = pl.BlockSpec((BLOCK, HDIM), lambda i: (i, 0))
    out = pl.BlockSpec((BLOCK, width), lambda i: (i, 0))
    return pl.pallas_call(
        prepare_kernel,
        grid=(rows // BLOCK,),
        in_specs=[
            pl.BlockSpec((BLOCK, 3 * width), lambda i: (i, 0)),
            pl.BlockSpec((2, BLOCK), lambda i: (0, i)),
            whole,
            whole,
            table,
            table,
        ],
        out_specs=[out] * 3,
        out_shape=[jax.ShapeDtypeStruct((rows, width), jnp.bfloat16)] * 3,
        cost_estimate=pl.CostEstimate(
            flops=rows * width * 20, bytes_accessed=rows * width * 20, transcendentals=0
        ),
        name="prepare",
    )(raw, squares, gain_q[None], gain_k[None], cosine, sine)


def allowed_keys(starts, first_key, first_query):
    shape = (BLOCK, BLOCK)
    keys = first_key + lax.broadcasted_iota(jnp.int32, shape, 0)
    queries = first_query + lax.broadcasted_iota(jnp.int32, shape, 1)
    return (keys >= starts) & (keys <= queries)


def forward_kernel(low_ref, q_ref, k_ref, v_ref, start_ref, attn_ref, full_ref, log_ref):
    block = pl.program_id(1)
    queries = q_ref[...]
    starts = start_ref[...]
    scale = 1.0 / math.sqrt(HDIM)

    def step(index, carried):
        peak, total, acc = carried
        rows = pl.ds(pl.multiple_of(index * BLOCK, BLOCK), BLOCK)
        scores = contract_cols(k_ref[rows, :], queries) * scale
        scores = jnp.where(
            allowed_keys(starts, index * BLOCK, block * BLOCK), scores, masked_score
        )
        new_peak = jnp.maximum(peak, jnp.max(scores, axis=0, keepdims=True))
        fade = jnp.exp(peak - new_peak)
        weights = jnp.exp(scores - new_peak)
        total = total * fade + jnp.sum(weights, axis=0, keepdims=True)
        acc = acc * fade + contract_rows(v_ref[rows, :], weights.astype(jnp.bfloat16))
        return (new_peak, total, acc)

    start = (
        jnp.full((1, BLOCK), masked_score, jnp.float32),
        jnp.zeros((1, BLOCK), jnp.float32),
        jnp.zeros((HDIM, BLOCK), jnp.float32),
    )
    carried = step(block, start)
    peak, total, acc = lax.fori_loop(low_ref[block], block, step, carried)
    out = jnp.transpose(acc / total)
    full_ref[...] = out
    attn_ref[...] = out.astype(jnp.bfloat16)
    log_ref[...] = peak + jnp.log(total)


def attention_forward(q_b, k_b, v_b, starts, low_block):
    rows, width = q_b.shape
    heads = width // HDIM
    own = pl.BlockSpec((BLOCK, HDIM), lambda h, i, low: (i, h))
    whole = pl.BlockSpec((rows, HDIM), lambda h, i, low: (0, h))
    return pl.pallas_call(
        forward_kernel,
        grid_spec=pltpu.PrefetchScalarGridSpec(
            num_scalar_prefetch=1,
            grid=(heads, rows // BLOCK),
            in_specs=[own, whole, whole, pl.BlockSpec((1, BLOCK), lambda h, i, low: (0, i))],
            out_specs=[own, own, pl.BlockSpec((None, 1, BLOCK), lambda h, i, low: (h, 0, i))],
        ),
        out_shape=[
            jax.ShapeDtypeStruct((rows, width), jnp.bfloat16),
            jax.ShapeDtypeStruct((rows, width), jnp.float32),
            jax.ShapeDtypeStruct((heads, 1, rows), jnp.float32),
        ],
        compiler_params=pltpu.CompilerParams(vmem_limit_bytes=VMEM_BYTES),
        cost_estimate=pl.CostEstimate(
            flops=heads * rows * rows * HDIM, bytes_accessed=rows * width * 12, transcendentals=heads * rows * rows // 4
        ),
        name="attention_forward",
    )(low_block, q_b, k_b, v_b, starts)


def backward_kernel(
    high_ref, q_ref, k_ref, v_ref, grad_ref, full_ref, log_ref, start_ref, dq_ref, dk_ref, dv_ref, delta
):
    block = pl.program_id(1)
    blocks = pl.num_programs(1)
    scale = 1.0 / math.sqrt(HDIM)

    @pl.when(block == 0)
    def _():
        dq_ref[...] = jnp.zeros_like(dq_ref)

        def one(index, unused):
            rows = pl.ds(pl.multiple_of(index * BLOCK, BLOCK), BLOCK)
            delta[:, rows] = row_sums(grad_ref[rows, :].astype(jnp.float32) * full_ref[rows, :])
            return unused

        lax.fori_loop(0, blocks, one, 0)

    here = pl.ds(pl.multiple_of(block * BLOCK, BLOCK), BLOCK)
    keys, values = k_ref[here, :], v_ref[here, :]

    def step(index, carried):
        dk, dv = carried
        rows = pl.ds(pl.multiple_of(index * BLOCK, BLOCK), BLOCK)
        queries, grads = q_ref[rows, :], grad_ref[rows, :]
        scores = contract_cols(keys, queries) * scale
        allowed = allowed_keys(start_ref[:, rows], block * BLOCK, index * BLOCK)
        probs = jnp.where(allowed, jnp.exp(scores - log_ref[:, rows]), 0.0)
        dv = dv + dot(probs.astype(jnp.bfloat16), grads)
        d_probs = contract_cols(values, grads)
        d_scores = (probs * (d_probs - delta[:, rows])).astype(jnp.bfloat16)
        dk = dk + dot(d_scores, queries)
        dq_ref[rows, :] += contract_rows(d_scores, keys)
        return (dk, dv)

    zero = jnp.zeros((BLOCK, HDIM), jnp.float32)
    dk, dv = lax.fori_loop(block, high_ref[block] + 1, step, (zero, zero))
    dk_ref[...] = dk * scale
    dv_ref[...] = dv

    @pl.when(block == blocks - 1)
    def _():
        dq_ref[...] = dq_ref[...] * scale


def attention_backward(q_b, k_b, v_b, grads, full, logs, starts, high_block):
    rows, width = q_b.shape
    heads = width // HDIM
    own = pl.BlockSpec((BLOCK, HDIM), lambda h, i, high: (i, h))
    whole = pl.BlockSpec((rows, HDIM), lambda h, i, high: (0, h))
    out = jax.ShapeDtypeStruct((rows, width), jnp.float32)
    return pl.pallas_call(
        backward_kernel,
        grid_spec=pltpu.PrefetchScalarGridSpec(
            num_scalar_prefetch=1,
            grid=(heads, rows // BLOCK),
            in_specs=[whole] * 5
            + [
                pl.BlockSpec((None, 1, rows), lambda h, i, high: (h, 0, 0)),
                pl.BlockSpec((1, rows), lambda h, i, high: (0, 0)),
            ],
            out_specs=[whole, own, own],
            scratch_shapes=[pltpu.VMEM((1, rows), jnp.float32)],
        ),
        out_shape=[out] * 3,
        compiler_params=pltpu.CompilerParams(vmem_limit_bytes=VMEM_BYTES),
        cost_estimate=pl.CostEstimate(
            flops=heads * rows * rows * HDIM * 3, bytes_accessed=rows * width * 24, transcendentals=heads * rows * rows // 4
        ),
        name="attention_backward",
    )(high_block, q_b, k_b, v_b, grads, full, logs, starts)


def norm_grads_kernel(
    dq_ref, dk_ref, raw, squares, gain_q, gain_k, cosine, sine, dq_out, dk_out, dots, q_part, k_part
):
    width = dq_ref.shape[1]
    table_c, table_s = cosine[...], sine[...]
    both = squares[...]

    @pl.when(pl.program_id(0) == 0)
    def _():
        q_part[...] = jnp.zeros_like(q_part)
        k_part[...] = jnp.zeros_like(k_part)

    for index, (grad, gain, out, gain_part) in enumerate(
        ((dq_ref, gain_q, dq_out, q_part), (dk_ref, gain_k, dk_out, k_part))
    ):
        rstd = rstd_of(both, index)
        products = jnp.zeros((BLOCK, HDIM), jnp.float32)
        for head in range(width // HDIM):
            cols = slice(head * HDIM, (head + 1) * HDIM)
            base = index * width + head * HDIM
            turned = grad[:, cols]
            norm = turned * table_c - pltpu.roll(turned, HDIM // 2, 1) * table_s
            out[:, cols] = norm
            product = raw[:, base : base + HDIM] * norm
            gain_part[:, cols] += jnp.sum((product * rstd).reshape(BLOCK // 8, 8, HDIM), axis=0)
            products = products + product * gain[:, cols]
        dots[index : index + 1, :] = row_sums(products)


def norm_grads(d_q_rot, d_k_rot, raw, squares, gain_q, gain_k, cosine, sine):
    rows, width = d_q_rot.shape
    whole = pl.BlockSpec((1, width), lambda i: (0, 0))
    table = pl.BlockSpec((BLOCK, HDIM), lambda i: (i, 0))
    own = pl.BlockSpec((BLOCK, width), lambda i: (i, 0))
    pair = pl.BlockSpec((2, BLOCK), lambda i: (0, i))
    total = pl.BlockSpec((8, width), lambda i: (0, 0))
    grad = jax.ShapeDtypeStruct((rows, width), jnp.float32)
    return pl.pallas_call(
        norm_grads_kernel,
        grid=(rows // BLOCK,),
        in_specs=[
            own,
            own,
            pl.BlockSpec((BLOCK, 3 * width), lambda i: (i, 0)),
            pair,
            whole,
            whole,
            table,
            table,
        ],
        out_specs=[own, own, pair, total, total],
        out_shape=[
            grad,
            grad,
            jax.ShapeDtypeStruct((2, rows), jnp.float32),
            jax.ShapeDtypeStruct((8, width), jnp.float32),
            jax.ShapeDtypeStruct((8, width), jnp.float32),
        ],
        cost_estimate=pl.CostEstimate(
            flops=rows * width * 30, bytes_accessed=rows * width * 32, transcendentals=0
        ),
        name="norm_grads",
    )(d_q_rot, d_k_rot, raw, squares, gain_q[None], gain_k[None], cosine, sine)


def raw_grads_kernel(dq_ref, dk_ref, dv_ref, raw, squares, dots, gain_q, gain_k, out):
    width = dq_ref.shape[1]
    both, sums = squares[...], dots[...]
    for index, (grad, gain) in enumerate(((dq_ref, gain_q), (dk_ref, gain_k))):
        rstd = rstd_of(both, index)
        share = rstd * rstd * rstd * columns_of(sums, index) * (1.0 / D)
        for head in range(width // HDIM):
            cols = slice(head * HDIM, (head + 1) * HDIM)
            base = index * width + head * HDIM
            value = rstd * gain[:, cols] * grad[:, cols] - raw[:, base : base + HDIM] * share
            out[:, base : base + HDIM] = value.astype(jnp.bfloat16)
    out[:, 2 * width :] = dv_ref[...].astype(jnp.bfloat16)


def raw_grads(d_q_norm, d_k_norm, d_v, raw, squares, dots, gain_q, gain_k):
    rows, width = d_q_norm.shape
    whole = pl.BlockSpec((1, width), lambda i: (0, 0))
    own = pl.BlockSpec((BLOCK, width), lambda i: (i, 0))
    wide = pl.BlockSpec((BLOCK, 3 * width), lambda i: (i, 0))
    pair = pl.BlockSpec((2, BLOCK), lambda i: (0, i))
    return pl.pallas_call(
        raw_grads_kernel,
        grid=(rows // BLOCK,),
        in_specs=[own, own, own, wide, pair, pair, whole, whole],
        out_specs=wide,
        out_shape=jax.ShapeDtypeStruct((rows, 3 * width), jnp.bfloat16),
        cost_estimate=pl.CostEstimate(
            flops=rows * width * 20, bytes_accessed=rows * width * 30, transcendentals=0
        ),
        name="raw_grads",
    )(d_q_norm, d_k_norm, d_v, raw, squares, dots, gain_q[None], gain_k[None])


def dot(left, right):
    return jnp.dot(left, right, preferred_element_type=jnp.float32)


def contract_rows(left, right):
    return lax.dot_general(
        left, right, (((0,), (0,)), ((), ())), preferred_element_type=jnp.float32
    )


def contract_cols(left, right):
    return lax.dot_general(
        left, right, (((1,), (1,)), ((), ())), preferred_element_type=jnp.float32
    )


def rms_back(values, rstd, gain_vec, grad):
    scaled = grad * gain_vec
    row_dots = jnp.sum(values * scaled, axis=1, keepdims=True)
    return rstd * scaled - values * (rstd * rstd * rstd) * row_dots / D


def per_device(
    tokens,
    upstream,
    lengths,
    permutation,
    w_query,
    w_key,
    w_value,
    w_out,
    w_gate,
    w_up,
    w_down,
    q_gain,
    k_gain,
    attn_gain,
    ffn_gain,
):
    rank = lax.axis_index("core") * lax.axis_size("tl") + lax.axis_index("tl")
    own_rows = tokens.shape[0]
    group_rows = own_rows * 2 * lax.axis_size("tl")
    local_width = w_query.shape[1]

    own_group = lax.axis_index("core") == lax.axis_index("th")
    length_row = jnp.where(own_group, lengths, swap(lengths, "core"))[0]
    perm_row = jnp.where(own_group, permutation, swap(permutation, "core"))[0]

    tokens_all, qkv_full, out_full, gate_full = enter(
        tokens, [(w_query, w_key, w_value), (w_out.T,), (w_gate,)]
    )
    (up_shard, down_shard), tokens_all = lax.optimization_barrier(((w_up, w_down.T), tokens_all))
    up_pieces, down_pieces = pieces_of_weight(up_shard), pieces_of_weight(down_shard)
    tokens = lax.dynamic_slice_in_dim(tokens_all, rank * own_rows, own_rows)
    upstream = turn(upstream)

    perm_place = row_place(perm_row, own_rows)
    slots = jnp.arange(group_rows, dtype=jnp.int32)
    inverse = jnp.zeros((group_rows,), jnp.int32).at[perm_place].set(slots)
    position, starts = layout(length_row, group_rows)
    cosine, sine = rotary_tables(position)
    blocks = group_rows // BLOCK
    low_block = starts[::BLOCK] // BLOCK
    last_keys = (jnp.arange(blocks, dtype=jnp.int32) + 1) * BLOCK - 1
    reached = jnp.sum((starts[None, :] <= last_keys[:, None]).astype(jnp.int32), axis=1)
    high_block = (reached - 1) // BLOCK

    packed = tokens_all[perm_row]
    raw = dot(packed, qkv_full)
    up_pieces, raw = lax.optimization_barrier((up_pieces, raw))
    up_full = gather_weight(up_pieces)
    q_raw = raw[:, :local_width]
    k_raw = raw[:, local_width : 2 * local_width]
    squares = sum_over(
        jnp.stack([jnp.sum(q_raw * q_raw, axis=1), jnp.sum(k_raw * k_raw, axis=1)]), RANK
    )
    gain_q = lax.dynamic_slice_in_dim(q_gain, rank * local_width, local_width)
    gain_k = lax.dynamic_slice_in_dim(k_gain, rank * local_width, local_width)
    q_b, k_b, v_b = prepare(raw, squares, gain_q, gain_k, cosine, sine)
    attn_b, attn_f, logs = attention_forward(q_b, k_b, v_b, starts[None], low_block)
    down_pieces, attn_b = lax.optimization_barrier((down_pieces, attn_b))
    down_full = gather_weight(down_pieces)
    attn_given = attn_b[inverse]

    def pieces_of(value):
        if not small_grid():
            return [value]
        return [part(value, 0, 0, 2), part(value, 0, 1, 2)]

    attn_out, _ = scatter_rows(
        [contract_cols(piece, out_full) for piece in pieces_of(attn_given)]
    )
    rstd_a = lax.rsqrt(jnp.mean(attn_out * attn_out, axis=1, keepdims=True) + epsilon)
    resid = tokens.astype(jnp.float32) + attn_out * rstd_a * attn_gain
    resid_pieces = gather_rows(resid.astype(jnp.bfloat16))
    gates, ups, hiddens, sums = [], [], [], []
    for index in range(len(resid_pieces)):
        piece = resid_pieces[index]
        gate = dot(piece, gate_full)
        up_part = dot(piece, up_full)
        hidden_b = (gate * jax.nn.sigmoid(gate) * up_part).astype(jnp.bfloat16)
        gates.append(gate)
        ups.append(up_part)
        hiddens.append(hidden_b)
        sums.append(contract_cols(hidden_b, down_full).astype(jnp.bfloat16))
        if index + 1 < len(resid_pieces):
            resid_pieces[index + 1], gates[-1], ups[-1], hiddens[-1] = lax.optimization_barrier(
                (resid_pieces[index + 1], gates[-1], ups[-1], hiddens[-1])
            )
    mlp_out, _ = scatter_rows(sums)
    rstd_m = lax.rsqrt(jnp.mean(mlp_out * mlp_out, axis=1, keepdims=True) + epsilon)
    normed_m = mlp_out * rstd_m
    layer_out = turn((resid + normed_m * ffn_gain).astype(jnp.bfloat16))

    grad_f = upstream.astype(jnp.float32)
    ffn_gain_part = jnp.sum(grad_f * normed_m, axis=0)
    d_mlp_b = rms_back(mlp_out, rstd_m, ffn_gain, grad_f).astype(jnp.bfloat16)
    d_mlp_pieces = gather_rows(d_mlp_b)
    d_gates, d_ups, sums = [], [], []
    for index in range(len(d_mlp_pieces)):
        gate, up_part, d_mlp = gates[index], ups[index], d_mlp_pieces[index]
        gate_sigmoid = jax.nn.sigmoid(gate)
        d_hidden = dot(d_mlp, down_full)
        d_gate_b = (
            d_hidden * up_part * gate_sigmoid * (1.0 + gate * (1.0 - gate_sigmoid))
        ).astype(jnp.bfloat16)
        d_up_b = (d_hidden * gate * gate_sigmoid).astype(jnp.bfloat16)
        d_gates.append(d_gate_b)
        d_ups.append(d_up_b)
        sums.append(
            (contract_cols(d_gate_b, gate_full) + contract_cols(d_up_b, up_full)).astype(
                jnp.bfloat16
            )
        )
        if index + 1 < len(d_mlp_pieces):
            d_mlp_pieces[index + 1], d_gates[-1], d_ups[-1], sums[-1] = lax.optimization_barrier(
                (d_mlp_pieces[index + 1], d_gates[-1], d_ups[-1], sums[-1])
            )

    def rows(pieces):
        return jnp.concatenate(pieces, axis=0)

    down_grad = contract_rows(rows(d_mlp_pieces), rows(hiddens)).astype(jnp.bfloat16)
    gate_grad = contract_rows(rows(resid_pieces), rows(d_gates)).astype(jnp.bfloat16)
    d_sums, (down_grad, gate_grad) = scatter_rows(sums, (down_grad, gate_grad))
    d_resid = grad_f + d_sums
    up_grad = contract_rows(rows(resid_pieces), rows(d_ups)).astype(jnp.bfloat16)

    attn_gain_part = jnp.sum(d_resid * attn_out * rstd_a, axis=0)
    d_attn_b = rms_back(attn_out, rstd_a, attn_gain, d_resid).astype(jnp.bfloat16)
    d_attn_pieces = gather_rows(d_attn_b)
    d_attn_pieces[-1], up_grad = lax.optimization_barrier((d_attn_pieces[-1], up_grad))
    down_shard = scatter_weight(down_grad).T
    gate_shard = scatter_weight(gate_grad)
    up_shard = scatter_weight(up_grad)
    d_attn_all = rows(d_attn_pieces)
    d_given_b = rows([dot(piece, out_full).astype(jnp.bfloat16) for piece in d_attn_pieces])
    d_packed = d_given_b[perm_place]
    d_q_rot, d_k_rot, d_v = attention_backward(
        q_b, k_b, v_b, d_packed, attn_f, logs, starts[None], high_block
    )
    d_q_norm, d_k_norm, dots, q_parts, k_parts = norm_grads(
        d_q_rot, d_k_rot, raw, squares, gain_q, gain_k, cosine, sine
    )
    q_gain_part, k_gain_part = jnp.sum(q_parts, axis=0), jnp.sum(k_parts, axis=0)
    dots = sum_over(dots, RANK)
    d_qkv_b = raw_grads(d_q_norm, d_k_norm, d_v, raw, squares, dots, gain_q, gain_k)
    d_qkv_given = d_qkv_b[inverse]
    tokens_grad, query_shard, key_shard, value_shard, out_shard = leave(
        contract_cols(d_qkv_given, qkv_full),
        d_resid,
        [
            (contract_rows(packed, d_qkv_b), [local_width] * 3),
            (contract_rows(d_attn_all, attn_given), [local_width]),
        ],
    )

    def placed(part_sum):
        return lax.dynamic_update_slice_in_dim(
            jnp.zeros((D,), jnp.float32), part_sum, rank * local_width, 0
        )

    gain_grads = sum_over(
        jnp.stack(
            [
                placed(q_gain_part),
                placed(k_gain_part),
                attn_gain_part,
                ffn_gain_part,
            ]
        ),
        DP + TENSOR,
    )
    return (
        layer_out,
        tokens_grad,
        query_shard,
        key_shard,
        value_shard,
        out_shard.T,
        gate_shard,
        up_shard,
        down_shard,
        gain_grads[0],
        gain_grads[1],
        gain_grads[2],
        gain_grads[3],
    )


def solution(mesh):
    dp, tensor = mesh.shape["dp"], mesh.shape["tensor"]
    fine = Mesh(mesh.devices.reshape(dp // 4, 2, 2, 2, tensor // 2), DP + TENSOR)
    rows, weight, weight_out = P(DP + TENSOR, None), P(DP, TENSOR), P(TENSOR, DP)
    return jax.shard_map(
        per_device,
        mesh=fine,
        in_specs=(rows, rows, P(DP, None), P(DP, None))
        + (weight,) * 3
        + (weight_out, weight, weight, weight_out)
        + (P(),) * 4,
        out_specs=(rows, rows)
        + (weight,) * 3
        + (weight_out, weight, weight, weight_out)
        + (P(),) * 4,
        check_vma=False,
    )
```

```python
import functools
import math

import jax
import jax.numpy as jnp
from jax import lax
from jax.experimental import pallas as pl
from jax.experimental.pallas import tpu as pltpu
from jax.sharding import Mesh, PartitionSpec as P

D = 2048
HDIM = 128

epsilon = 1e-06
rope_base = 500000.0
masked_score = -1e30
BLOCK = 256
VMEM_BYTES = 48 * 1024 * 1024
MESH = pl.DeviceIdType.MESH
BESIDE = pl.CostEstimate(flops=1, bytes_accessed=1, transcendentals=0)
PARTS = 2

SWAP = [(0, 1), (1, 0)]
TURN = [(1, 2), (2, 1)]
CYCLE = [(0, 1), (1, 3), (3, 2), (2, 0)]
CYCLE_BACK = [(d, s) for s, d in CYCLE]
DP = ("a", "b", "core")
TENSOR = ("th", "tl")
RANK = ("core", "tl")


def swap(value, axis):
    return lax.ppermute(value, axis, SWAP)


def start_turn(value):
    return value, lax.ppermute(value, ("core", "th"), TURN)


def finish_turn(kept, arrived):
    stays = lax.axis_index("core") == lax.axis_index("th")
    return jnp.where(stays, kept, arrived)


def turn(value):
    return finish_turn(*start_turn(value))


def small_grid():
    return lax.axis_size("a") == 2 and lax.axis_size("tl") == 2


def part(value, dim, index, count):
    size = value.shape[dim] // count
    return lax.slice_in_dim(value, index * size, (index + 1) * size, axis=dim)


def in_turn(left, right):
    upper = lax.axis_index("th") == 0
    return jnp.where(upper, left, right), jnp.where(upper, right, left)


def pair_of_weight(shard):
    second = lax.ppermute(shard, ("core", "th"), CYCLE)
    return jnp.concatenate(in_turn(turn(shard), second), axis=0)


def gather_weight(pair):
    return lax.all_gather(pair, ("a", "b"), axis=0, tiled=True)


def scatter_pair(total):
    return lax.psum_scatter(
        total.astype(jnp.bfloat16), ("a", "b"), scatter_dimension=0, tiled=True
    )


def start_split(pair):
    first, second = in_turn(part(pair, 0, 0, 2), part(pair, 0, 1, 2))
    return first, start_turn(first)[1], lax.ppermute(second, ("core", "th"), CYCLE_BACK)


def finish_split(first, arrived, other):
    return finish_turn(first, arrived).astype(jnp.float32) + other.astype(jnp.float32)


def greet():
    a, b, core = lax.axis_index("a"), lax.axis_index("b"), lax.axis_index("core")
    th, tl = lax.axis_index("th"), lax.axis_index("tl")
    barrier = pltpu.get_barrier_semaphore()
    others = (
        {"a": 1 - a},
        {"b": 1 - b},
        {"core": 1 - core},
        {"tl": 1 - tl},
        {"th": 1 - th},
        {"core": 1 - core, "th": 1 - th},
    )
    for other in others:
        pl.semaphore_signal(barrier, inc=1, device_id=other, device_id_type=MESH)
    pl.semaphore_wait(barrier, len(others))


CHUNKS = 4


def entry_slots(plan):
    return 4 * CHUNKS + sum(3 * len(units) + 6 for units, _ in plan)


def entry_kernel(plan, *refs):
    shard_count = sum(len(units) for units, _ in plan)
    tokens, shards = refs[0], refs[1 : 1 + shard_count]
    tokens_all, fulls = refs[1 + shard_count], refs[2 + shard_count : -3]
    send, recv, local = refs[-3:]
    a, b, core = lax.axis_index("a"), lax.axis_index("b"), lax.axis_index("core")
    th, tl = lax.axis_index("th"), lax.axis_index("tl")
    stays = core == th
    greet()
    used = [0]

    def slots(count):
        used[0] += count
        return used[0] - count

    def remote(source, target, slot, to):
        return pltpu.make_async_remote_copy(
            src_ref=source,
            dst_ref=target,
            send_sem=send.at[slot],
            recv_sem=recv.at[slot],
            device_id=to,
            device_id_type=MESH,
        )

    def arrived(target, slot):
        remote(target, target, slot, {"core": 1 - core}).wait_recv()

    stages, taken = [], 0
    for full, (units, rings) in zip(fulls, plan):
        stage = []
        for column in units:
            shard = shards[taken]
            base = slots(3)
            height, width = shard.shape

            def place(sub, full=full, column=column, height=height, width=width, rings=rings):
                block = 4 * a + 2 * b if rings else 0
                row = pl.multiple_of((block + sub) * height, height)
                return full.at[pl.ds(row, height), pl.ds(column, width)]

            stage.append((shard, place, base, taken))
            taken += 1
        stages.append(stage)

    def near_copy(shard, place, base):
        return remote(shard, place(core), base + 2, {"core": 1 - core})

    def far_copy(shard, place, base):
        return remote(shard, place(core), base + core, {"core": th, "th": 1 - th})

    def start_stage(stage):
        for shard, place, base, index in stage:
            far_copy(shard, place, base).start()

            @pl.when(stays)
            def _():
                pltpu.make_async_copy(shard, place(core), local.at[index]).start()

            @pl.when(jnp.logical_not(stays))
            def _():
                near_copy(shard, place, base).start()

    def finish_stage(stage):
        for shard, place, base, index in stage:

            @pl.when(stays)
            def _():
                pltpu.make_async_copy(shard, place(core), local.at[index]).wait()
                arrived(place(1 - core), base + 2)

            @pl.when(jnp.logical_not(stays))
            def _():
                arrived(place(0), base)
                arrived(place(1), base + 1)

    def piece(full, block_a, block_b, sub):
        height = full.shape[0] // 8
        row = pl.multiple_of((4 * block_a + 2 * block_b + sub) * height, height)
        return full.at[pl.ds(row, height), :]

    def ring(full, base):
        to_a, to_b = {"a": 1 - a}, {"b": 1 - b}
        return (
            [remote(piece(full, a, b, sub), piece(full, a, b, sub), base + sub, to_b) for sub in (0, 1)],
            [remote(piece(full, a, b, sub), piece(full, a, b, sub), base + 2 + sub, to_a) for sub in (0, 1)],
            remote(piece(full, a, 1 - b, 0), piece(full, a, 1 - b, 0), base + 4, to_a),
            remote(piece(full, 1 - a, b, 1), piece(full, 1 - a, b, 1), base + 5, to_b),
        )

    ring_base = [slots(6) for _ in fulls]

    def start_ring(index):
        over_b, over_a, _, _ = ring(fulls[index], ring_base[index])
        for copy in (over_b[0], over_a[1], over_b[1], over_a[0]):
            copy.start()

    def forward_ring(index):
        full, base = fulls[index], ring_base[index]
        arrived(piece(full, a, 1 - b, 0), base)
        ring(full, base)[2].start()
        arrived(piece(full, 1 - a, b, 1), base + 3)
        ring(full, base)[3].start()

    def finish_ring(index):
        full, base = fulls[index], ring_base[index]
        arrived(piece(full, a, 1 - b, 1), base + 1)
        arrived(piece(full, 1 - a, b, 0), base + 2)
        arrived(piece(full, 1 - a, 1 - b, 0), base + 4)
        arrived(piece(full, 1 - a, 1 - b, 1), base + 5)
        over_b, over_a, first, second = ring(full, base)
        for copy in (*over_b, *over_a, first, second):
            copy.wait_send()

    rows = tokens.shape[0]
    step = rows // CHUNKS
    row_base = slots(4 * CHUNKS)

    def rows_of(block_core, block_tl, chunk):
        row = pl.multiple_of((2 * block_core + block_tl) * rows + chunk * step, step)
        return tokens_all.at[pl.ds(row, step), :]

    def row_copies(chunk):
        slot = row_base + 4 * chunk
        own, other = rows_of(core, tl, chunk), rows_of(core, 1 - tl, chunk)
        return (
            remote(
                tokens.at[pl.ds(chunk * step, step), :],
                rows_of(th, tl, chunk),
                slot,
                {"core": th, "th": core},
            ),
            remote(own, own, slot + 1, {"tl": 1 - tl}),
            remote(own, own, slot + 2, {"core": 1 - core}),
            remote(other, other, slot + 3, {"core": 1 - core}),
        )

    def own_rows(chunk):
        return pltpu.make_async_copy(
            tokens.at[pl.ds(chunk * step, step), :],
            rows_of(core, tl, chunk),
            local.at[shard_count + chunk],
        )

    for chunk in range(CHUNKS):

        @pl.when(stays)
        def _():
            own_rows(chunk).start()

    ringed = [index for index, (_, rings) in enumerate(plan) if rings]
    for index in ringed:
        start_stage(stages[index])
    for chunk in range(CHUNKS):

        @pl.when(jnp.logical_not(stays))
        def _():
            row_copies(chunk)[0].start()

        @pl.when(stays)
        def _():
            own_rows(chunk).wait()
            row_copies(chunk)[1].start()
            row_copies(chunk)[2].start()

    for index in ringed:
        finish_stage(stages[index])
        start_ring(index)
    for index in range(len(plan)):
        if index not in ringed:
            start_stage(stages[index])
    for chunk in range(CHUNKS):

        @pl.when(jnp.logical_not(stays))
        def _():
            arrived(rows_of(core, tl, chunk), row_base + 4 * chunk)
            row_copies(chunk)[1].start()
            row_copies(chunk)[2].start()

    for index in ringed:
        forward_ring(index)
    for chunk in range(CHUNKS):
        arrived(rows_of(core, 1 - tl, chunk), row_base + 4 * chunk + 1)
        row_copies(chunk)[3].start()
    for index in ringed:
        finish_ring(index)
    for index in range(len(plan)):
        if index not in ringed:
            finish_stage(stages[index])
    for chunk in range(CHUNKS):
        arrived(rows_of(1 - core, tl, chunk), row_base + 4 * chunk + 2)
        arrived(rows_of(1 - core, 1 - tl, chunk), row_base + 4 * chunk + 3)

        @pl.when(jnp.logical_not(stays))
        def _():
            row_copies(chunk)[0].wait_send()

        for copy in row_copies(chunk)[1:]:
            copy.wait_send()
    for stage in stages:
        for shard, place, base, _ in stage:
            far_copy(shard, place, base).wait_send()

            @pl.when(jnp.logical_not(stays))
            def _():
                near_copy(shard, place, base).wait_send()


def leave_kernel(cuts, paired, *refs):
    count = len(cuts)
    ringed = [index for index in range(count) if not paired[index]]
    partial, resid, gains, totals = refs[0], refs[1], refs[2], refs[3 : 3 + count]
    outs = refs[3 + count : 3 + count + 2 + sum(len(cut) for cut in cuts)]
    rows_out, gains_out, shard_outs = outs[0], outs[1], outs[2:]
    scratch = refs[3 + count + len(outs) :]
    peer_far, peer_near, far_sum, from_far, done_rows = scratch[:5]
    boxes, taken = [], 5
    for alone in paired:
        boxes.append(scratch[taken : taken + (1 if alone else 8)])
        taken += 1 if alone else 8
    gain_box, send, recv, local = scratch[-4:]
    a, b, core = lax.axis_index("a"), lax.axis_index("b"), lax.axis_index("core")
    th, tl = lax.axis_index("th"), lax.axis_index("tl")
    stays = core == th
    to_a, to_b, to_core, to_tl = {"a": 1 - a}, {"b": 1 - b}, {"core": 1 - core}, {"tl": 1 - tl}
    greet()

    def remote(source, target, slot, to, send_slot=None):
        return pltpu.make_async_remote_copy(
            src_ref=source,
            dst_ref=target,
            send_sem=send.at[slot if send_slot is None else send_slot],
            recv_sem=recv.at[slot],
            device_id=to,
            device_id_type=MESH,
        )

    def arrived(target, slot):
        remote(target, target, slot, to_core).wait_recv()

    def add(target, target_row, height, *sources):
        step = 16

        def one(index, unused):
            value = None
            for source, first in sources:
                here = pl.ds(pl.multiple_of(first + index * step, step), step)
                term = source[here, :].astype(jnp.float32)
                value = term if value is None else value + term
            there = pl.ds(pl.multiple_of(target_row + index * step, step), step)
            target[there, :] = value.astype(target.dtype)
            return unused

        lax.fori_loop(0, height // step, one, 0)

    rows = resid.shape[0]
    step = rows // CHUNKS

    own, peer, far, peer_of_far = range(4)

    size = rows // PARTS

    def row_of(block, chunk):
        place = chunk * step
        return (place // size) * 4 * size + block * size + place % size

    def at(ref, row):
        return ref.at[pl.ds(row, step), :]

    def row_copies(chunk):
        here = chunk * step
        return (
            remote(at(partial, row_of(peer_of_far, chunk)), at(peer_far, here), 4 * chunk, to_core),
            remote(at(partial, row_of(peer, chunk)), at(peer_near, here), 4 * chunk + 1, to_core),
            remote(at(far_sum, here), at(from_far, here), 4 * chunk + 2, to_tl),
            remote(at(done_rows, here), at(rows_out, here), 4 * chunk + 3, {"core": th, "th": core}),
        )

    def kept_rows(chunk):
        here = chunk * step
        return pltpu.make_async_copy(at(done_rows, here), at(rows_out, here), local.at[chunk])

    base = 4 * CHUNKS

    def piece(ref, block_a, block_b, sub):
        height = ref.shape[0] // 8
        return pl.multiple_of((4 * block_a + 2 * block_b + sub) * height, height), height

    def slice_of(ref, block_a, block_b, sub):
        row, height = piece(ref, block_a, block_b, sub)
        return ref.at[pl.ds(row, height), :]

    def copies(index):
        total = totals[index]
        _, over_a, over_b, send_b, send_a, from_b, from_a, _ = boxes[index]
        slot = base + 10 * index
        height = total.shape[0] // 8

        def half(ref, sub):
            return ref.at[pl.ds(sub * height, height), :]

        return (
            remote(slice_of(total, 1 - a, 1 - b, 0), over_a, slot, to_a),
            remote(slice_of(total, 1 - a, 1 - b, 1), over_b, slot + 1, to_b),
            remote(slice_of(total, a, 1 - b, 1), half(from_b, 1), slot + 2, to_b),
            remote(slice_of(total, 1 - a, b, 0), half(from_a, 0), slot + 3, to_a),
            remote(send_b, half(from_b, 0), slot + 4, to_b),
            remote(send_a, half(from_a, 1), slot + 5, to_a),
        )

    def own_sum(index, sub):
        sums = totals[index] if paired[index] else boxes[index][7]
        height = sums.shape[0] // 2
        return sums.at[pl.ds(pl.multiple_of(sub * height, height), height), :]

    def last_copies(index):
        inbox = boxes[index][0]
        slot = base + 10 * index + 6
        return (
            remote(own_sum(index, 1 - core), inbox.at[0], slot, to_core),
            remote(own_sum(index, 0), inbox.at[1], slot + 1, {"core": 0, "th": core}),
            remote(own_sum(index, 1), inbox.at[1], slot + 1, {"core": 1, "th": core}, slot + 2),
        )

    def start_last(index):
        @pl.when(stays)
        def _():
            last_copies(index)[0].start()

        @pl.when(jnp.logical_not(stays))
        def _():
            last_copies(index)[1].start()
            last_copies(index)[2].start()

    gain_axes = ({"core": 1 - core}, {"tl": 1 - tl}, {"b": 1 - b}, {"a": 1 - a}, {"th": 1 - th})

    def gain_copy(turn_index):
        source = gains if turn_index == 0 else gain_box.at[4 + turn_index]
        return remote(
            source,
            gain_box.at[turn_index],
            base + 10 * count + turn_index,
            gain_axes[turn_index],
        )

    def gain_step(turn_index):
        arrived(gain_box.at[turn_index], base + 10 * count + turn_index)
        mine = gains[...] if turn_index == 0 else gain_box[4 + turn_index]
        total = mine + gain_box[turn_index]
        if turn_index == 4:
            gains_out[...] = total
        else:
            gain_box[5 + turn_index] = total
            gain_copy(turn_index + 1).start()

    def start_ring(index):
        for copy in copies(index)[:4]:
            copy.start()

    def turn_ring(index):
        total = totals[index]
        _, over_a, over_b, send_b, send_a, _, _, _ = boxes[index]
        height = total.shape[0] // 8
        arrived(over_a, base + 10 * index)
        add(send_b, 0, height, (total, piece(total, a, 1 - b, 0)[0]), (over_a, 0))
        copies(index)[4].start()
        arrived(over_b, base + 10 * index + 1)
        add(send_a, 0, height, (total, piece(total, 1 - a, b, 1)[0]), (over_b, 0))
        copies(index)[5].start()

    def finish_ring(index):
        total = totals[index]
        _, _, _, _, _, from_b, from_a, sums = boxes[index]
        height = total.shape[0] // 8
        slot = base + 10 * index
        for sub in (0, 1):
            arrived(from_b.at[pl.ds(sub * height, height), :], slot + (4 if sub == 0 else 2))
            arrived(from_a.at[pl.ds(sub * height, height), :], slot + (3 if sub == 0 else 5))
            add(
                sums,
                sub * height,
                height,
                (total, piece(total, a, b, sub)[0]),
                (from_b, sub * height),
                (from_a, sub * height),
            )
        start_last(index)

    def finish_chunk(chunk):
        here = chunk * step
        arrived(at(peer_near, here), 4 * chunk + 1)
        arrived(at(from_far, here), 4 * chunk + 2)
        add(
            done_rows,
            here,
            step,
            (partial, row_of(own, chunk)),
            (peer_near, here),
            (from_far, here),
            (resid, here),
        )

        @pl.when(stays)
        def _():
            kept_rows(chunk).start()

        @pl.when(jnp.logical_not(stays))
        def _():
            row_copies(chunk)[3].start()

    for chunk in range(CHUNKS):
        row_copies(chunk)[0].start()
    for chunk in range(CHUNKS):
        row_copies(chunk)[1].start()
    for index in range(count):
        if paired[index]:
            start_last(index)
    for chunk in range(CHUNKS):
        arrived(at(peer_far, chunk * step), 4 * chunk)
        add(
            far_sum,
            chunk * step,
            step,
            (partial, row_of(far, chunk)),
            (peer_far, chunk * step),
        )
        row_copies(chunk)[2].start()
    for index in ringed:
        start_ring(index)
    gain_copy(0).start()
    gain_step(0)
    for place in range(max(len(ringed), CHUNKS)):
        if place < len(ringed):
            turn_ring(ringed[place])
        if place < CHUNKS:
            finish_chunk(place)
    for step_index in (1, 2, 3):
        gain_step(step_index)
    for index in ringed:
        finish_ring(index)
    gain_step(4)
    for index, cut in sorted(enumerate(cuts), key=lambda pair: not paired[pair[0]]):
        inbox = boxes[index][0]
        sums = totals[index] if paired[index] else boxes[index][-1]
        height = inbox.shape[1]
        slot = base + 10 * index + 6
        taken = sum(len(other) for other in cuts[:index])
        arrived(inbox.at[1], slot + 1)

        @pl.when(jnp.logical_not(stays))
        def _():
            arrived(inbox.at[0], slot)

        def one(step_index, unused, cut=cut, taken=taken, sums=sums, inbox=inbox, height=height):
            row = pl.multiple_of(step_index * 16, 16)
            here = pl.ds(row, 16)
            other = inbox[1, here, :].astype(jnp.float32)

            def store(value):
                first = 0
                for offset, end in enumerate(cut):
                    shard_outs[taken + offset][here, :] = (value + other)[:, first:end]
                    first = end

            @pl.when(stays)
            def _():
                own_row = pl.multiple_of(core * height + row, 16)
                store(sums[pl.ds(own_row, 16), :].astype(jnp.float32))

            @pl.when(jnp.logical_not(stays))
            def _():
                store(inbox[0, here, :].astype(jnp.float32))

            return unused

        lax.fori_loop(0, height // 16, one, 0)
    for chunk in range(CHUNKS):
        for copy in row_copies(chunk)[:3]:
            copy.wait_send()

        @pl.when(stays)
        def _():
            kept_rows(chunk).wait()

        @pl.when(jnp.logical_not(stays))
        def _():
            row_copies(chunk)[3].wait_send()
            arrived(at(rows_out, chunk * step), 4 * chunk + 3)

    for turn_index in range(5):
        gain_copy(turn_index).wait_send()
    for index in ringed:
        for copy in copies(index):
            copy.wait_send()
    for index in range(count):

        @pl.when(stays)
        def _():
            last_copies(index)[0].wait_send()

        @pl.when(jnp.logical_not(stays))
        def _():
            last_copies(index)[1].wait_send()
            last_copies(index)[2].wait_send()


def leave(partial, resid, gains, totals):
    if not small_grid():
        summed = finish_scatter_rows(start_scatter([partial.astype(jnp.bfloat16)]), None)
        shards = []
        for total, parts, alone in totals:
            shard, first = finish_split(*start_split(total if alone else scatter_pair(total))), 0
            for width in parts:
                shards.append(shard[:, first : first + width])
                first += width
        total_gains = sum_over(gains, DP + TENSOR)
        return [turn((resid + summed).astype(jnp.bfloat16)), total_gains] + shards
    rows, columns = resid.shape
    cuts, scratch = [], []
    outs = [
        jax.ShapeDtypeStruct((rows, columns), jnp.bfloat16),
        jax.ShapeDtypeStruct(gains.shape, jnp.float32),
    ]
    for total, parts, alone in totals:
        height, width = total.shape[0] // (2 if alone else 8), total.shape[1]
        cuts.append(tuple(sum(parts[: index + 1]) for index in range(len(parts))))
        outs += [jax.ShapeDtypeStruct((height, part_width), jnp.float32) for part_width in parts]
        shapes = [(2, height, width)]
        if not alone:
            shapes += [(height, width)] * 4 + [(2 * height, width)] * 3
        scratch += [pltpu.VMEM(shape, jnp.bfloat16) for shape in shapes]
    paired = tuple(alone for _, _, alone in totals)
    slots = 4 * CHUNKS + 10 * len(totals) + 5
    vmem = pl.BlockSpec(memory_space=pltpu.VMEM)
    return pl.pallas_call(
        functools.partial(leave_kernel, tuple(cuts), paired),
        in_specs=[vmem] * (3 + len(totals)),
        out_specs=[pl.BlockSpec(memory_space=pl.ANY)] + [vmem] * (len(outs) - 1),
        out_shape=outs,
        scratch_shapes=[pltpu.VMEM((rows, columns), jnp.bfloat16)] * 5
        + scratch
        + [
            pltpu.VMEM((9, *gains.shape), jnp.float32),
            pltpu.SemaphoreType.DMA((slots,)),
            pltpu.SemaphoreType.DMA((slots,)),
            pltpu.SemaphoreType.DMA((CHUNKS,)),
        ],
        compiler_params=pltpu.CompilerParams(
            collective_id=1, has_side_effects=True, vmem_limit_bytes=60 * 1024 * 1024
        ),
        cost_estimate=BESIDE,
        name="leave",
    )(partial.astype(jnp.bfloat16), resid, gains, *[total.astype(jnp.bfloat16) for total, _, _ in totals])


def enter(tokens, matrices):
    if not small_grid():
        own = turn(tokens)
        pairs = [
            (pair_of_weight(jnp.concatenate(shards, axis=1)), whole) for shards, whole in matrices
        ]
        return [lax.all_gather(own, RANK, axis=0, tiled=True)] + [
            gather_weight(pair) if whole else pair for pair, whole in pairs
        ]
    plan, outs = [], [jax.ShapeDtypeStruct((4 * tokens.shape[0], tokens.shape[1]), tokens.dtype)]
    for shards, whole in matrices:
        columns = [0]
        for shard in shards:
            columns.append(columns[-1] + shard.shape[1])
        plan.append((tuple(columns[:-1]), whole))
        height = (8 if whole else 2) * shards[0].shape[0]
        outs.append(jax.ShapeDtypeStruct((height, columns[-1]), tokens.dtype))
    flat = [shard for shards, _ in matrices for shard in shards]
    slots = entry_slots(plan)
    anywhere = pl.BlockSpec(memory_space=pl.ANY)
    return pl.pallas_call(
        functools.partial(entry_kernel, tuple(plan)),
        in_specs=[anywhere] * (1 + len(flat)),
        out_specs=[anywhere] * len(outs),
        out_shape=outs,
        scratch_shapes=[
            pltpu.SemaphoreType.DMA((slots,)),
            pltpu.SemaphoreType.DMA((slots,)),
            pltpu.SemaphoreType.DMA((len(flat) + CHUNKS,)),
        ],
        compiler_params=pltpu.CompilerParams(collective_id=0, has_side_effects=True),
        cost_estimate=BESIDE,
        name="enter",
    )(tokens, *flat)


def row_place(row, own_rows):
    if not small_grid():
        return row
    mask = 2 * lax.axis_index("core") + lax.axis_index("tl")
    block = (row // own_rows) ^ mask
    block = (block // 2) + 2 * (block % 2)
    size = own_rows // PARTS
    place = row % own_rows
    return (place // size) * 4 * size + block * size + place % size


def after(token, value):
    return value if token is None else lax.optimization_barrier((value, token))[0]


def start_gather(value):
    if not small_grid():
        return lax.all_gather(value, RANK, axis=0, tiled=True), None
    return jnp.concatenate([value, swap(value, "core")], axis=0), swap(value, "tl")


def forward_rows(rows, token):
    far = after(token, rows[1])
    return jnp.concatenate([far, swap(far, "core")], axis=0)


def start_scatter(pieces):
    if not small_grid():
        return (lax.psum_scatter(pieces[0], RANK, scatter_dimension=0, tiled=True),)
    near, far = pieces
    rows = near.shape[0] // 2
    far_peer = swap(far[rows:], "core")
    far_sum = (far[:rows].astype(jnp.float32) + far_peer.astype(jnp.float32)).astype(jnp.bfloat16)
    return near[:rows], swap(near[rows:], "core"), swap(far_sum, "tl")


def finish_scatter_rows(terms, token):
    terms = [*terms[:-1], after(token, terms[-1])]
    return sum(term.astype(jnp.float32) for term in terms)


def sum_over(value, axes):
    for axis in axes:
        if lax.axis_size(axis) == 2:
            value = value + swap(value, axis)
        else:
            value = lax.psum(value, axis)
    return value


def layout(length_row, group_rows):
    positions = jnp.arange(group_rows, dtype=jnp.int32)
    start = jnp.int32(0)
    offset = jnp.zeros((group_rows,), jnp.int32)
    starts = positions
    for index in range(length_row.shape[0]):
        end = start + length_row[index]
        inside = (positions >= start) & (positions < end)
        offset = jnp.where(inside, start, offset)
        starts = jnp.where(inside, start, starts)
        start = end
    return (positions - offset, starts)


def rotary_tables(position):
    half_dim = HDIM // 2
    exponents = jnp.arange(half_dim, dtype=jnp.float32) * (2.0 / HDIM)
    frequency = jnp.power(jnp.float32(rope_base), -exponents)
    angles = position.astype(jnp.float32)[:, None] * frequency[None, :]
    cosine, sine = jnp.cos(angles), jnp.sin(angles)
    return (
        jnp.concatenate([cosine, cosine], axis=1),
        jnp.concatenate([-sine, sine], axis=1),
    )


def columns_of(rows, index):
    chosen = (lax.broadcasted_iota(jnp.int32, (rows.shape[0], HDIM), 0) == index).astype(
        jnp.float32
    )
    return lax.dot_general(
        rows,
        chosen,
        (((0,), (0,)), ((), ())),
        precision=lax.Precision.HIGHEST,
        preferred_element_type=jnp.float32,
    )


def row_sums(values):
    ones = jnp.ones((8, values.shape[1]), jnp.float32)
    return lax.dot_general(
        ones,
        values,
        (((1,), (1,)), ((), ())),
        precision=lax.Precision.HIGHEST,
        preferred_element_type=jnp.float32,
    )[:1]


def rstd_of(squares, index):
    return lax.rsqrt(columns_of(squares, index) * (1.0 / D) + epsilon)


def prepare_kernel(raw, squares, gain_q, gain_k, cosine, sine, q_out, k_out, v_out):
    width = q_out.shape[1]
    table_c, table_s = cosine[...], sine[...]
    both = squares[...]
    for index, (gain, out) in enumerate(((gain_q, q_out), (gain_k, k_out))):
        rstd = rstd_of(both, index)
        for head in range(width // HDIM):
            cols = slice(head * HDIM, (head + 1) * HDIM)
            base = index * width + head * HDIM
            norm = raw[:, base : base + HDIM] * rstd * gain[:, cols]
            turned = norm * table_c + pltpu.roll(norm, HDIM // 2, 1) * table_s
            out[:, cols] = turned.astype(jnp.bfloat16)
    v_out[...] = raw[:, 2 * width :].astype(jnp.bfloat16)


def prepare(raw, squares, gain_q, gain_k, cosine, sine):
    rows, width = raw.shape[0], raw.shape[1] // 3
    whole = pl.BlockSpec((1, width), lambda i: (0, 0))
    table = pl.BlockSpec((BLOCK, HDIM), lambda i: (i, 0))
    out = pl.BlockSpec((BLOCK, width), lambda i: (i, 0))
    return pl.pallas_call(
        prepare_kernel,
        grid=(rows // BLOCK,),
        in_specs=[
            pl.BlockSpec((BLOCK, 3 * width), lambda i: (i, 0)),
            pl.BlockSpec((2, BLOCK), lambda i: (0, i)),
            whole,
            whole,
            table,
            table,
        ],
        out_specs=[out] * 3,
        out_shape=[jax.ShapeDtypeStruct((rows, width), jnp.bfloat16)] * 3,
        cost_estimate=BESIDE,
        name="prepare",
    )(raw, squares, gain_q[None], gain_k[None], cosine, sine)


def allowed_keys(starts, first_key, first_query):
    shape = (BLOCK, BLOCK)
    keys = first_key + lax.broadcasted_iota(jnp.int32, shape, 0)
    queries = first_query + lax.broadcasted_iota(jnp.int32, shape, 1)
    return (keys >= starts) & (keys <= queries)


def forward_kernel(low_ref, q_ref, k_ref, v_ref, start_ref, attn_ref, full_ref, log_ref):
    block = pl.program_id(1)
    queries = q_ref[...]
    starts = start_ref[...]
    scale = 1.0 / math.sqrt(HDIM)

    def step(index, carried):
        peak, total, acc = carried
        rows = pl.ds(pl.multiple_of(index * BLOCK, BLOCK), BLOCK)
        scores = contract_cols(k_ref[rows, :], queries) * scale
        scores = jnp.where(
            allowed_keys(starts, index * BLOCK, block * BLOCK), scores, masked_score
        )
        new_peak = jnp.maximum(peak, jnp.max(scores, axis=0, keepdims=True))
        fade = jnp.exp(peak - new_peak)
        weights = jnp.exp(scores - new_peak)
        total = total * fade + jnp.sum(weights, axis=0, keepdims=True)
        acc = acc * fade + contract_rows(v_ref[rows, :], weights.astype(jnp.bfloat16))
        return (new_peak, total, acc)

    start = (
        jnp.full((1, BLOCK), masked_score, jnp.float32),
        jnp.zeros((1, BLOCK), jnp.float32),
        jnp.zeros((HDIM, BLOCK), jnp.float32),
    )
    carried = step(block, start)
    peak, total, acc = lax.fori_loop(low_ref[block], block, step, carried)
    out = jnp.transpose(acc / total)
    full_ref[...] = out
    attn_ref[...] = out.astype(jnp.bfloat16)
    log_ref[...] = peak + jnp.log(total)


def attention_forward(q_b, k_b, v_b, starts, low_block):
    rows, width = q_b.shape
    heads = width // HDIM
    own = pl.BlockSpec((BLOCK, HDIM), lambda h, i, low: (i, h))
    whole = pl.BlockSpec((rows, HDIM), lambda h, i, low: (0, h))
    return pl.pallas_call(
        forward_kernel,
        grid_spec=pltpu.PrefetchScalarGridSpec(
            num_scalar_prefetch=1,
            grid=(heads, rows // BLOCK),
            in_specs=[own, whole, whole, pl.BlockSpec((1, BLOCK), lambda h, i, low: (0, i))],
            out_specs=[own, own, pl.BlockSpec((None, 1, BLOCK), lambda h, i, low: (h, 0, i))],
        ),
        out_shape=[
            jax.ShapeDtypeStruct((rows, width), jnp.bfloat16),
            jax.ShapeDtypeStruct((rows, width), jnp.float32),
            jax.ShapeDtypeStruct((heads, 1, rows), jnp.float32),
        ],
        compiler_params=pltpu.CompilerParams(vmem_limit_bytes=VMEM_BYTES),
        cost_estimate=BESIDE,
        name="attention_forward",
    )(low_block, q_b, k_b, v_b, starts)


def backward_kernel(
    high_ref, q_ref, k_ref, v_ref, grad_ref, full_ref, log_ref, start_ref, dq_ref, dk_ref, dv_ref, delta
):
    block = pl.program_id(1)
    blocks = pl.num_programs(1)
    scale = 1.0 / math.sqrt(HDIM)

    @pl.when(block == 0)
    def _():
        dq_ref[...] = jnp.zeros_like(dq_ref)

        def one(index, unused):
            rows = pl.ds(pl.multiple_of(index * BLOCK, BLOCK), BLOCK)
            delta[:, rows] = row_sums(grad_ref[rows, :].astype(jnp.float32) * full_ref[rows, :])
            return unused

        lax.fori_loop(0, blocks, one, 0)

    here = pl.ds(pl.multiple_of(block * BLOCK, BLOCK), BLOCK)
    keys, values = k_ref[here, :], v_ref[here, :]

    def step(index, carried):
        dk, dv = carried
        rows = pl.ds(pl.multiple_of(index * BLOCK, BLOCK), BLOCK)
        queries, grads = q_ref[rows, :], grad_ref[rows, :]
        scores = contract_cols(keys, queries) * scale
        allowed = allowed_keys(start_ref[:, rows], block * BLOCK, index * BLOCK)
        probs = jnp.where(allowed, jnp.exp(scores - log_ref[:, rows]), 0.0)
        dv = dv + dot(probs.astype(jnp.bfloat16), grads)
        d_probs = contract_cols(values, grads)
        d_scores = (probs * (d_probs - delta[:, rows])).astype(jnp.bfloat16)
        dk = dk + dot(d_scores, queries)
        dq_ref[rows, :] += contract_rows(d_scores, keys)
        return (dk, dv)

    zero = jnp.zeros((BLOCK, HDIM), jnp.float32)
    dk, dv = lax.fori_loop(block, high_ref[block] + 1, step, (zero, zero))
    dk_ref[...] = dk * scale
    dv_ref[...] = dv

    @pl.when(block == blocks - 1)
    def _():
        dq_ref[...] = dq_ref[...] * scale


def attention_backward(q_b, k_b, v_b, grads, full, logs, starts, high_block):
    rows, width = q_b.shape
    heads = width // HDIM
    own = pl.BlockSpec((BLOCK, HDIM), lambda h, i, high: (i, h))
    whole = pl.BlockSpec((rows, HDIM), lambda h, i, high: (0, h))
    out = jax.ShapeDtypeStruct((rows, width), jnp.float32)
    return pl.pallas_call(
        backward_kernel,
        grid_spec=pltpu.PrefetchScalarGridSpec(
            num_scalar_prefetch=1,
            grid=(heads, rows // BLOCK),
            in_specs=[whole] * 5
            + [
                pl.BlockSpec((None, 1, rows), lambda h, i, high: (h, 0, 0)),
                pl.BlockSpec((1, rows), lambda h, i, high: (0, 0)),
            ],
            out_specs=[whole, own, own],
            scratch_shapes=[pltpu.VMEM((1, rows), jnp.float32)],
        ),
        out_shape=[out] * 3,
        compiler_params=pltpu.CompilerParams(vmem_limit_bytes=VMEM_BYTES),
        cost_estimate=BESIDE,
        name="attention_backward",
    )(high_block, q_b, k_b, v_b, grads, full, logs, starts)


def norm_grads_kernel(
    dq_ref, dk_ref, raw, squares, gain_q, gain_k, cosine, sine, dq_out, dk_out, dots, q_part, k_part
):
    width = dq_ref.shape[1]
    table_c, table_s = cosine[...], sine[...]
    both = squares[...]

    @pl.when(pl.program_id(0) == 0)
    def _():
        q_part[...] = jnp.zeros_like(q_part)
        k_part[...] = jnp.zeros_like(k_part)

    for index, (grad, gain, out, gain_part) in enumerate(
        ((dq_ref, gain_q, dq_out, q_part), (dk_ref, gain_k, dk_out, k_part))
    ):
        rstd = rstd_of(both, index)
        products = jnp.zeros((BLOCK, HDIM), jnp.float32)
        for head in range(width // HDIM):
            cols = slice(head * HDIM, (head + 1) * HDIM)
            base = index * width + head * HDIM
            turned = grad[:, cols]
            norm = turned * table_c - pltpu.roll(turned, HDIM // 2, 1) * table_s
            out[:, cols] = norm
            product = raw[:, base : base + HDIM] * norm
            gain_part[:, cols] += jnp.sum((product * rstd).reshape(BLOCK // 8, 8, HDIM), axis=0)
            products = products + product * gain[:, cols]
        dots[index : index + 1, :] = row_sums(products)


def norm_grads(d_q_rot, d_k_rot, raw, squares, gain_q, gain_k, cosine, sine):
    rows, width = d_q_rot.shape
    whole = pl.BlockSpec((1, width), lambda i: (0, 0))
    table = pl.BlockSpec((BLOCK, HDIM), lambda i: (i, 0))
    own = pl.BlockSpec((BLOCK, width), lambda i: (i, 0))
    pair = pl.BlockSpec((2, BLOCK), lambda i: (0, i))
    total = pl.BlockSpec((8, width), lambda i: (0, 0))
    grad = jax.ShapeDtypeStruct((rows, width), jnp.float32)
    return pl.pallas_call(
        norm_grads_kernel,
        grid=(rows // BLOCK,),
        in_specs=[
            own,
            own,
            pl.BlockSpec((BLOCK, 3 * width), lambda i: (i, 0)),
            pair,
            whole,
            whole,
            table,
            table,
        ],
        out_specs=[own, own, pair, total, total],
        out_shape=[
            grad,
            grad,
            jax.ShapeDtypeStruct((2, rows), jnp.float32),
            jax.ShapeDtypeStruct((8, width), jnp.float32),
            jax.ShapeDtypeStruct((8, width), jnp.float32),
        ],
        cost_estimate=BESIDE,
        name="norm_grads",
    )(d_q_rot, d_k_rot, raw, squares, gain_q[None], gain_k[None], cosine, sine)


def raw_grads_kernel(dq_ref, dk_ref, dv_ref, raw, squares, dots, gain_q, gain_k, out):
    width = dq_ref.shape[1]
    both, sums = squares[...], dots[...]
    for index, (grad, gain) in enumerate(((dq_ref, gain_q), (dk_ref, gain_k))):
        rstd = rstd_of(both, index)
        share = rstd * rstd * rstd * columns_of(sums, index) * (1.0 / D)
        for head in range(width // HDIM):
            cols = slice(head * HDIM, (head + 1) * HDIM)
            base = index * width + head * HDIM
            value = rstd * gain[:, cols] * grad[:, cols] - raw[:, base : base + HDIM] * share
            out[:, base : base + HDIM] = value.astype(jnp.bfloat16)
    out[:, 2 * width :] = dv_ref[...].astype(jnp.bfloat16)


def raw_grads(d_q_norm, d_k_norm, d_v, raw, squares, dots, gain_q, gain_k):
    rows, width = d_q_norm.shape
    whole = pl.BlockSpec((1, width), lambda i: (0, 0))
    own = pl.BlockSpec((BLOCK, width), lambda i: (i, 0))
    wide = pl.BlockSpec((BLOCK, 3 * width), lambda i: (i, 0))
    pair = pl.BlockSpec((2, BLOCK), lambda i: (0, i))
    return pl.pallas_call(
        raw_grads_kernel,
        grid=(rows // BLOCK,),
        in_specs=[own, own, own, wide, pair, pair, whole, whole],
        out_specs=wide,
        out_shape=jax.ShapeDtypeStruct((rows, 3 * width), jnp.bfloat16),
        cost_estimate=BESIDE,
        name="raw_grads",
    )(d_q_norm, d_k_norm, d_v, raw, squares, dots, gain_q[None], gain_k[None])


def dot(left, right):
    return jnp.dot(left, right, preferred_element_type=jnp.float32)


def contract_rows(left, right):
    return lax.dot_general(
        left, right, (((0,), (0,)), ((), ())), preferred_element_type=jnp.float32
    )


def contract_cols(left, right):
    return lax.dot_general(
        left, right, (((1,), (1,)), ((), ())), preferred_element_type=jnp.float32
    )


def column_block(rows, width):
    return min(width, 512 if rows <= 1024 else 256)


def matmul_params():
    return pltpu.CompilerParams(vmem_limit_bytes=56 * 1024 * 1024)


def hidden_kernel(x_ref, gate_w, up_w, gate_out, up_out, hidden_out):
    gate = dot(x_ref[...], gate_w[...])
    up_part = dot(x_ref[...], up_w[...])
    gate_out[...] = gate
    up_out[...] = up_part
    hidden_out[...] = (gate * jax.nn.sigmoid(gate) * up_part).astype(jnp.bfloat16)


def hidden_units(x, gate_full, up_full):
    rows, depth = x.shape
    width = gate_full.shape[1]
    block = column_block(rows, width)
    weight = pl.BlockSpec((depth, block), lambda j: (0, j))
    out = pl.BlockSpec((rows, block), lambda j: (0, j))
    return pl.pallas_call(
        hidden_kernel,
        grid=(width // block,),
        in_specs=[pl.BlockSpec((rows, depth), lambda j: (0, 0)), weight, weight],
        out_specs=[out] * 3,
        out_shape=[
            jax.ShapeDtypeStruct((rows, width), jnp.float32),
            jax.ShapeDtypeStruct((rows, width), jnp.float32),
            jax.ShapeDtypeStruct((rows, width), jnp.bfloat16),
        ],
        compiler_params=matmul_params(),
        cost_estimate=BESIDE,
        name="hidden_units",
    )(x, gate_full, up_full)


def hidden_grads_kernel(grad_ref, weight, gate_ref, up_ref, gate_out, up_out):
    d_hidden = dot(grad_ref[...], weight[...])
    gate = gate_ref[...]
    gate_sigmoid = jax.nn.sigmoid(gate)
    silu = gate * gate_sigmoid
    gate_out[...] = (
        d_hidden * up_ref[...] * (gate_sigmoid * (1.0 + gate * (1.0 - gate_sigmoid)))
    ).astype(jnp.bfloat16)
    up_out[...] = (d_hidden * silu).astype(jnp.bfloat16)


def hidden_grads(grad, down_full, gate, up_part):
    rows, depth = grad.shape
    width = down_full.shape[1]
    block = column_block(rows, width)
    part_spec = pl.BlockSpec((rows, block), lambda j: (0, j))
    out = jax.ShapeDtypeStruct((rows, width), jnp.bfloat16)
    return pl.pallas_call(
        hidden_grads_kernel,
        grid=(width // block,),
        in_specs=[
            pl.BlockSpec((rows, depth), lambda j: (0, 0)),
            pl.BlockSpec((depth, block), lambda j: (0, j)),
            part_spec,
            part_spec,
        ],
        out_specs=[part_spec] * 2,
        out_shape=[out] * 2,
        compiler_params=matmul_params(),
        cost_estimate=BESIDE,
        name="hidden_grads",
    )(grad, down_full, gate, up_part)


def products_kernel(count, *refs):
    total = None
    for left, right in zip(refs[:count], refs[count : 2 * count]):
        term = contract_cols(left[...], right[...])
        total = term if total is None else total + term
    refs[-1][...] = total.astype(jnp.bfloat16)


def sum_products(lefts, rights):
    rows, depth = lefts[0].shape
    width = rights[0].shape[0]
    block = column_block(rows, width)
    return pl.pallas_call(
        functools.partial(products_kernel, len(lefts)),
        grid=(width // block,),
        in_specs=[pl.BlockSpec((rows, depth), lambda j: (0, 0)) for _ in lefts]
        + [pl.BlockSpec((block, depth), lambda j: (j, 0)) for _ in rights],
        out_specs=pl.BlockSpec((rows, block), lambda j: (0, j)),
        out_shape=jax.ShapeDtypeStruct((rows, width), jnp.bfloat16),
        compiler_params=matmul_params(),
        cost_estimate=BESIDE,
        name="sum_products",
    )(*lefts, *rights)


def weight_grad_kernel(count, *refs):
    total = None
    for left, right in zip(refs[:count], refs[count : 2 * count]):
        term = contract_rows(left[...], right[...])
        total = term if total is None else total + term
    refs[-1][...] = total.astype(jnp.bfloat16)


def weight_grad(lefts, rights, first=0, width=None):
    height, width = lefts[0].shape[1], rights[0].shape[1] if width is None else width
    tall, wide = min(height, 512), min(width, 1024)
    blocks = width // wide
    return pl.pallas_call(
        functools.partial(weight_grad_kernel, len(lefts)),
        grid=(width // wide, height // tall),
        in_specs=[pl.BlockSpec((left.shape[0], tall), lambda j, i: (0, i)) for left in lefts]
        + [pl.BlockSpec((right.shape[0], wide), lambda j, i: (0, first * blocks + j)) for right in rights],
        out_specs=pl.BlockSpec((tall, wide), lambda j, i: (i, j)),
        out_shape=jax.ShapeDtypeStruct((height, width), jnp.bfloat16),
        compiler_params=matmul_params(),
        cost_estimate=BESIDE,
        name="weight_grad",
    )(*lefts, *rights)


def move_rows(places, wanted_first, count, rows_ref):
    wanted = wanted_first + lax.broadcasted_iota(jnp.int32, (count, places.shape[1]), 0)
    chosen = jnp.where(places == wanted, 1.0, 0.0).astype(jnp.bfloat16)
    return dot(chosen, rows_ref[...]).astype(jnp.bfloat16)


def pick_rows(places, rows_ref):
    columns = lax.broadcasted_iota(jnp.int32, (places.shape[0], rows_ref.shape[0]), 1)
    chosen = jnp.where(places == columns, 1.0, 0.0).astype(jnp.bfloat16)
    return dot(chosen, rows_ref[...]).astype(jnp.bfloat16)


def pack_kernel(places, tokens_ref, weight, packed_out, raw_out, squares_out):
    packed = pick_rows(places[...], tokens_ref)
    packed_out[...] = packed
    raw = dot(packed, weight[...])
    raw_out[...] = raw
    width = raw.shape[1] // 3
    for index in range(2):
        cols = raw[:, index * width : (index + 1) * width]
        squares_out[index : index + 1, :] = row_sums(cols * cols)


def pack(perm_row, tokens_all, qkv_full):
    rows, depth = tokens_all.shape
    width = qkv_full.shape[1]
    return pl.pallas_call(
        pack_kernel,
        grid=(rows // BLOCK,),
        in_specs=[
            pl.BlockSpec((BLOCK, 1), lambda i: (i, 0)),
            pl.BlockSpec((rows, depth), lambda i: (0, 0)),
            pl.BlockSpec((depth, width), lambda i: (0, 0)),
        ],
        out_specs=[
            pl.BlockSpec((BLOCK, depth), lambda i: (i, 0)),
            pl.BlockSpec((BLOCK, width), lambda i: (i, 0)),
            pl.BlockSpec((2, BLOCK), lambda i: (0, i)),
        ],
        out_shape=[
            jax.ShapeDtypeStruct((rows, depth), jnp.bfloat16),
            jax.ShapeDtypeStruct((rows, width), jnp.float32),
            jax.ShapeDtypeStruct((2, rows), jnp.float32),
        ],
        compiler_params=matmul_params(),
        cost_estimate=BESIDE,
        name="pack",
    )(perm_row[:, None], tokens_all, qkv_full)


def given_kernel(count, places, rows_ref, weight, moved_out, product_out):
    moved = move_rows(places[...], pl.program_id(0) * count, count, rows_ref)
    moved_out[...] = moved
    product_out[...] = contract_cols(moved, weight[...]).astype(jnp.bfloat16)


def give_back(place_row, value, weight):
    rows, depth = value.shape
    width = weight.shape[0]
    count = 512
    return pl.pallas_call(
        functools.partial(given_kernel, count),
        grid=(rows // count,),
        in_specs=[
            pl.BlockSpec((1, rows), lambda i: (0, 0)),
            pl.BlockSpec((rows, depth), lambda i: (0, 0)),
            pl.BlockSpec((width, depth), lambda i: (0, 0)),
        ],
        out_specs=[
            pl.BlockSpec((count, depth), lambda i: (i, 0)),
            pl.BlockSpec((count, width), lambda i: (i, 0)),
        ],
        out_shape=[
            jax.ShapeDtypeStruct((rows, depth), jnp.bfloat16),
            jax.ShapeDtypeStruct((rows, width), jnp.bfloat16),
        ],
        compiler_params=matmul_params(),
        cost_estimate=BESIDE,
        name="give_back",
    )(place_row[None], value, weight)


def pick_kernel(places, rows_ref, out):
    out[...] = pick_rows(places[...], rows_ref)


def pick(place_row, value):
    rows, depth = value.shape
    count = 512
    return pl.pallas_call(
        pick_kernel,
        grid=(rows // count,),
        in_specs=[
            pl.BlockSpec((count, 1), lambda i: (i, 0)),
            pl.BlockSpec((rows, depth), lambda i: (0, 0)),
        ],
        out_specs=pl.BlockSpec((count, depth), lambda i: (i, 0)),
        out_shape=jax.ShapeDtypeStruct((rows, depth), jnp.bfloat16),
        compiler_params=matmul_params(),
        cost_estimate=BESIDE,
        name="pick",
    )(place_row[:, None], value)


def rms_back(values, rstd, gain_vec, grad):
    scaled = grad * gain_vec
    row_dots = jnp.sum(values * scaled, axis=1, keepdims=True)
    return rstd * scaled - values * (rstd * rstd * rstd) * row_dots / D


def per_device(
    tokens,
    upstream,
    lengths,
    permutation,
    w_query,
    w_key,
    w_value,
    w_out,
    w_gate,
    w_up,
    w_down,
    q_gain,
    k_gain,
    attn_gain,
    ffn_gain,
):
    rank = lax.axis_index("core") * lax.axis_size("tl") + lax.axis_index("tl")
    own_rows = tokens.shape[0]
    group_rows = own_rows * 2 * lax.axis_size("tl")
    local_width = w_query.shape[1]

    own_group = lax.axis_index("core") == lax.axis_index("th")
    layout_row = jnp.concatenate([permutation, lengths], axis=1)
    layout_row = jnp.where(own_group, layout_row, swap(layout_row, "core"))[0]
    perm_row, length_row = layout_row[:group_rows], layout_row[group_rows:]

    tokens_all, qkv_full, out_full, gate_pair = enter(
        tokens,
        [((w_query, w_key, w_value), True), ((w_out.T,), True), ((w_gate,), False)],
    )
    gate_full = gather_weight(gate_pair)
    up_shard, tokens_all = lax.optimization_barrier((w_up, tokens_all))
    up_pair = pair_of_weight(up_shard)
    tokens = lax.dynamic_slice_in_dim(tokens_all, rank * own_rows, own_rows)

    perm_place = row_place(perm_row, own_rows)
    position, starts = layout(length_row, group_rows)
    cosine, sine = rotary_tables(position)
    blocks = group_rows // BLOCK
    low_block = starts[::BLOCK] // BLOCK
    last_keys = (jnp.arange(blocks, dtype=jnp.int32) + 1) * BLOCK - 1
    reached = jnp.sum((starts[None, :] <= last_keys[:, None]).astype(jnp.int32), axis=1)
    high_block = (reached - 1) // BLOCK

    packed, raw, squares = pack(perm_row, tokens_all, qkv_full)
    up_pair, raw = lax.optimization_barrier((up_pair, raw))
    up_full = gather_weight(up_pair)
    squares = sum_over(squares, RANK)
    down_shard, squares = lax.optimization_barrier((w_down.T, squares))
    down_pair = pair_of_weight(down_shard)
    gain_q = lax.dynamic_slice_in_dim(q_gain, rank * local_width, local_width)
    gain_k = lax.dynamic_slice_in_dim(k_gain, rank * local_width, local_width)
    q_b, k_b, v_b = prepare(raw, squares, gain_q, gain_k, cosine, sine)
    attn_b, attn_f, logs = attention_forward(q_b, k_b, v_b, starts[None], low_block)

    parts = PARTS if small_grid() else 1
    part_rows = own_rows // parts

    def part_of(value, index):
        return part(value, 0, index, parts)

    def pieces_of(value, index):
        whole = part_of(value, index)
        return [part(whole, 0, 0, 2), part(whole, 0, 1, 2)] if small_grid() else [whole]

    sides = 2 if small_grid() else 1
    attn_given, attn_parts = give_back(perm_place, attn_b, out_full)
    down_pair, attn_parts = lax.optimization_barrier((down_pair, attn_parts))
    down_full = gather_weight(down_pair)
    order = [(side, index) for side in range(sides) for index in range(parts)]
    token = None

    def pass_through(make_rows, begin, finish, late, between=None):
        nonlocal token
        gathered, far_pieces, begun, sums, scattered = {}, {}, {}, {}, []

        def complete(side, index):
            nonlocal token
            sums[side, index] = finish(*begun[side, index], token)
            token = sums[side, index]

        def scatter(index):
            scattered.append(start_scatter([sums[side, index] for side in range(sides)]))

        for side, index in order:
            if side == 0:
                gathered[index] = start_gather(make_rows(index, token))
                if sides == 2 and index > 0:
                    far_pieces[index - 1] = forward_rows(gathered[index - 1], token)
                piece = gathered[index][0]
            else:
                if index == 0:
                    far_pieces[parts - 1] = forward_rows(gathered[parts - 1], token)
                    if between is not None:
                        near = [gathered[each][0] for each in range(parts)]
                        token = between(near, [far_pieces[each] for each in range(parts)], token)
                piece = far_pieces[index]
            begun[side, index] = begin((index, side), piece, token)
            token = begun[side, index][0]
            if not late:
                complete(side, index)
                if side == sides - 1:
                    scatter(index)
        if late:
            for index in range(parts):
                for side in reversed(range(sides)):
                    complete(side, index)
                scatter(index)
        return scattered

    attn_sums = [start_scatter(pieces_of(attn_parts, index)) for index in range(parts)]
    attn_outs, resids, saved = [], [], {}

    def resid_rows(index, token):
        attn_out = finish_scatter_rows(attn_sums[index], token)
        rstd_a = lax.rsqrt(jnp.mean(attn_out * attn_out, axis=1, keepdims=True) + epsilon)
        attn_outs.append((attn_out, rstd_a))
        resids.append(part_of(tokens, index).astype(jnp.float32) + attn_out * rstd_a * attn_gain)
        return resids[-1].astype(jnp.bfloat16)

    def feed_forward(key, piece, token):
        gate, up_part, hidden_b = hidden_units(after(token, piece), gate_full, up_full)
        saved[key] = (piece, gate, up_part, hidden_b)
        return (hidden_b,)

    def feed_down(hidden_b, token):
        return sum_products([after(token, hidden_b)], [down_full])

    upstream_turn = start_turn(after(attn_parts, upstream))
    mlp_sums = pass_through(resid_rows, feed_forward, feed_down, True)
    token, upstream_turn = lax.optimization_barrier((token, upstream_turn))
    upstream = finish_turn(*upstream_turn)
    layer_outs, gain_parts, grads_f, back = [], [], [], {}

    def d_mlp_rows(index, token):
        mlp_out = finish_scatter_rows(mlp_sums[index], token)
        rstd_m = lax.rsqrt(jnp.mean(mlp_out * mlp_out, axis=1, keepdims=True) + epsilon)
        normed_m = mlp_out * rstd_m
        layer_outs.append((resids[index] + normed_m * ffn_gain).astype(jnp.bfloat16))
        grads_f.append(part_of(upstream, index).astype(jnp.float32))
        gain_parts.append(jnp.sum(grads_f[index] * normed_m, axis=0))
        return rms_back(mlp_out, rstd_m, ffn_gain, grads_f[index]).astype(jnp.bfloat16)

    def feed_back(key, piece, token):
        _, gate, up_part, _ = saved[key]
        d_gate_b, d_up_b = hidden_grads(after(token, piece), down_full, gate, up_part)
        back[key] = (piece, d_gate_b, d_up_b)
        return d_gate_b, d_up_b

    def feed_up(d_gate_b, d_up_b, token):
        return sum_products([after(token, d_gate_b), d_up_b], [gate_full, up_full])

    weight_grads = []

    def first_weight_grad(near, far, token):
        grads = [piece for index in range(parts) for piece in (near[index], far[index])]
        weight_grads.append(weight_grad(after(token, grads), [saved[key][3] for key in sorted(saved)]))
        return weight_grads[0]

    resid_sums = pass_through(d_mlp_rows, feed_back, feed_up, False, first_weight_grad)
    layer_out = jnp.concatenate(layer_outs, axis=0)
    keys = sorted(saved)
    ffn_gain_part = sum(gain_parts)
    attn_gain_part = 0.0
    d_resids, gathered = [], []
    operands = [
        ([back[key][0] for key in keys], [saved[key][3] for key in keys]),
        ([saved[key][0] for key in keys], [back[key][1] for key in keys]),
        ([saved[key][0] for key in keys], [back[key][2] for key in keys]),
    ]

    def next_weight_grad(token):
        left, right = operands[len(weight_grads)]
        left, right = after(token, (left, right))
        weight_grads.append(weight_grad(left, right))
        return weight_grads[-1]

    for index in range(parts):
        terms = resid_sums[index]
        if index == 0:
            d_sums = finish_scatter_rows(terms, token)
        else:
            last, weight_grads[-1] = lax.optimization_barrier((terms[-1], weight_grads[-1]))
            d_sums = finish_scatter_rows([*terms[:-1], last], None)
        attn_out, rstd_a = attn_outs[index]
        d_resid = grads_f[index] + d_sums
        d_resids.append(d_resid)
        attn_gain_part = attn_gain_part + jnp.sum(d_resid * attn_out * rstd_a, axis=0)
        d_attn_b = rms_back(attn_out, rstd_a, attn_gain, d_resid).astype(jnp.bfloat16)
        gathered.append(start_gather(d_attn_b))
        token = next_weight_grad((d_attn_b, token))
    far_pieces = []
    for index in range(parts):
        if sides == 2:
            far, weight_grads[-1] = lax.optimization_barrier((gathered[index][1], weight_grads[-1]))
            far_pieces.append(jnp.concatenate([far, swap(far, "core")], axis=0))
            token = far
        if len(weight_grads) < 3:
            token = next_weight_grad(token)
    while len(weight_grads) < 3:
        token = next_weight_grad(token)
    down_grad, gate_grad, up_grad = weight_grads
    d_attn_pieces = []
    for index in range(parts):
        d_attn_pieces.append(gathered[index][0])
        if sides == 2:
            d_attn_pieces.append(far_pieces[index])
    d_givens = [dot(piece, out_full).astype(jnp.bfloat16) for piece in d_attn_pieces]
    d_resid = jnp.concatenate(d_resids, axis=0)
    d_given_b = jnp.concatenate(d_givens, axis=0)
    out_total = weight_grad(
        d_attn_pieces,
        [piece for index in range(parts) for piece in pieces_of(attn_given, index)],
    )
    d_given_b, out_total = lax.optimization_barrier((d_given_b, out_total))
    down_split, gate_split = start_split(scatter_pair(down_grad)), start_split(scatter_pair(gate_grad))
    up_sum = scatter_pair(up_grad)
    d_packed = pick(perm_place, d_given_b)
    d_q_rot, d_k_rot, d_v = attention_backward(
        q_b, k_b, v_b, d_packed, attn_f, logs, starts[None], high_block
    )
    d_q_rot, down_split, gate_split = lax.optimization_barrier((d_q_rot, down_split, gate_split))
    d_q_norm, d_k_norm, dots, q_parts, k_parts = norm_grads(
        d_q_rot, d_k_rot, raw, squares, gain_q, gain_k, cosine, sine
    )
    up_split = start_split(after(d_q_norm, up_sum))
    layer_turn = start_turn(after(d_q_norm, layer_out))
    q_gain_part, k_gain_part = jnp.sum(q_parts, axis=0), jnp.sum(k_parts, axis=0)
    dots = sum_over(dots, RANK)
    d_qkv_b = raw_grads(d_q_norm, d_k_norm, d_v, raw, squares, dots, gain_q, gain_k)
    qkv_totals = [weight_grad([packed], [d_qkv_b], index, local_width) for index in range(3)]
    last_total, d_qkv_b = lax.optimization_barrier((qkv_totals[-1], d_qkv_b))
    _, input_parts = give_back(perm_place, d_qkv_b, qkv_full)
    input_parts, up_split, layer_turn = lax.optimization_barrier((input_parts, up_split, layer_turn))
    layer_out = finish_turn(*layer_turn)
    down_shard = finish_split(*down_split).T
    gate_shard, up_shard = finish_split(*gate_split), finish_split(*up_split)

    def placed(part_sum):
        return lax.dynamic_update_slice_in_dim(
            jnp.zeros((D,), jnp.float32), part_sum, rank * local_width, 0
        )

    gains = jnp.stack(
        [placed(q_gain_part), placed(k_gain_part), attn_gain_part, ffn_gain_part]
        + [jnp.zeros((D,), jnp.float32)] * 4
    )
    tokens_grad, gain_grads, out_shard, query_shard, key_shard, value_shard = leave(
        input_parts,
        d_resid,
        gains,
        [
            (out_total, [local_width], False),
            *[(total, [local_width], False) for total in qkv_totals],
        ],
    )

    return (
        layer_out,
        tokens_grad,
        query_shard,
        key_shard,
        value_shard,
        out_shard.T,
        gate_shard,
        up_shard,
        down_shard,
        gain_grads[0],
        gain_grads[1],
        gain_grads[2],
        gain_grads[3],
    )


def solution(mesh):
    dp, tensor = mesh.shape["dp"], mesh.shape["tensor"]
    fine = Mesh(mesh.devices.reshape(dp // 4, 2, 2, 2, tensor // 2), DP + TENSOR)
    rows, weight, weight_out = P(DP + TENSOR, None), P(DP, TENSOR), P(TENSOR, DP)
    return jax.shard_map(
        per_device,
        mesh=fine,
        in_specs=(rows, rows, P(DP, None), P(DP, None))
        + (weight,) * 3
        + (weight_out, weight, weight, weight_out)
        + (P(),) * 4,
        out_specs=(rows, rows)
        + (weight,) * 3
        + (weight_out, weight, weight, weight_out)
        + (P(),) * 4,
        check_vma=False,
    )
```

```python
import functools
import math

import jax
import jax.numpy as jnp
from jax import lax
from jax.experimental import pallas as pl
from jax.experimental.pallas import tpu as pltpu
from jax.sharding import Mesh, PartitionSpec as P

D = 2048
HDIM = 128

epsilon = 1e-06
rope_base = 500000.0
masked_score = -1e30
BLOCK = 256
VMEM_BYTES = 48 * 1024 * 1024
MESH = pl.DeviceIdType.MESH
BESIDE = pl.CostEstimate(flops=1, bytes_accessed=1, transcendentals=0)
PARTS = 2

SWAP = [(0, 1), (1, 0)]
TURN = [(1, 2), (2, 1)]
CYCLE = [(0, 1), (1, 3), (3, 2), (2, 0)]
CYCLE_BACK = [(d, s) for s, d in CYCLE]
DP = ("a", "b", "core")
TENSOR = ("th", "tl")
RANK = ("core", "tl")


def swap(value, axis):
    return lax.ppermute(value, axis, SWAP)


def start_turn(value):
    return value, lax.ppermute(value, ("core", "th"), TURN)


def finish_turn(kept, arrived):
    stays = lax.axis_index("core") == lax.axis_index("th")
    return jnp.where(stays, kept, arrived)


def turn(value):
    return finish_turn(*start_turn(value))


def small_grid():
    return lax.axis_size("a") == 2 and lax.axis_size("tl") == 2


def part(value, dim, index, count):
    size = value.shape[dim] // count
    return lax.slice_in_dim(value, index * size, (index + 1) * size, axis=dim)


def in_turn(left, right):
    upper = lax.axis_index("th") == 0
    return jnp.where(upper, left, right), jnp.where(upper, right, left)


def pair_of_weight(shard):
    second = lax.ppermute(shard, ("core", "th"), CYCLE)
    return jnp.concatenate(in_turn(turn(shard), second), axis=0)


def gather_weight(pair):
    return lax.all_gather(pair, ("a", "b"), axis=0, tiled=True)


def scatter_pair(total):
    return lax.psum_scatter(
        total.astype(jnp.bfloat16), ("a", "b"), scatter_dimension=0, tiled=True
    )


def start_split(pair):
    first, second = in_turn(part(pair, 0, 0, 2), part(pair, 0, 1, 2))
    return first, start_turn(first)[1], lax.ppermute(second, ("core", "th"), CYCLE_BACK)


def finish_split(first, arrived, other):
    return finish_turn(first, arrived).astype(jnp.float32) + other.astype(jnp.float32)


def greet():
    a, b, core = lax.axis_index("a"), lax.axis_index("b"), lax.axis_index("core")
    th, tl = lax.axis_index("th"), lax.axis_index("tl")
    barrier = pltpu.get_barrier_semaphore()
    others = (
        {"a": 1 - a},
        {"b": 1 - b},
        {"core": 1 - core},
        {"tl": 1 - tl},
        {"th": 1 - th},
        {"core": 1 - core, "th": 1 - th},
    )
    for other in others:
        pl.semaphore_signal(barrier, inc=1, device_id=other, device_id_type=MESH)
    pl.semaphore_wait(barrier, len(others))


CHUNKS = 4


def entry_slots(plan):
    return 4 * CHUNKS + sum(3 * len(units) + 6 for units, _ in plan)


def entry_kernel(plan, *refs):
    shard_count = sum(len(units) for units, _ in plan)
    tokens, shards = refs[0], refs[1 : 1 + shard_count]
    tokens_all, fulls = refs[1 + shard_count], refs[2 + shard_count : -3]
    send, recv, local = refs[-3:]
    a, b, core = lax.axis_index("a"), lax.axis_index("b"), lax.axis_index("core")
    th, tl = lax.axis_index("th"), lax.axis_index("tl")
    stays = core == th
    greet()
    used = [0]

    def slots(count):
        used[0] += count
        return used[0] - count

    def remote(source, target, slot, to):
        return pltpu.make_async_remote_copy(
            src_ref=source,
            dst_ref=target,
            send_sem=send.at[slot],
            recv_sem=recv.at[slot],
            device_id=to,
            device_id_type=MESH,
        )

    def arrived(target, slot):
        remote(target, target, slot, {"core": 1 - core}).wait_recv()

    stages, taken = [], 0
    for full, (units, rings) in zip(fulls, plan):
        stage = []
        for column in units:
            shard = shards[taken]
            base = slots(3)
            height, width = shard.shape

            def place(sub, full=full, column=column, height=height, width=width, rings=rings):
                block = 4 * a + 2 * b if rings else 0
                row = pl.multiple_of((block + sub) * height, height)
                return full.at[pl.ds(row, height), pl.ds(column, width)]

            stage.append((shard, place, base, taken))
            taken += 1
        stages.append(stage)

    def near_copy(shard, place, base):
        return remote(shard, place(core), base + 2, {"core": 1 - core})

    def far_copy(shard, place, base):
        return remote(shard, place(core), base + core, {"core": th, "th": 1 - th})

    def start_stage(stage):
        for shard, place, base, index in stage:
            far_copy(shard, place, base).start()

            @pl.when(stays)
            def _():
                pltpu.make_async_copy(shard, place(core), local.at[index]).start()

            @pl.when(jnp.logical_not(stays))
            def _():
                near_copy(shard, place, base).start()

    def finish_stage(stage):
        for shard, place, base, index in stage:

            @pl.when(stays)
            def _():
                pltpu.make_async_copy(shard, place(core), local.at[index]).wait()
                arrived(place(1 - core), base + 2)

            @pl.when(jnp.logical_not(stays))
            def _():
                arrived(place(0), base)
                arrived(place(1), base + 1)

    def piece(full, block_a, block_b, sub):
        height = full.shape[0] // 8
        row = pl.multiple_of((4 * block_a + 2 * block_b + sub) * height, height)
        return full.at[pl.ds(row, height), :]

    def ring(full, base):
        to_a, to_b = {"a": 1 - a}, {"b": 1 - b}
        return (
            [remote(piece(full, a, b, sub), piece(full, a, b, sub), base + sub, to_b) for sub in (0, 1)],
            [remote(piece(full, a, b, sub), piece(full, a, b, sub), base + 2 + sub, to_a) for sub in (0, 1)],
            remote(piece(full, a, 1 - b, 0), piece(full, a, 1 - b, 0), base + 4, to_a),
            remote(piece(full, 1 - a, b, 1), piece(full, 1 - a, b, 1), base + 5, to_b),
        )

    ring_base = [slots(6) for _ in fulls]

    def start_ring(index):
        over_b, over_a, _, _ = ring(fulls[index], ring_base[index])
        for copy in (over_b[0], over_a[1], over_b[1], over_a[0]):
            copy.start()

    def forward_ring(index):
        full, base = fulls[index], ring_base[index]
        arrived(piece(full, a, 1 - b, 0), base)
        ring(full, base)[2].start()
        arrived(piece(full, 1 - a, b, 1), base + 3)
        ring(full, base)[3].start()

    def finish_ring(index):
        full, base = fulls[index], ring_base[index]
        arrived(piece(full, a, 1 - b, 1), base + 1)
        arrived(piece(full, 1 - a, b, 0), base + 2)
        arrived(piece(full, 1 - a, 1 - b, 0), base + 4)
        arrived(piece(full, 1 - a, 1 - b, 1), base + 5)
        over_b, over_a, first, second = ring(full, base)
        for copy in (*over_b, *over_a, first, second):
            copy.wait_send()

    rows = tokens.shape[0]
    step = rows // CHUNKS
    row_base = slots(4 * CHUNKS)

    def rows_of(block_core, block_tl, chunk):
        row = pl.multiple_of((2 * block_core + block_tl) * rows + chunk * step, step)
        return tokens_all.at[pl.ds(row, step), :]

    def row_copies(chunk):
        slot = row_base + 4 * chunk
        own, other = rows_of(core, tl, chunk), rows_of(core, 1 - tl, chunk)
        return (
            remote(
                tokens.at[pl.ds(chunk * step, step), :],
                rows_of(th, tl, chunk),
                slot,
                {"core": th, "th": core},
            ),
            remote(own, own, slot + 1, {"tl": 1 - tl}),
            remote(own, own, slot + 2, {"core": 1 - core}),
            remote(other, other, slot + 3, {"core": 1 - core}),
        )

    def own_rows(chunk):
        return pltpu.make_async_copy(
            tokens.at[pl.ds(chunk * step, step), :],
            rows_of(core, tl, chunk),
            local.at[shard_count + chunk],
        )

    for chunk in range(CHUNKS):

        @pl.when(stays)
        def _():
            own_rows(chunk).start()

    ringed = [index for index, (_, rings) in enumerate(plan) if rings]
    for index in ringed:
        start_stage(stages[index])
    for chunk in range(CHUNKS):

        @pl.when(jnp.logical_not(stays))
        def _():
            row_copies(chunk)[0].start()

        @pl.when(stays)
        def _():
            own_rows(chunk).wait()
            row_copies(chunk)[1].start()
            row_copies(chunk)[2].start()

    for index in ringed:
        finish_stage(stages[index])
        start_ring(index)
    for index in range(len(plan)):
        if index not in ringed:
            start_stage(stages[index])
    for chunk in range(CHUNKS):

        @pl.when(jnp.logical_not(stays))
        def _():
            arrived(rows_of(core, tl, chunk), row_base + 4 * chunk)
            row_copies(chunk)[1].start()
            row_copies(chunk)[2].start()

    for index in ringed:
        forward_ring(index)
    for chunk in range(CHUNKS):
        arrived(rows_of(core, 1 - tl, chunk), row_base + 4 * chunk + 1)
        row_copies(chunk)[3].start()
    for index in ringed:
        finish_ring(index)
    for index in range(len(plan)):
        if index not in ringed:
            finish_stage(stages[index])
    for chunk in range(CHUNKS):
        arrived(rows_of(1 - core, tl, chunk), row_base + 4 * chunk + 2)
        arrived(rows_of(1 - core, 1 - tl, chunk), row_base + 4 * chunk + 3)

        @pl.when(jnp.logical_not(stays))
        def _():
            row_copies(chunk)[0].wait_send()

        for copy in row_copies(chunk)[1:]:
            copy.wait_send()
    for stage in stages:
        for shard, place, base, _ in stage:
            far_copy(shard, place, base).wait_send()

            @pl.when(jnp.logical_not(stays))
            def _():
                near_copy(shard, place, base).wait_send()


def leave_kernel(cuts, paired, stacks, *refs):
    count = len(cuts)
    ringed = [index for index in range(count) if not paired[index]]
    partial, resid, gains, given = refs[0], refs[1], refs[2], refs[3 : 3 + len(stacks)]
    totals = []
    for ref, stack in zip(given, stacks):
        totals += [ref] if stack == 1 else [ref.at[k] for k in range(stack)]
    taken = 3 + len(stacks)
    outs = refs[taken : taken + 2 + sum(len(cut) for cut in cuts)]
    rows_out, gains_out, shard_outs = outs[0], outs[1], outs[2:]
    scratch = refs[taken + len(outs) :]
    peer_far, peer_near, far_sum, from_far, done_rows = scratch[:5]
    boxes, taken = [], 5
    for alone in paired:
        boxes.append(scratch[taken : taken + (1 if alone else 8)])
        taken += 1 if alone else 8
    gain_box, send, recv, local = scratch[-4:]
    a, b, core = lax.axis_index("a"), lax.axis_index("b"), lax.axis_index("core")
    th, tl = lax.axis_index("th"), lax.axis_index("tl")
    stays = core == th
    to_a, to_b, to_core, to_tl = {"a": 1 - a}, {"b": 1 - b}, {"core": 1 - core}, {"tl": 1 - tl}
    greet()

    def remote(source, target, slot, to, send_slot=None):
        return pltpu.make_async_remote_copy(
            src_ref=source,
            dst_ref=target,
            send_sem=send.at[slot if send_slot is None else send_slot],
            recv_sem=recv.at[slot],
            device_id=to,
            device_id_type=MESH,
        )

    def arrived(target, slot):
        remote(target, target, slot, to_core).wait_recv()

    def add(target, target_row, height, *sources):
        step = 16

        def one(index, unused):
            value = None
            for source, first in sources:
                here = pl.ds(pl.multiple_of(first + index * step, step), step)
                term = source[here, :].astype(jnp.float32)
                value = term if value is None else value + term
            there = pl.ds(pl.multiple_of(target_row + index * step, step), step)
            target[there, :] = value.astype(target.dtype)
            return unused

        lax.fori_loop(0, height // step, one, 0)

    rows = resid.shape[0]
    step = rows // CHUNKS

    own, peer, far, peer_of_far = range(4)

    size = rows // PARTS

    def row_of(block, chunk):
        place = chunk * step
        return (place // size) * 4 * size + block * size + place % size

    def at(ref, row):
        return ref.at[pl.ds(row, step), :]

    def row_copies(chunk):
        here = chunk * step
        return (
            remote(at(partial, row_of(peer_of_far, chunk)), at(peer_far, here), 4 * chunk, to_core),
            remote(at(partial, row_of(peer, chunk)), at(peer_near, here), 4 * chunk + 1, to_core),
            remote(at(far_sum, here), at(from_far, here), 4 * chunk + 2, to_tl),
            remote(at(done_rows, here), at(rows_out, here), 4 * chunk + 3, {"core": th, "th": core}),
        )

    def kept_rows(chunk):
        here = chunk * step
        return pltpu.make_async_copy(at(done_rows, here), at(rows_out, here), local.at[chunk])

    base = 4 * CHUNKS

    def piece(ref, block_a, block_b, sub):
        height = ref.shape[0] // 8
        return pl.multiple_of((4 * block_a + 2 * block_b + sub) * height, height), height

    def slice_of(ref, block_a, block_b, sub):
        row, height = piece(ref, block_a, block_b, sub)
        return ref.at[pl.ds(row, height), :]

    def copies(index):
        total = totals[index]
        _, over_a, over_b, send_b, send_a, from_b, from_a, _ = boxes[index]
        slot = base + 10 * index
        height = total.shape[0] // 8

        def half(ref, sub):
            return ref.at[pl.ds(sub * height, height), :]

        return (
            remote(slice_of(total, 1 - a, 1 - b, 0), over_a, slot, to_a),
            remote(slice_of(total, 1 - a, 1 - b, 1), over_b, slot + 1, to_b),
            remote(slice_of(total, a, 1 - b, 1), half(from_b, 1), slot + 2, to_b),
            remote(slice_of(total, 1 - a, b, 0), half(from_a, 0), slot + 3, to_a),
            remote(send_b, half(from_b, 0), slot + 4, to_b),
            remote(send_a, half(from_a, 1), slot + 5, to_a),
        )

    def own_sum(index, sub):
        sums = totals[index] if paired[index] else boxes[index][7]
        height = sums.shape[0] // 2
        return sums.at[pl.ds(pl.multiple_of(sub * height, height), height), :]

    def last_copies(index):
        inbox = boxes[index][0]
        slot = base + 10 * index + 6
        return (
            remote(own_sum(index, 1 - core), inbox.at[0], slot, to_core),
            remote(own_sum(index, 0), inbox.at[1], slot + 1, {"core": 0, "th": core}),
            remote(own_sum(index, 1), inbox.at[1], slot + 1, {"core": 1, "th": core}, slot + 2),
        )

    def start_last(index):
        @pl.when(stays)
        def _():
            last_copies(index)[0].start()

        @pl.when(jnp.logical_not(stays))
        def _():
            last_copies(index)[1].start()
            last_copies(index)[2].start()

    gain_axes = ({"core": 1 - core}, {"tl": 1 - tl}, {"b": 1 - b}, {"a": 1 - a}, {"th": 1 - th})

    def gain_copy(turn_index):
        source = gains if turn_index == 0 else gain_box.at[4 + turn_index]
        return remote(
            source,
            gain_box.at[turn_index],
            base + 10 * count + turn_index,
            gain_axes[turn_index],
        )

    def gain_step(turn_index):
        arrived(gain_box.at[turn_index], base + 10 * count + turn_index)
        mine = gains[...] if turn_index == 0 else gain_box[4 + turn_index]
        total = mine + gain_box[turn_index]
        if turn_index == 4:
            gains_out[...] = total
        else:
            gain_box[5 + turn_index] = total
            gain_copy(turn_index + 1).start()

    def start_ring(index):
        for copy in copies(index)[:4]:
            copy.start()

    def turn_ring(index):
        total = totals[index]
        _, over_a, over_b, send_b, send_a, _, _, _ = boxes[index]
        height = total.shape[0] // 8
        arrived(over_a, base + 10 * index)
        add(send_b, 0, height, (total, piece(total, a, 1 - b, 0)[0]), (over_a, 0))
        copies(index)[4].start()
        arrived(over_b, base + 10 * index + 1)
        add(send_a, 0, height, (total, piece(total, 1 - a, b, 1)[0]), (over_b, 0))
        copies(index)[5].start()

    def finish_ring(index):
        total = totals[index]
        _, _, _, _, _, from_b, from_a, sums = boxes[index]
        height = total.shape[0] // 8
        slot = base + 10 * index
        for sub in (0, 1):
            arrived(from_b.at[pl.ds(sub * height, height), :], slot + (4 if sub == 0 else 2))
            arrived(from_a.at[pl.ds(sub * height, height), :], slot + (3 if sub == 0 else 5))
            add(
                sums,
                sub * height,
                height,
                (total, piece(total, a, b, sub)[0]),
                (from_b, sub * height),
                (from_a, sub * height),
            )
        start_last(index)

    def finish_chunk(chunk):
        here = chunk * step
        arrived(at(peer_near, here), 4 * chunk + 1)
        arrived(at(from_far, here), 4 * chunk + 2)
        add(
            done_rows,
            here,
            step,
            (partial, row_of(own, chunk)),
            (peer_near, here),
            (from_far, here),
            (resid, here),
        )

        @pl.when(stays)
        def _():
            kept_rows(chunk).start()

        @pl.when(jnp.logical_not(stays))
        def _():
            row_copies(chunk)[3].start()

    for chunk in range(CHUNKS):
        row_copies(chunk)[0].start()
    for chunk in range(CHUNKS):
        row_copies(chunk)[1].start()
    for index in range(count):
        if paired[index]:
            start_last(index)
    for chunk in range(CHUNKS):
        arrived(at(peer_far, chunk * step), 4 * chunk)
        add(
            far_sum,
            chunk * step,
            step,
            (partial, row_of(far, chunk)),
            (peer_far, chunk * step),
        )
        row_copies(chunk)[2].start()
    for index in ringed:
        start_ring(index)
    gain_copy(0).start()
    gain_step(0)
    for place in range(max(len(ringed), CHUNKS)):
        if place < len(ringed):
            turn_ring(ringed[place])
        if place < CHUNKS:
            finish_chunk(place)
    for step_index in (1, 2, 3):
        gain_step(step_index)
    for index in ringed:
        finish_ring(index)
    gain_step(4)
    for index, cut in sorted(enumerate(cuts), key=lambda pair: not paired[pair[0]]):
        inbox = boxes[index][0]
        sums = totals[index] if paired[index] else boxes[index][-1]
        height = inbox.shape[1]
        slot = base + 10 * index + 6
        taken = sum(len(other) for other in cuts[:index])
        arrived(inbox.at[1], slot + 1)

        @pl.when(jnp.logical_not(stays))
        def _():
            arrived(inbox.at[0], slot)

        def one(step_index, unused, cut=cut, taken=taken, sums=sums, inbox=inbox, height=height):
            row = pl.multiple_of(step_index * 16, 16)
            here = pl.ds(row, 16)
            other = inbox[1, here, :].astype(jnp.float32)

            def store(value):
                first = 0
                for offset, end in enumerate(cut):
                    shard_outs[taken + offset][here, :] = (value + other)[:, first:end]
                    first = end

            @pl.when(stays)
            def _():
                own_row = pl.multiple_of(core * height + row, 16)
                store(sums[pl.ds(own_row, 16), :].astype(jnp.float32))

            @pl.when(jnp.logical_not(stays))
            def _():
                store(inbox[0, here, :].astype(jnp.float32))

            return unused

        lax.fori_loop(0, height // 16, one, 0)
    for chunk in range(CHUNKS):
        for copy in row_copies(chunk)[:3]:
            copy.wait_send()

        @pl.when(stays)
        def _():
            kept_rows(chunk).wait()

        @pl.when(jnp.logical_not(stays))
        def _():
            row_copies(chunk)[3].wait_send()
            arrived(at(rows_out, chunk * step), 4 * chunk + 3)

    for turn_index in range(5):
        gain_copy(turn_index).wait_send()
    for index in ringed:
        for copy in copies(index):
            copy.wait_send()
    for index in range(count):

        @pl.when(stays)
        def _():
            last_copies(index)[0].wait_send()

        @pl.when(jnp.logical_not(stays))
        def _():
            last_copies(index)[1].wait_send()
            last_copies(index)[2].wait_send()


def unstacked(totals):
    flat = []
    for total, parts, alone in totals:
        for matrix in [total] if total.ndim == 2 else [total[k] for k in range(total.shape[0])]:
            flat.append((matrix, parts, alone))
    return flat


def leave(partial, resid, gains, totals):
    if not small_grid():
        summed = finish_scatter_rows(start_scatter([partial.astype(jnp.bfloat16)]), None)
        shards = []
        for total, parts, alone in unstacked(totals):
            shard, first = finish_split(*start_split(total if alone else scatter_pair(total))), 0
            for width in parts:
                shards.append(shard[:, first : first + width])
                first += width
        total_gains = sum_over(gains, DP + TENSOR)
        return [turn((resid + summed).astype(jnp.bfloat16)), total_gains] + shards
    rows, columns = resid.shape
    cuts, scratch = [], []
    outs = [
        jax.ShapeDtypeStruct((rows, columns), jnp.bfloat16),
        jax.ShapeDtypeStruct(gains.shape, jnp.float32),
    ]
    stacks = tuple(1 if total.ndim == 2 else total.shape[0] for total, _, _ in totals)
    arrays = [total.astype(jnp.bfloat16) for total, _, _ in totals]
    for total, parts, alone in unstacked(totals):
        height, width = total.shape[0] // (2 if alone else 8), total.shape[1]
        cuts.append(tuple(sum(parts[: index + 1]) for index in range(len(parts))))
        outs += [jax.ShapeDtypeStruct((height, part_width), jnp.float32) for part_width in parts]
        shapes = [(2, height, width)]
        if not alone:
            shapes += [(height, width)] * 4 + [(2 * height, width)] * 3
        scratch += [pltpu.VMEM(shape, jnp.bfloat16) for shape in shapes]
    paired = tuple(alone for _, _, alone in unstacked(totals))
    slots = 4 * CHUNKS + 10 * len(paired) + 5
    vmem = pl.BlockSpec(memory_space=pltpu.VMEM)
    return pl.pallas_call(
        functools.partial(leave_kernel, tuple(cuts), paired, stacks),
        in_specs=[vmem] * (3 + len(totals)),
        out_specs=[pl.BlockSpec(memory_space=pl.ANY)] + [vmem] * (len(outs) - 1),
        out_shape=outs,
        scratch_shapes=[pltpu.VMEM((rows, columns), jnp.bfloat16)] * 5
        + scratch
        + [
            pltpu.VMEM((9, *gains.shape), jnp.float32),
            pltpu.SemaphoreType.DMA((slots,)),
            pltpu.SemaphoreType.DMA((slots,)),
            pltpu.SemaphoreType.DMA((CHUNKS,)),
        ],
        compiler_params=pltpu.CompilerParams(
            collective_id=1, has_side_effects=True, vmem_limit_bytes=60 * 1024 * 1024
        ),
        cost_estimate=BESIDE,
        name="leave",
    )(partial.astype(jnp.bfloat16), resid, gains, *arrays)


def enter(tokens, matrices):
    if not small_grid():
        own = turn(tokens)
        pairs = [
            (pair_of_weight(jnp.concatenate(shards, axis=1)), whole) for shards, whole in matrices
        ]
        return [lax.all_gather(own, RANK, axis=0, tiled=True)] + [
            gather_weight(pair) if whole else pair for pair, whole in pairs
        ]
    plan, outs = [], [jax.ShapeDtypeStruct((4 * tokens.shape[0], tokens.shape[1]), tokens.dtype)]
    for shards, whole in matrices:
        columns = [0]
        for shard in shards:
            columns.append(columns[-1] + shard.shape[1])
        plan.append((tuple(columns[:-1]), whole))
        height = (8 if whole else 2) * shards[0].shape[0]
        outs.append(jax.ShapeDtypeStruct((height, columns[-1]), tokens.dtype))
    flat = [shard for shards, _ in matrices for shard in shards]
    slots = entry_slots(plan)
    anywhere = pl.BlockSpec(memory_space=pl.ANY)
    return pl.pallas_call(
        functools.partial(entry_kernel, tuple(plan)),
        in_specs=[anywhere] * (1 + len(flat)),
        out_specs=[anywhere] * len(outs),
        out_shape=outs,
        scratch_shapes=[
            pltpu.SemaphoreType.DMA((slots,)),
            pltpu.SemaphoreType.DMA((slots,)),
            pltpu.SemaphoreType.DMA((len(flat) + CHUNKS,)),
        ],
        compiler_params=pltpu.CompilerParams(collective_id=0, has_side_effects=True),
        cost_estimate=BESIDE,
        name="enter",
    )(tokens, *flat)


def row_place(row, own_rows):
    if not small_grid():
        return row
    mask = 2 * lax.axis_index("core") + lax.axis_index("tl")
    block = (row // own_rows) ^ mask
    block = (block // 2) + 2 * (block % 2)
    size = own_rows // PARTS
    place = row % own_rows
    return (place // size) * 4 * size + block * size + place % size


def after(token, value):
    return value if token is None else lax.optimization_barrier((value, token))[0]


def start_gather(value):
    if not small_grid():
        return lax.all_gather(value, RANK, axis=0, tiled=True), None
    return jnp.concatenate([value, swap(value, "core")], axis=0), swap(value, "tl")


def forward_rows(rows, token):
    far = after(token, rows[1])
    return jnp.concatenate([far, swap(far, "core")], axis=0)


def start_scatter(pieces):
    if not small_grid():
        return (lax.psum_scatter(pieces[0], RANK, scatter_dimension=0, tiled=True),)
    near, far = pieces
    rows = near.shape[0] // 2
    far_peer = swap(far[rows:], "core")
    far_sum = (far[:rows].astype(jnp.float32) + far_peer.astype(jnp.float32)).astype(jnp.bfloat16)
    return near[:rows], swap(near[rows:], "core"), swap(far_sum, "tl")


def finish_scatter_rows(terms, token):
    terms = [*terms[:-1], after(token, terms[-1])]
    return sum(term.astype(jnp.float32) for term in terms)


def sum_over(value, axes):
    for axis in axes:
        if lax.axis_size(axis) == 2:
            value = value + swap(value, axis)
        else:
            value = lax.psum(value, axis)
    return value


def layout(length_row, group_rows):
    positions = jnp.arange(group_rows, dtype=jnp.int32)
    start = jnp.int32(0)
    offset = jnp.zeros((group_rows,), jnp.int32)
    starts = positions
    for index in range(length_row.shape[0]):
        end = start + length_row[index]
        inside = (positions >= start) & (positions < end)
        offset = jnp.where(inside, start, offset)
        starts = jnp.where(inside, start, starts)
        start = end
    return (positions - offset, starts)


def rotary_tables(position):
    half_dim = HDIM // 2
    exponents = jnp.arange(half_dim, dtype=jnp.float32) * (2.0 / HDIM)
    frequency = jnp.power(jnp.float32(rope_base), -exponents)
    angles = position.astype(jnp.float32)[:, None] * frequency[None, :]
    cosine, sine = jnp.cos(angles), jnp.sin(angles)
    return (
        jnp.concatenate([cosine, cosine], axis=1),
        jnp.concatenate([-sine, sine], axis=1),
    )


def columns_of(rows, index):
    chosen = (lax.broadcasted_iota(jnp.int32, (rows.shape[0], HDIM), 0) == index).astype(
        jnp.float32
    )
    return lax.dot_general(
        rows,
        chosen,
        (((0,), (0,)), ((), ())),
        precision=lax.Precision.HIGHEST,
        preferred_element_type=jnp.float32,
    )


def row_sums(values):
    ones = jnp.ones((8, values.shape[1]), jnp.float32)
    return lax.dot_general(
        ones,
        values,
        (((1,), (1,)), ((), ())),
        precision=lax.Precision.HIGHEST,
        preferred_element_type=jnp.float32,
    )[:1]


def rstd_of(squares, index):
    return lax.rsqrt(columns_of(squares, index) * (1.0 / D) + epsilon)


def prepare_kernel(raw, squares, gain_q, gain_k, cosine, sine, q_out, k_out, v_out):
    width = q_out.shape[1]
    table_c, table_s = cosine[...], sine[...]
    both = squares[...]
    for index, (gain, out) in enumerate(((gain_q, q_out), (gain_k, k_out))):
        rstd = rstd_of(both, index)
        for head in range(width // HDIM):
            cols = slice(head * HDIM, (head + 1) * HDIM)
            base = index * width + head * HDIM
            norm = raw[:, base : base + HDIM] * rstd * gain[:, cols]
            turned = norm * table_c + pltpu.roll(norm, HDIM // 2, 1) * table_s
            out[:, cols] = turned.astype(jnp.bfloat16)
    v_out[...] = raw[:, 2 * width :].astype(jnp.bfloat16)


def prepare(raw, squares, gain_q, gain_k, cosine, sine):
    rows, width = raw.shape[0], raw.shape[1] // 3
    whole = pl.BlockSpec((1, width), lambda i: (0, 0))
    table = pl.BlockSpec((BLOCK, HDIM), lambda i: (i, 0))
    out = pl.BlockSpec((BLOCK, width), lambda i: (i, 0))
    return pl.pallas_call(
        prepare_kernel,
        grid=(rows // BLOCK,),
        in_specs=[
            pl.BlockSpec((BLOCK, 3 * width), lambda i: (i, 0)),
            pl.BlockSpec((2, BLOCK), lambda i: (0, i)),
            whole,
            whole,
            table,
            table,
        ],
        out_specs=[out] * 3,
        out_shape=[jax.ShapeDtypeStruct((rows, width), jnp.bfloat16)] * 3,
        cost_estimate=BESIDE,
        name="prepare",
    )(raw, squares, gain_q[None], gain_k[None], cosine, sine)


def allowed_keys(starts, first_key, first_query):
    shape = (BLOCK, BLOCK)
    keys = first_key + lax.broadcasted_iota(jnp.int32, shape, 0)
    queries = first_query + lax.broadcasted_iota(jnp.int32, shape, 1)
    return (keys >= starts) & (keys <= queries)


def head_columns(head):
    return slice(head * HDIM, (head + 1) * HDIM)


def forward_kernel(low_ref, q_ref, k_ref, v_ref, start_ref, attn_ref, full_ref, log_ref):
    block = pl.program_id(0)
    heads = q_ref.shape[1] // HDIM
    starts = start_ref[...]
    scale = 1.0 / math.sqrt(HDIM)

    def step(index, carried):
        rows = pl.ds(pl.multiple_of(index * BLOCK, BLOCK), BLOCK)
        allowed = allowed_keys(starts, index * BLOCK, block * BLOCK)
        after_step = []
        for head, (peak, total, acc) in enumerate(carried):
            cols = head_columns(head)
            scores = contract_cols(k_ref[rows, cols], q_ref[:, cols]) * scale
            scores = jnp.where(allowed, scores, masked_score)
            new_peak = jnp.maximum(peak, jnp.max(scores, axis=0, keepdims=True))
            fade = jnp.exp(peak - new_peak)
            weights = jnp.exp(scores - new_peak)
            total = total * fade + jnp.sum(weights, axis=0, keepdims=True)
            acc = acc * fade + contract_rows(v_ref[rows, cols], weights.astype(jnp.bfloat16))
            after_step.append((new_peak, total, acc))
        return tuple(after_step)

    start = (
        jnp.full((1, BLOCK), masked_score, jnp.float32),
        jnp.zeros((1, BLOCK), jnp.float32),
        jnp.zeros((HDIM, BLOCK), jnp.float32),
    )
    carried = step(block, (start,) * heads)
    carried = lax.fori_loop(low_ref[block], block, step, carried)
    for head, (peak, total, acc) in enumerate(carried):
        out = jnp.transpose(acc / total)
        full_ref[:, head_columns(head)] = out
        attn_ref[:, head_columns(head)] = out.astype(jnp.bfloat16)
        log_ref[head] = peak + jnp.log(total)


def attention_forward(q_b, k_b, v_b, starts, low_block):
    rows, width = q_b.shape
    heads = width // HDIM
    own = pl.BlockSpec((BLOCK, width), lambda i, low: (i, 0))
    whole = pl.BlockSpec((rows, width), lambda i, low: (0, 0))
    return pl.pallas_call(
        forward_kernel,
        grid_spec=pltpu.PrefetchScalarGridSpec(
            num_scalar_prefetch=1,
            grid=(rows // BLOCK,),
            in_specs=[own, whole, whole, pl.BlockSpec((1, BLOCK), lambda i, low: (0, i))],
            out_specs=[own, own, pl.BlockSpec((heads, 1, BLOCK), lambda i, low: (0, 0, i))],
        ),
        out_shape=[
            jax.ShapeDtypeStruct((rows, width), jnp.bfloat16),
            jax.ShapeDtypeStruct((rows, width), jnp.float32),
            jax.ShapeDtypeStruct((heads, 1, rows), jnp.float32),
        ],
        compiler_params=pltpu.CompilerParams(vmem_limit_bytes=VMEM_BYTES),
        cost_estimate=BESIDE,
        name="attention_forward",
    )(low_block, q_b, k_b, v_b, starts)


def backward_kernel(
    high_ref, q_ref, k_ref, v_ref, grad_ref, full_ref, log_ref, start_ref, dq_ref, dk_ref, dv_ref, delta
):
    block = pl.program_id(0)
    blocks = pl.num_programs(0)
    heads = q_ref.shape[1] // HDIM
    scale = 1.0 / math.sqrt(HDIM)

    @pl.when(block == 0)
    def _():
        dq_ref[...] = jnp.zeros_like(dq_ref)

        def one(index, unused):
            rows = pl.ds(pl.multiple_of(index * BLOCK, BLOCK), BLOCK)
            for head in range(heads):
                cols = head_columns(head)
                delta[head, :, rows] = row_sums(
                    grad_ref[rows, cols].astype(jnp.float32) * full_ref[rows, cols]
                )
            return unused

        lax.fori_loop(0, blocks, one, 0)

    here = pl.ds(pl.multiple_of(block * BLOCK, BLOCK), BLOCK)

    def step(index, carried):
        rows = pl.ds(pl.multiple_of(index * BLOCK, BLOCK), BLOCK)
        allowed = allowed_keys(start_ref[:, rows], block * BLOCK, index * BLOCK)
        after_step = []
        for head, (dk, dv) in enumerate(carried):
            cols = head_columns(head)
            keys, values = k_ref[here, cols], v_ref[here, cols]
            queries, grads = q_ref[rows, cols], grad_ref[rows, cols]
            scores = contract_cols(keys, queries) * scale
            probs = jnp.where(allowed, jnp.exp(scores - log_ref[head, :, rows]), 0.0)
            dv = dv + dot(probs.astype(jnp.bfloat16), grads)
            d_probs = contract_cols(values, grads)
            d_scores = (probs * (d_probs - delta[head, :, rows])).astype(jnp.bfloat16)
            dk = dk + dot(d_scores, queries)
            dq_ref[rows, cols] += contract_rows(d_scores, keys)
            after_step.append((dk, dv))
        return tuple(after_step)

    zero = jnp.zeros((BLOCK, HDIM), jnp.float32)
    carried = lax.fori_loop(block, high_ref[block] + 1, step, ((zero, zero),) * heads)
    for head, (dk, dv) in enumerate(carried):
        dk_ref[:, head_columns(head)] = dk * scale
        dv_ref[:, head_columns(head)] = dv

    @pl.when(block == blocks - 1)
    def _():
        dq_ref[...] = dq_ref[...] * scale


def attention_backward(q_b, k_b, v_b, grads, full, logs, starts, high_block):
    rows, width = q_b.shape
    heads = width // HDIM
    own = pl.BlockSpec((BLOCK, width), lambda i, high: (i, 0))
    whole = pl.BlockSpec((rows, width), lambda i, high: (0, 0))
    out = jax.ShapeDtypeStruct((rows, width), jnp.float32)
    return pl.pallas_call(
        backward_kernel,
        grid_spec=pltpu.PrefetchScalarGridSpec(
            num_scalar_prefetch=1,
            grid=(rows // BLOCK,),
            in_specs=[whole] * 5
            + [
                pl.BlockSpec((heads, 1, rows), lambda i, high: (0, 0, 0)),
                pl.BlockSpec((1, rows), lambda i, high: (0, 0)),
            ],
            out_specs=[whole, own, own],
            scratch_shapes=[pltpu.VMEM((heads, 1, rows), jnp.float32)],
        ),
        out_shape=[out] * 3,
        compiler_params=pltpu.CompilerParams(vmem_limit_bytes=VMEM_BYTES),
        cost_estimate=BESIDE,
        name="attention_backward",
    )(high_block, q_b, k_b, v_b, grads, full, logs, starts)


def norm_grads_kernel(
    dq_ref, dk_ref, raw, squares, gain_q, gain_k, cosine, sine, dq_out, dk_out, dots, q_part, k_part
):
    width = dq_ref.shape[1]
    table_c, table_s = cosine[...], sine[...]
    both = squares[...]

    @pl.when(pl.program_id(0) == 0)
    def _():
        q_part[...] = jnp.zeros_like(q_part)
        k_part[...] = jnp.zeros_like(k_part)

    for index, (grad, gain, out, gain_part) in enumerate(
        ((dq_ref, gain_q, dq_out, q_part), (dk_ref, gain_k, dk_out, k_part))
    ):
        rstd = rstd_of(both, index)
        products = jnp.zeros((BLOCK, HDIM), jnp.float32)
        for head in range(width // HDIM):
            cols = slice(head * HDIM, (head + 1) * HDIM)
            base = index * width + head * HDIM
            turned = grad[:, cols]
            norm = turned * table_c - pltpu.roll(turned, HDIM // 2, 1) * table_s
            out[:, cols] = norm
            product = raw[:, base : base + HDIM] * norm
            gain_part[:, cols] += jnp.sum((product * rstd).reshape(BLOCK // 8, 8, HDIM), axis=0)
            products = products + product * gain[:, cols]
        dots[index : index + 1, :] = row_sums(products)


def norm_grads(d_q_rot, d_k_rot, raw, squares, gain_q, gain_k, cosine, sine):
    rows, width = d_q_rot.shape
    whole = pl.BlockSpec((1, width), lambda i: (0, 0))
    table = pl.BlockSpec((BLOCK, HDIM), lambda i: (i, 0))
    own = pl.BlockSpec((BLOCK, width), lambda i: (i, 0))
    pair = pl.BlockSpec((2, BLOCK), lambda i: (0, i))
    total = pl.BlockSpec((8, width), lambda i: (0, 0))
    grad = jax.ShapeDtypeStruct((rows, width), jnp.float32)
    return pl.pallas_call(
        norm_grads_kernel,
        grid=(rows // BLOCK,),
        in_specs=[
            own,
            own,
            pl.BlockSpec((BLOCK, 3 * width), lambda i: (i, 0)),
            pair,
            whole,
            whole,
            table,
            table,
        ],
        out_specs=[own, own, pair, total, total],
        out_shape=[
            grad,
            grad,
            jax.ShapeDtypeStruct((2, rows), jnp.float32),
            jax.ShapeDtypeStruct((8, width), jnp.float32),
            jax.ShapeDtypeStruct((8, width), jnp.float32),
        ],
        cost_estimate=BESIDE,
        name="norm_grads",
    )(d_q_rot, d_k_rot, raw, squares, gain_q[None], gain_k[None], cosine, sine)


def raw_grads_kernel(dq_ref, dk_ref, dv_ref, raw, squares, dots, gain_q, gain_k, out):
    width = dq_ref.shape[1]
    both, sums = squares[...], dots[...]
    for index, (grad, gain) in enumerate(((dq_ref, gain_q), (dk_ref, gain_k))):
        rstd = rstd_of(both, index)
        share = rstd * rstd * rstd * columns_of(sums, index) * (1.0 / D)
        for head in range(width // HDIM):
            cols = slice(head * HDIM, (head + 1) * HDIM)
            base = index * width + head * HDIM
            value = rstd * gain[:, cols] * grad[:, cols] - raw[:, base : base + HDIM] * share
            out[:, base : base + HDIM] = value.astype(jnp.bfloat16)
    out[:, 2 * width :] = dv_ref[...].astype(jnp.bfloat16)


def raw_grads(d_q_norm, d_k_norm, d_v, raw, squares, dots, gain_q, gain_k):
    rows, width = d_q_norm.shape
    whole = pl.BlockSpec((1, width), lambda i: (0, 0))
    own = pl.BlockSpec((BLOCK, width), lambda i: (i, 0))
    wide = pl.BlockSpec((BLOCK, 3 * width), lambda i: (i, 0))
    pair = pl.BlockSpec((2, BLOCK), lambda i: (0, i))
    return pl.pallas_call(
        raw_grads_kernel,
        grid=(rows // BLOCK,),
        in_specs=[own, own, own, wide, pair, pair, whole, whole],
        out_specs=wide,
        out_shape=jax.ShapeDtypeStruct((rows, 3 * width), jnp.bfloat16),
        cost_estimate=BESIDE,
        name="raw_grads",
    )(d_q_norm, d_k_norm, d_v, raw, squares, dots, gain_q[None], gain_k[None])


def dot(left, right):
    return jnp.dot(left, right, preferred_element_type=jnp.float32)


def contract_rows(left, right):
    return lax.dot_general(
        left, right, (((0,), (0,)), ((), ())), preferred_element_type=jnp.float32
    )


def contract_cols(left, right):
    return lax.dot_general(
        left, right, (((1,), (1,)), ((), ())), preferred_element_type=jnp.float32
    )


def column_block(rows, width):
    return min(width, 512 if rows <= 1024 else 256)


def matmul_params():
    return pltpu.CompilerParams(vmem_limit_bytes=56 * 1024 * 1024)


def hidden_kernel(x_ref, gate_w, up_w, gate_out, up_out, hidden_out):
    gate = dot(x_ref[...], gate_w[...])
    up_part = dot(x_ref[...], up_w[...])
    gate_out[...] = gate
    up_out[...] = up_part
    hidden_out[...] = (gate * jax.nn.sigmoid(gate) * up_part).astype(jnp.bfloat16)


def hidden_units(x, gate_full, up_full):
    rows, depth = x.shape
    width = gate_full.shape[1]
    block = column_block(rows, width)
    weight = pl.BlockSpec((depth, block), lambda j: (0, j))
    out = pl.BlockSpec((rows, block), lambda j: (0, j))
    return pl.pallas_call(
        hidden_kernel,
        grid=(width // block,),
        in_specs=[pl.BlockSpec((rows, depth), lambda j: (0, 0)), weight, weight],
        out_specs=[out] * 3,
        out_shape=[
            jax.ShapeDtypeStruct((rows, width), jnp.float32),
            jax.ShapeDtypeStruct((rows, width), jnp.float32),
            jax.ShapeDtypeStruct((rows, width), jnp.bfloat16),
        ],
        compiler_params=matmul_params(),
        cost_estimate=BESIDE,
        name="hidden_units",
    )(x, gate_full, up_full)


def hidden_grads_kernel(grad_ref, weight, gate_ref, up_ref, gate_out, up_out):
    d_hidden = dot(grad_ref[...], weight[...])
    gate = gate_ref[...]
    gate_sigmoid = jax.nn.sigmoid(gate)
    silu = gate * gate_sigmoid
    gate_out[...] = (
        d_hidden * up_ref[...] * (gate_sigmoid * (1.0 + gate * (1.0 - gate_sigmoid)))
    ).astype(jnp.bfloat16)
    up_out[...] = (d_hidden * silu).astype(jnp.bfloat16)


def hidden_grads(grad, down_full, gate, up_part):
    rows, depth = grad.shape
    width = down_full.shape[1]
    block = column_block(rows, width)
    part_spec = pl.BlockSpec((rows, block), lambda j: (0, j))
    out = jax.ShapeDtypeStruct((rows, width), jnp.bfloat16)
    return pl.pallas_call(
        hidden_grads_kernel,
        grid=(width // block,),
        in_specs=[
            pl.BlockSpec((rows, depth), lambda j: (0, 0)),
            pl.BlockSpec((depth, block), lambda j: (0, j)),
            part_spec,
            part_spec,
        ],
        out_specs=[part_spec] * 2,
        out_shape=[out] * 2,
        compiler_params=matmul_params(),
        cost_estimate=BESIDE,
        name="hidden_grads",
    )(grad, down_full, gate, up_part)


def products_kernel(count, *refs):
    total = None
    for left, right in zip(refs[:count], refs[count : 2 * count]):
        term = contract_cols(left[...], right[...])
        total = term if total is None else total + term
    refs[-1][...] = total.astype(jnp.bfloat16)


def sum_products(lefts, rights):
    rows, depth = lefts[0].shape
    width = rights[0].shape[0]
    block = column_block(rows, width)
    return pl.pallas_call(
        functools.partial(products_kernel, len(lefts)),
        grid=(width // block,),
        in_specs=[pl.BlockSpec((rows, depth), lambda j: (0, 0)) for _ in lefts]
        + [pl.BlockSpec((block, depth), lambda j: (j, 0)) for _ in rights],
        out_specs=pl.BlockSpec((rows, block), lambda j: (0, j)),
        out_shape=jax.ShapeDtypeStruct((rows, width), jnp.bfloat16),
        compiler_params=matmul_params(),
        cost_estimate=BESIDE,
        name="sum_products",
    )(*lefts, *rights)


def weight_grad_kernel(count, *refs):
    total = None
    for left, right in zip(refs[:count], refs[count : 2 * count]):
        term = contract_rows(left[...], right[...])
        total = term if total is None else total + term
    refs[-1][...] = total.astype(jnp.bfloat16)


def weight_grad(lefts, rights):
    heights = [left.shape[0] for left in lefts]
    if len(rights) == 1 < len(lefts):
        rights, places = rights * len(lefts), list(range(len(lefts)))
    else:
        places = [0] * len(lefts)
    height, width = lefts[0].shape[1], rights[0].shape[1]
    tall, wide = min(height, 512), min(width, 1024)
    return pl.pallas_call(
        functools.partial(weight_grad_kernel, len(lefts)),
        grid=(width // wide, height // tall),
        in_specs=[pl.BlockSpec((rows, tall), lambda j, i: (0, i)) for rows in heights]
        + [
            pl.BlockSpec((rows, wide), functools.partial(lambda place, j, i: (place, j), place))
            for rows, place in zip(heights, places)
        ],
        out_specs=pl.BlockSpec((tall, wide), lambda j, i: (i, j)),
        out_shape=jax.ShapeDtypeStruct((height, width), jnp.bfloat16),
        compiler_params=matmul_params(),
        cost_estimate=BESIDE,
        name="weight_grad",
    )(*lefts, *rights)


def stacked_weight_grad(left, right, count):
    rows, height = left.shape
    width = right.shape[1] // count
    tall = min(height, 512)
    return pl.pallas_call(
        functools.partial(weight_grad_kernel, 1),
        grid=(count, height // tall),
        in_specs=[
            pl.BlockSpec((rows, tall), lambda j, i: (0, i)),
            pl.BlockSpec((rows, width), lambda j, i: (0, j)),
        ],
        out_specs=pl.BlockSpec((None, tall, width), lambda j, i: (j, i, 0)),
        out_shape=jax.ShapeDtypeStruct((count, height, width), jnp.bfloat16),
        compiler_params=matmul_params(),
        cost_estimate=BESIDE,
        name="stacked_weight_grad",
    )(left, right)


def move_rows(places, wanted_first, count, rows_ref):
    wanted = wanted_first + lax.broadcasted_iota(jnp.int32, (count, places.shape[1]), 0)
    chosen = jnp.where(places == wanted, 1.0, 0.0).astype(jnp.bfloat16)
    return dot(chosen, rows_ref[...]).astype(jnp.bfloat16)


def pick_rows(places, rows_ref):
    columns = lax.broadcasted_iota(jnp.int32, (places.shape[0], rows_ref.shape[0]), 1)
    chosen = jnp.where(places == columns, 1.0, 0.0).astype(jnp.bfloat16)
    return dot(chosen, rows_ref[...]).astype(jnp.bfloat16)


def pack_kernel(places, tokens_ref, weight, packed_out, raw_out, squares_out):
    packed = pick_rows(places[...], tokens_ref)
    packed_out[...] = packed
    raw = dot(packed, weight[...])
    raw_out[...] = raw
    width = raw.shape[1] // 3
    for index in range(2):
        cols = raw[:, index * width : (index + 1) * width]
        squares_out[index : index + 1, :] = row_sums(cols * cols)


def pack(perm_row, tokens_all, qkv_full):
    rows, depth = tokens_all.shape
    width = qkv_full.shape[1]
    return pl.pallas_call(
        pack_kernel,
        grid=(rows // BLOCK,),
        in_specs=[
            pl.BlockSpec((BLOCK, 1), lambda i: (i, 0)),
            pl.BlockSpec((rows, depth), lambda i: (0, 0)),
            pl.BlockSpec((depth, width), lambda i: (0, 0)),
        ],
        out_specs=[
            pl.BlockSpec((BLOCK, depth), lambda i: (i, 0)),
            pl.BlockSpec((BLOCK, width), lambda i: (i, 0)),
            pl.BlockSpec((2, BLOCK), lambda i: (0, i)),
        ],
        out_shape=[
            jax.ShapeDtypeStruct((rows, depth), jnp.bfloat16),
            jax.ShapeDtypeStruct((rows, width), jnp.float32),
            jax.ShapeDtypeStruct((2, rows), jnp.float32),
        ],
        compiler_params=matmul_params(),
        cost_estimate=BESIDE,
        name="pack",
    )(perm_row[:, None], tokens_all, qkv_full)


def given_kernel(count, places, rows_ref, weight, moved_out, product_out):
    moved = move_rows(places[...], pl.program_id(0) * count, count, rows_ref)
    moved_out[...] = moved
    product_out[...] = contract_cols(moved, weight[...]).astype(jnp.bfloat16)


def give_back(place_row, value, weight):
    rows, depth = value.shape
    width = weight.shape[0]
    count = 512
    return pl.pallas_call(
        functools.partial(given_kernel, count),
        grid=(rows // count,),
        in_specs=[
            pl.BlockSpec((1, rows), lambda i: (0, 0)),
            pl.BlockSpec((rows, depth), lambda i: (0, 0)),
            pl.BlockSpec((width, depth), lambda i: (0, 0)),
        ],
        out_specs=[
            pl.BlockSpec((count, depth), lambda i: (i, 0)),
            pl.BlockSpec((count, width), lambda i: (i, 0)),
        ],
        out_shape=[
            jax.ShapeDtypeStruct((rows, depth), jnp.bfloat16),
            jax.ShapeDtypeStruct((rows, width), jnp.bfloat16),
        ],
        compiler_params=matmul_params(),
        cost_estimate=BESIDE,
        name="give_back",
    )(place_row[None], value, weight)


def pick_products_kernel(count, *refs):
    places, pieces, weight = refs[0], refs[1 : 1 + count], refs[1 + count]
    out, products = refs[2 + count], refs[3 + count]
    step, first = BLOCK, 0
    for piece in pieces:
        height = piece.shape[0]

        def one(index, unused, piece=piece, first=first):
            here = pl.ds(pl.multiple_of(index * step, step), step)
            there = pl.ds(pl.multiple_of(first + index * step, step), step)
            products[there, :] = dot(piece[here, :], weight[...]).astype(jnp.bfloat16)
            return unused

        lax.fori_loop(0, height // step, one, 0)
        first += height

    def pick_block(index, unused):
        here = pl.ds(pl.multiple_of(index * step, step), step)
        out[here, :] = pick_rows(places[here, :], products)
        return unused

    lax.fori_loop(0, out.shape[0] // step, pick_block, 0)


def pick_products(place_row, pieces, weight):
    rows, width = place_row.shape[0], weight.shape[1]
    vmem = pl.BlockSpec(memory_space=pltpu.VMEM)
    return pl.pallas_call(
        functools.partial(pick_products_kernel, len(pieces)),
        in_specs=[vmem] * (2 + len(pieces)),
        out_specs=vmem,
        out_shape=jax.ShapeDtypeStruct((rows, width), jnp.bfloat16),
        scratch_shapes=[pltpu.VMEM((rows, width), jnp.bfloat16)],
        compiler_params=matmul_params(),
        cost_estimate=BESIDE,
        name="pick_products",
    )(place_row[:, None], *pieces, weight)


def rms_back(values, rstd, gain_vec, grad):
    scaled = grad * gain_vec
    row_dots = jnp.sum(values * scaled, axis=1, keepdims=True)
    return rstd * scaled - values * (rstd * rstd * rstd) * row_dots / D


def per_device(
    tokens,
    upstream,
    lengths,
    permutation,
    w_query,
    w_key,
    w_value,
    w_out,
    w_gate,
    w_up,
    w_down,
    q_gain,
    k_gain,
    attn_gain,
    ffn_gain,
):
    rank = lax.axis_index("core") * lax.axis_size("tl") + lax.axis_index("tl")
    own_rows = tokens.shape[0]
    group_rows = own_rows * 2 * lax.axis_size("tl")
    local_width = w_query.shape[1]

    own_group = lax.axis_index("core") == lax.axis_index("th")
    layout_row = jnp.concatenate([permutation, lengths], axis=1)
    layout_row = jnp.where(own_group, layout_row, swap(layout_row, "core"))[0]
    perm_row, length_row = layout_row[:group_rows], layout_row[group_rows:]

    tokens_all, qkv_full, out_full, gate_pair = enter(
        tokens,
        [((w_query, w_key, w_value), True), ((w_out.T,), True), ((w_gate,), False)],
    )
    gate_full = gather_weight(gate_pair)
    up_shard, tokens_all = lax.optimization_barrier((w_up, tokens_all))
    up_pair = pair_of_weight(up_shard)
    tokens = lax.dynamic_slice_in_dim(tokens_all, rank * own_rows, own_rows)

    perm_place = row_place(perm_row, own_rows)
    position, starts = layout(length_row, group_rows)
    cosine, sine = rotary_tables(position)
    blocks = group_rows // BLOCK
    low_block = starts[::BLOCK] // BLOCK
    last_keys = (jnp.arange(blocks, dtype=jnp.int32) + 1) * BLOCK - 1
    reached = jnp.sum((starts[None, :] <= last_keys[:, None]).astype(jnp.int32), axis=1)
    high_block = (reached - 1) // BLOCK

    packed, raw, squares = pack(perm_row, tokens_all, qkv_full)
    up_pair, raw = lax.optimization_barrier((up_pair, raw))
    up_full = gather_weight(up_pair)
    squares = sum_over(squares, RANK)
    down_shard, squares = lax.optimization_barrier((w_down.T, squares))
    down_pair = pair_of_weight(down_shard)
    gain_q = lax.dynamic_slice_in_dim(q_gain, rank * local_width, local_width)
    gain_k = lax.dynamic_slice_in_dim(k_gain, rank * local_width, local_width)
    q_b, k_b, v_b = prepare(raw, squares, gain_q, gain_k, cosine, sine)
    attn_b, attn_f, logs = attention_forward(q_b, k_b, v_b, starts[None], low_block)

    parts = PARTS if small_grid() else 1
    part_rows = own_rows // parts

    def part_of(value, index):
        return part(value, 0, index, parts)

    def pieces_of(value, index):
        whole = part_of(value, index)
        return [part(whole, 0, 0, 2), part(whole, 0, 1, 2)] if small_grid() else [whole]

    sides = 2 if small_grid() else 1
    attn_given, attn_parts = give_back(perm_place, attn_b, out_full)
    down_pair, attn_parts = lax.optimization_barrier((down_pair, attn_parts))
    down_full = gather_weight(down_pair)
    order = [(side, index) for side in range(sides) for index in range(parts)]
    token = None

    def pass_through(make_rows, begin, finish, late, between=None):
        nonlocal token
        gathered, far_pieces, begun, sums, scattered = {}, {}, {}, {}, []

        def complete(side, index):
            nonlocal token
            sums[side, index] = finish(*begun[side, index], token)
            if scattered and sides == 2 and not late:
                *others, last = scattered[-1]
                sums[side, index], last = lax.optimization_barrier((sums[side, index], last))
                scattered[-1] = (*others, last)
            token = sums[side, index]

        def scatter(index):
            scattered.append(start_scatter([sums[side, index] for side in range(sides)]))

        for side, index in order:
            if side == 0:
                gathered[index] = start_gather(make_rows(index, token))
                if sides == 2 and index > 0 and not late:
                    far_pieces[index - 1] = forward_rows(gathered[index - 1], token)
                piece = gathered[index][0]
            else:
                if late:
                    far_pieces[index] = forward_rows(gathered[index], token)
                elif index == 0:
                    far_pieces[parts - 1] = forward_rows(gathered[parts - 1], token)
                    if between is not None:
                        near = [gathered[each][0] for each in range(parts)]
                        token = between(near, [far_pieces[each] for each in range(parts)], token)
                piece = far_pieces[index]
            begun[side, index] = begin((index, side), piece, token)
            token = begun[side, index][0]
            if not late:
                complete(side, index)
                if side == sides - 1:
                    scatter(index)
        if late:
            for index in range(parts):
                for side in reversed(range(sides)):
                    complete(side, index)
                scatter(index)
        return scattered

    attn_sums = [start_scatter(pieces_of(attn_parts, index)) for index in range(parts)]
    attn_outs, resids, saved = [], [], {}

    def resid_rows(index, token):
        attn_out = finish_scatter_rows(attn_sums[index], token)
        rstd_a = lax.rsqrt(jnp.mean(attn_out * attn_out, axis=1, keepdims=True) + epsilon)
        attn_outs.append((attn_out, rstd_a))
        resids.append(part_of(tokens, index).astype(jnp.float32) + attn_out * rstd_a * attn_gain)
        return resids[-1].astype(jnp.bfloat16)

    def feed_forward(key, piece, token):
        gate, up_part, hidden_b = hidden_units(after(token, piece), gate_full, up_full)
        saved[key] = (piece, gate, up_part, hidden_b)
        return (hidden_b,)

    def feed_down(hidden_b, token):
        return sum_products([after(token, hidden_b)], [down_full])

    upstream_turn = start_turn(after(attn_parts, upstream))
    mlp_sums = pass_through(resid_rows, feed_forward, feed_down, True)
    token, upstream_turn = lax.optimization_barrier((token, upstream_turn))
    upstream = finish_turn(*upstream_turn)
    layer_outs, gain_parts, grads_f, back = [], [], [], {}

    def d_mlp_rows(index, token):
        mlp_out = finish_scatter_rows(mlp_sums[index], token)
        rstd_m = lax.rsqrt(jnp.mean(mlp_out * mlp_out, axis=1, keepdims=True) + epsilon)
        normed_m = mlp_out * rstd_m
        layer_outs.append((resids[index] + normed_m * ffn_gain).astype(jnp.bfloat16))
        grads_f.append(part_of(upstream, index).astype(jnp.float32))
        gain_parts.append(jnp.sum(grads_f[index] * normed_m, axis=0))
        return rms_back(mlp_out, rstd_m, ffn_gain, grads_f[index]).astype(jnp.bfloat16)

    def feed_back(key, piece, token):
        _, gate, up_part, _ = saved[key]
        d_gate_b, d_up_b = hidden_grads(after(token, piece), down_full, gate, up_part)
        back[key] = (piece, d_gate_b, d_up_b)
        return d_gate_b, d_up_b

    def feed_up(d_gate_b, d_up_b, token):
        return sum_products([after(token, d_gate_b), d_up_b], [gate_full, up_full])

    weight_grads = []

    def first_weight_grad(near, far, token):
        grads = [piece for index in range(parts) for piece in (near[index], far[index])]
        weight_grads.append(weight_grad(after(token, grads), [saved[key][3] for key in sorted(saved)]))
        return weight_grads[0]

    resid_sums = pass_through(d_mlp_rows, feed_back, feed_up, False, first_weight_grad)
    layer_out = jnp.concatenate(layer_outs, axis=0)
    keys = sorted(saved)
    ffn_gain_part = sum(gain_parts)
    attn_gain_part = 0.0
    d_resids, gathered, near_pieces = [], [], []
    operands = [
        ([back[key][0] for key in keys], [saved[key][3] for key in keys]),
        ([saved[key][0] for key in keys], [back[key][1] for key in keys]),
        ([saved[key][0] for key in keys], [back[key][2] for key in keys]),
    ]

    def next_weight_grad(token):
        left, right = operands[len(weight_grads)]
        left, right = after(token, (left, right))
        weight_grads.append(weight_grad(left, right))
        return weight_grads[-1]

    for index in range(parts):
        terms = resid_sums[index]
        if index == 0:
            d_sums = finish_scatter_rows(terms, token)
        else:
            last, weight_grads[-1] = lax.optimization_barrier((terms[-1], weight_grads[-1]))
            d_sums = finish_scatter_rows([*terms[:-1], last], None)
        attn_out, rstd_a = attn_outs[index]
        d_resid = grads_f[index] + d_sums
        d_resids.append(d_resid)
        attn_gain_part = attn_gain_part + jnp.sum(d_resid * attn_out * rstd_a, axis=0)
        d_attn_b = rms_back(attn_out, rstd_a, attn_gain, d_resid).astype(jnp.bfloat16)
        if sides == 2:
            near_pieces.append([d_attn_b, swap(d_attn_b, "core")])
            gathered.append((None, swap(d_attn_b, "tl")))
        else:
            gathered.append(start_gather(d_attn_b))
        token = next_weight_grad((d_attn_b, token))
    far_pieces = []
    for index in range(parts):
        if sides == 2:
            far, weight_grads[-1] = lax.optimization_barrier((gathered[index][1], weight_grads[-1]))
            far_pieces.append([far, swap(far, "core")])
            token = far
        if len(weight_grads) < 3:
            token = next_weight_grad(token)
    while len(weight_grads) < 3:
        token = next_weight_grad(token)
    down_grad, gate_grad, up_grad = weight_grads
    d_attn_pieces = []
    for index in range(parts):
        if sides == 2:
            d_attn_pieces += [*near_pieces[index], *far_pieces[index]]
        else:
            d_attn_pieces.append(gathered[index][0])
    d_resid = jnp.concatenate(d_resids, axis=0)
    out_total = weight_grad(d_attn_pieces, [attn_given])
    d_packed = pick_products(perm_place, d_attn_pieces, out_full)
    down_split = start_split(scatter_pair(down_grad))
    gate_sum, up_sum = scatter_pair(gate_grad), scatter_pair(up_grad)
    layer_turn = start_turn(layer_out)
    d_packed, out_total = lax.optimization_barrier((d_packed, out_total))
    d_q_rot, d_k_rot, d_v = attention_backward(
        q_b, k_b, v_b, d_packed, attn_f, logs, starts[None], high_block
    )
    d_q_rot, down_split, layer_turn = lax.optimization_barrier((d_q_rot, down_split, layer_turn))
    gate_split = start_split(after(d_q_rot, gate_sum))
    d_q_norm, d_k_norm, dots, q_parts, k_parts = norm_grads(
        d_q_rot, d_k_rot, raw, squares, gain_q, gain_k, cosine, sine
    )
    q_gain_part, k_gain_part = jnp.sum(q_parts, axis=0), jnp.sum(k_parts, axis=0)
    dots = sum_over(dots, RANK)
    d_qkv_b = raw_grads(d_q_norm, d_k_norm, d_v, raw, squares, dots, gain_q, gain_k)
    qkv_totals = stacked_weight_grad(packed, d_qkv_b, 3)
    up_split = start_split(after(d_qkv_b, up_sum))
    _, input_parts = give_back(perm_place, d_qkv_b, qkv_full)
    input_parts, gate_split, up_split = lax.optimization_barrier((input_parts, gate_split, up_split))
    layer_out = finish_turn(*layer_turn)
    down_shard = finish_split(*down_split).T
    gate_shard, up_shard = finish_split(*gate_split), finish_split(*up_split)

    def placed(part_sum):
        return lax.dynamic_update_slice_in_dim(
            jnp.zeros((D,), jnp.float32), part_sum, rank * local_width, 0
        )

    gains = jnp.stack(
        [placed(q_gain_part), placed(k_gain_part), attn_gain_part, ffn_gain_part]
        + [jnp.zeros((D,), jnp.float32)] * 4
    )
    tokens_grad, gain_grads, out_shard, query_shard, key_shard, value_shard = leave(
        input_parts,
        d_resid,
        gains,
        [
            (out_total, [local_width], False),
            (qkv_totals, [local_width], False),
        ],
    )

    return (
        layer_out,
        tokens_grad,
        query_shard,
        key_shard,
        value_shard,
        out_shard.T,
        gate_shard,
        up_shard,
        down_shard,
        gain_grads[0],
        gain_grads[1],
        gain_grads[2],
        gain_grads[3],
    )


def solution(mesh):
    dp, tensor = mesh.shape["dp"], mesh.shape["tensor"]
    fine = Mesh(mesh.devices.reshape(dp // 4, 2, 2, 2, tensor // 2), DP + TENSOR)
    rows, weight, weight_out = P(DP + TENSOR, None), P(DP, TENSOR), P(TENSOR, DP)
    return jax.shard_map(
        per_device,
        mesh=fine,
        in_specs=(rows, rows, P(DP, None), P(DP, None))
        + (weight,) * 3
        + (weight_out, weight, weight, weight_out)
        + (P(),) * 4,
        out_specs=(rows, rows)
        + (weight,) * 3
        + (weight_out, weight, weight, weight_out)
        + (P(),) * 4,
        check_vma=False,
    )
```

```python
import functools
import math

import jax
import jax.numpy as jnp
from jax import lax
from jax.experimental import pallas as pl
from jax.experimental.pallas import tpu as pltpu
from jax.sharding import Mesh, PartitionSpec as P

D = 2048
HDIM = 128

epsilon = 1e-06
rope_base = 500000.0
masked_score = -1e30
BLOCK = 256
VMEM_BYTES = 48 * 1024 * 1024
MESH = pl.DeviceIdType.MESH
BESIDE = pl.CostEstimate(flops=1, bytes_accessed=1, transcendentals=0)
PARTS = 2

SWAP = [(0, 1), (1, 0)]
TURN = [(1, 2), (2, 1)]
CYCLE = [(0, 1), (1, 3), (3, 2), (2, 0)]
CYCLE_BACK = [(d, s) for s, d in CYCLE]
DP = ("a", "b", "core")
TENSOR = ("th", "tl")
RANK = ("core", "tl")


def swap(value, axis):
    return lax.ppermute(value, axis, SWAP)


def start_turn(value):
    return value, lax.ppermute(value, ("core", "th"), TURN)


def finish_turn(kept, arrived):
    stays = lax.axis_index("core") == lax.axis_index("th")
    return jnp.where(stays, kept, arrived)


def turn(value):
    return finish_turn(*start_turn(value))


def small_grid():
    return lax.axis_size("a") == 2 and lax.axis_size("tl") == 2


def part(value, dim, index, count):
    size = value.shape[dim] // count
    return lax.slice_in_dim(value, index * size, (index + 1) * size, axis=dim)


def in_turn(left, right):
    upper = lax.axis_index("th") == 0
    return jnp.where(upper, left, right), jnp.where(upper, right, left)


def pair_of_weight(shard):
    second = lax.ppermute(shard, ("core", "th"), CYCLE)
    return jnp.concatenate(in_turn(turn(shard), second), axis=0)


def gather_weight(pair):
    return lax.all_gather(pair, ("a", "b"), axis=0, tiled=True)


def scatter_pair(total):
    return lax.psum_scatter(
        total.astype(jnp.bfloat16), ("a", "b"), scatter_dimension=0, tiled=True
    )


def start_split(pair):
    first, second = in_turn(part(pair, 0, 0, 2), part(pair, 0, 1, 2))
    return first, start_turn(first)[1], lax.ppermute(second, ("core", "th"), CYCLE_BACK)


def finish_split(first, arrived, other):
    return finish_turn(first, arrived).astype(jnp.float32) + other.astype(jnp.float32)


def greet():
    a, b, core = lax.axis_index("a"), lax.axis_index("b"), lax.axis_index("core")
    th, tl = lax.axis_index("th"), lax.axis_index("tl")
    barrier = pltpu.get_barrier_semaphore()
    others = (
        {"a": 1 - a},
        {"b": 1 - b},
        {"core": 1 - core},
        {"tl": 1 - tl},
        {"th": 1 - th},
        {"core": 1 - core, "th": 1 - th},
    )
    for other in others:
        pl.semaphore_signal(barrier, inc=1, device_id=other, device_id_type=MESH)
    pl.semaphore_wait(barrier, len(others))


CHUNKS = 4


def entry_slots(plan):
    return 4 * CHUNKS + sum(3 * len(units) + 6 for units, _ in plan)


def entry_kernel(plan, *refs):
    shard_count = sum(len(units) for units, _ in plan)
    tokens, shards = refs[0], refs[1 : 1 + shard_count]
    tokens_all, fulls = refs[1 + shard_count], refs[2 + shard_count : -3]
    send, recv, local = refs[-3:]
    a, b, core = lax.axis_index("a"), lax.axis_index("b"), lax.axis_index("core")
    th, tl = lax.axis_index("th"), lax.axis_index("tl")
    stays = core == th
    greet()
    used = [0]

    def slots(count):
        used[0] += count
        return used[0] - count

    def remote(source, target, slot, to):
        return pltpu.make_async_remote_copy(
            src_ref=source,
            dst_ref=target,
            send_sem=send.at[slot],
            recv_sem=recv.at[slot],
            device_id=to,
            device_id_type=MESH,
        )

    def arrived(target, slot):
        remote(target, target, slot, {"core": 1 - core}).wait_recv()

    stages, taken = [], 0
    for full, (units, rings) in zip(fulls, plan):
        stage = []
        for column in units:
            shard = shards[taken]
            base = slots(3)
            height, width = shard.shape

            def place(sub, full=full, column=column, height=height, width=width, rings=rings):
                block = 4 * a + 2 * b if rings else 0
                row = pl.multiple_of((block + sub) * height, height)
                return full.at[pl.ds(row, height), pl.ds(column, width)]

            stage.append((shard, place, base, taken))
            taken += 1
        stages.append(stage)

    def near_copy(shard, place, base):
        return remote(shard, place(core), base + 2, {"core": 1 - core})

    def far_copy(shard, place, base):
        return remote(shard, place(core), base + core, {"core": th, "th": 1 - th})

    def start_stage(stage):
        for shard, place, base, index in stage:
            far_copy(shard, place, base).start()

            @pl.when(stays)
            def _():
                pltpu.make_async_copy(shard, place(core), local.at[index]).start()

            @pl.when(jnp.logical_not(stays))
            def _():
                near_copy(shard, place, base).start()

    def finish_stage(stage):
        for shard, place, base, index in stage:

            @pl.when(stays)
            def _():
                pltpu.make_async_copy(shard, place(core), local.at[index]).wait()
                arrived(place(1 - core), base + 2)

            @pl.when(jnp.logical_not(stays))
            def _():
                arrived(place(0), base)
                arrived(place(1), base + 1)

    def piece(full, block_a, block_b, sub):
        height = full.shape[0] // 8
        row = pl.multiple_of((4 * block_a + 2 * block_b + sub) * height, height)
        return full.at[pl.ds(row, height), :]

    def ring(full, base):
        to_a, to_b = {"a": 1 - a}, {"b": 1 - b}
        return (
            [remote(piece(full, a, b, sub), piece(full, a, b, sub), base + sub, to_b) for sub in (0, 1)],
            [remote(piece(full, a, b, sub), piece(full, a, b, sub), base + 2 + sub, to_a) for sub in (0, 1)],
            remote(piece(full, a, 1 - b, 0), piece(full, a, 1 - b, 0), base + 4, to_a),
            remote(piece(full, 1 - a, b, 1), piece(full, 1 - a, b, 1), base + 5, to_b),
        )

    ring_base = [slots(6) for _ in fulls]

    def start_ring(index):
        over_b, over_a, _, _ = ring(fulls[index], ring_base[index])
        for copy in (over_b[0], over_a[1], over_b[1], over_a[0]):
            copy.start()

    def forward_ring(index):
        full, base = fulls[index], ring_base[index]
        arrived(piece(full, a, 1 - b, 0), base)
        ring(full, base)[2].start()
        arrived(piece(full, 1 - a, b, 1), base + 3)
        ring(full, base)[3].start()

    def finish_ring(index):
        full, base = fulls[index], ring_base[index]
        arrived(piece(full, a, 1 - b, 1), base + 1)
        arrived(piece(full, 1 - a, b, 0), base + 2)
        arrived(piece(full, 1 - a, 1 - b, 0), base + 4)
        arrived(piece(full, 1 - a, 1 - b, 1), base + 5)
        over_b, over_a, first, second = ring(full, base)
        for copy in (*over_b, *over_a, first, second):
            copy.wait_send()

    rows = tokens.shape[0]
    step = rows // CHUNKS
    row_base = slots(4 * CHUNKS)

    def rows_of(block_core, block_tl, chunk):
        row = pl.multiple_of((2 * block_core + block_tl) * rows + chunk * step, step)
        return tokens_all.at[pl.ds(row, step), :]

    def row_copies(chunk):
        slot = row_base + 4 * chunk
        own, other = rows_of(core, tl, chunk), rows_of(core, 1 - tl, chunk)
        return (
            remote(
                tokens.at[pl.ds(chunk * step, step), :],
                rows_of(th, tl, chunk),
                slot,
                {"core": th, "th": core},
            ),
            remote(own, own, slot + 1, {"tl": 1 - tl}),
            remote(own, own, slot + 2, {"core": 1 - core}),
            remote(other, other, slot + 3, {"core": 1 - core}),
        )

    def own_rows(chunk):
        return pltpu.make_async_copy(
            tokens.at[pl.ds(chunk * step, step), :],
            rows_of(core, tl, chunk),
            local.at[shard_count + chunk],
        )

    for chunk in range(CHUNKS):

        @pl.when(stays)
        def _():
            own_rows(chunk).start()

    ringed = [index for index, (_, rings) in enumerate(plan) if rings]
    for index in ringed:
        start_stage(stages[index])
    for chunk in range(CHUNKS):

        @pl.when(jnp.logical_not(stays))
        def _():
            row_copies(chunk)[0].start()

        @pl.when(stays)
        def _():
            own_rows(chunk).wait()
            row_copies(chunk)[1].start()
            row_copies(chunk)[2].start()

    for index in ringed:
        finish_stage(stages[index])
        start_ring(index)
    for index in range(len(plan)):
        if index not in ringed:
            start_stage(stages[index])
    for chunk in range(CHUNKS):

        @pl.when(jnp.logical_not(stays))
        def _():
            arrived(rows_of(core, tl, chunk), row_base + 4 * chunk)
            row_copies(chunk)[1].start()
            row_copies(chunk)[2].start()

    for index in ringed:
        forward_ring(index)
    for chunk in range(CHUNKS):
        arrived(rows_of(core, 1 - tl, chunk), row_base + 4 * chunk + 1)
        row_copies(chunk)[3].start()
    for index in ringed:
        finish_ring(index)
    for index in range(len(plan)):
        if index not in ringed:
            finish_stage(stages[index])
    for chunk in range(CHUNKS):
        arrived(rows_of(1 - core, tl, chunk), row_base + 4 * chunk + 2)
        arrived(rows_of(1 - core, 1 - tl, chunk), row_base + 4 * chunk + 3)

        @pl.when(jnp.logical_not(stays))
        def _():
            row_copies(chunk)[0].wait_send()

        for copy in row_copies(chunk)[1:]:
            copy.wait_send()
    for stage in stages:
        for shard, place, base, _ in stage:
            far_copy(shard, place, base).wait_send()

            @pl.when(jnp.logical_not(stays))
            def _():
                near_copy(shard, place, base).wait_send()


def leave_kernel(cuts, paired, stacks, *refs):
    count = len(cuts)
    ringed = [index for index in range(count) if not paired[index]]
    partial, resid, gains, given = refs[0], refs[1], refs[2], refs[3 : 3 + len(stacks)]
    totals = []
    for ref, stack in zip(given, stacks):
        totals += [ref] if stack == 1 else [ref.at[k] for k in range(stack)]
    taken = 3 + len(stacks)
    outs = refs[taken : taken + 2 + sum(len(cut) for cut in cuts)]
    rows_out, gains_out, shard_outs = outs[0], outs[1], outs[2:]
    scratch = refs[taken + len(outs) :]
    peer_far, peer_near, far_sum, from_far, done_rows = scratch[:5]
    boxes, taken = [], 5
    for alone in paired:
        boxes.append(scratch[taken : taken + (1 if alone else 8)])
        taken += 1 if alone else 8
    gain_box, send, recv, local = scratch[-4:]
    a, b, core = lax.axis_index("a"), lax.axis_index("b"), lax.axis_index("core")
    th, tl = lax.axis_index("th"), lax.axis_index("tl")
    stays = core == th
    to_a, to_b, to_core, to_tl = {"a": 1 - a}, {"b": 1 - b}, {"core": 1 - core}, {"tl": 1 - tl}
    greet()

    def remote(source, target, slot, to, send_slot=None):
        return pltpu.make_async_remote_copy(
            src_ref=source,
            dst_ref=target,
            send_sem=send.at[slot if send_slot is None else send_slot],
            recv_sem=recv.at[slot],
            device_id=to,
            device_id_type=MESH,
        )

    def arrived(target, slot):
        remote(target, target, slot, to_core).wait_recv()

    def add(target, target_row, height, *sources):
        step = 16

        def one(index, unused):
            value = None
            for source, first in sources:
                here = pl.ds(pl.multiple_of(first + index * step, step), step)
                term = source[here, :].astype(jnp.float32)
                value = term if value is None else value + term
            there = pl.ds(pl.multiple_of(target_row + index * step, step), step)
            target[there, :] = value.astype(target.dtype)
            return unused

        lax.fori_loop(0, height // step, one, 0)

    rows = resid.shape[0]
    step = rows // CHUNKS

    own, peer, far, peer_of_far = range(4)

    size = rows // PARTS

    def row_of(block, chunk):
        place = chunk * step
        return (place // size) * 4 * size + block * size + place % size

    def at(ref, row):
        return ref.at[pl.ds(row, step), :]

    def row_copies(chunk):
        here = chunk * step
        return (
            remote(at(partial, row_of(peer_of_far, chunk)), at(peer_far, here), 4 * chunk, to_core),
            remote(at(partial, row_of(peer, chunk)), at(peer_near, here), 4 * chunk + 1, to_core),
            remote(at(far_sum, here), at(from_far, here), 4 * chunk + 2, to_tl),
            remote(at(done_rows, here), at(rows_out, here), 4 * chunk + 3, {"core": th, "th": core}),
        )

    def kept_rows(chunk):
        here = chunk * step
        return pltpu.make_async_copy(at(done_rows, here), at(rows_out, here), local.at[chunk])

    base = 4 * CHUNKS

    def piece(ref, block_a, block_b, sub):
        height = ref.shape[0] // 8
        return pl.multiple_of((4 * block_a + 2 * block_b + sub) * height, height), height

    def slice_of(ref, block_a, block_b, sub):
        row, height = piece(ref, block_a, block_b, sub)
        return ref.at[pl.ds(row, height), :]

    def copies(index):
        total = totals[index]
        _, over_a, over_b, send_b, send_a, from_b, from_a, _ = boxes[index]
        slot = base + 10 * index
        height = total.shape[0] // 8

        def half(ref, sub):
            return ref.at[pl.ds(sub * height, height), :]

        return (
            remote(slice_of(total, 1 - a, 1 - b, 0), over_a, slot, to_a),
            remote(slice_of(total, 1 - a, 1 - b, 1), over_b, slot + 1, to_b),
            remote(slice_of(total, a, 1 - b, 1), half(from_b, 1), slot + 2, to_b),
            remote(slice_of(total, 1 - a, b, 0), half(from_a, 0), slot + 3, to_a),
            remote(send_b, half(from_b, 0), slot + 4, to_b),
            remote(send_a, half(from_a, 1), slot + 5, to_a),
        )

    def own_sum(index, sub):
        sums = totals[index] if paired[index] else boxes[index][7]
        height = sums.shape[0] // 2
        return sums.at[pl.ds(pl.multiple_of(sub * height, height), height), :]

    def last_copies(index):
        inbox = boxes[index][0]
        slot = base + 10 * index + 6
        return (
            remote(own_sum(index, 1 - core), inbox.at[0], slot, to_core),
            remote(own_sum(index, 0), inbox.at[1], slot + 1, {"core": 0, "th": core}),
            remote(own_sum(index, 1), inbox.at[1], slot + 1, {"core": 1, "th": core}, slot + 2),
        )

    def start_last(index):
        @pl.when(stays)
        def _():
            last_copies(index)[0].start()

        @pl.when(jnp.logical_not(stays))
        def _():
            last_copies(index)[1].start()
            last_copies(index)[2].start()

    gain_axes = ({"core": 1 - core}, {"tl": 1 - tl}, {"b": 1 - b}, {"a": 1 - a}, {"th": 1 - th})

    def gain_copy(turn_index):
        source = gains if turn_index == 0 else gain_box.at[4 + turn_index]
        return remote(
            source,
            gain_box.at[turn_index],
            base + 10 * count + turn_index,
            gain_axes[turn_index],
        )

    def gain_step(turn_index):
        arrived(gain_box.at[turn_index], base + 10 * count + turn_index)
        mine = gains[...] if turn_index == 0 else gain_box[4 + turn_index]
        total = mine + gain_box[turn_index]
        if turn_index == 4:
            gains_out[...] = total
        else:
            gain_box[5 + turn_index] = total
            gain_copy(turn_index + 1).start()

    def start_ring(index):
        for copy in copies(index)[:4]:
            copy.start()

    def turn_ring(index):
        total = totals[index]
        _, over_a, over_b, send_b, send_a, _, _, _ = boxes[index]
        height = total.shape[0] // 8
        arrived(over_a, base + 10 * index)
        add(send_b, 0, height, (total, piece(total, a, 1 - b, 0)[0]), (over_a, 0))
        copies(index)[4].start()
        arrived(over_b, base + 10 * index + 1)
        add(send_a, 0, height, (total, piece(total, 1 - a, b, 1)[0]), (over_b, 0))
        copies(index)[5].start()

    def finish_ring(index):
        total = totals[index]
        _, _, _, _, _, from_b, from_a, sums = boxes[index]
        height = total.shape[0] // 8
        slot = base + 10 * index
        for sub in (0, 1):
            arrived(from_b.at[pl.ds(sub * height, height), :], slot + (4 if sub == 0 else 2))
            arrived(from_a.at[pl.ds(sub * height, height), :], slot + (3 if sub == 0 else 5))
            add(
                sums,
                sub * height,
                height,
                (total, piece(total, a, b, sub)[0]),
                (from_b, sub * height),
                (from_a, sub * height),
            )
        start_last(index)

    def finish_chunk(chunk):
        here = chunk * step
        arrived(at(peer_near, here), 4 * chunk + 1)
        arrived(at(from_far, here), 4 * chunk + 2)
        add(
            done_rows,
            here,
            step,
            (partial, row_of(own, chunk)),
            (peer_near, here),
            (from_far, here),
            (resid, here),
        )

        @pl.when(stays)
        def _():
            kept_rows(chunk).start()

        @pl.when(jnp.logical_not(stays))
        def _():
            row_copies(chunk)[3].start()

    for chunk in range(CHUNKS):
        row_copies(chunk)[0].start()
    for chunk in range(CHUNKS):
        row_copies(chunk)[1].start()
    for index in range(count):
        if paired[index]:
            start_last(index)
    for chunk in range(CHUNKS):
        arrived(at(peer_far, chunk * step), 4 * chunk)
        add(
            far_sum,
            chunk * step,
            step,
            (partial, row_of(far, chunk)),
            (peer_far, chunk * step),
        )
        row_copies(chunk)[2].start()
    for index in ringed:
        start_ring(index)
    gain_copy(0).start()
    gain_step(0)
    for place in range(max(len(ringed), CHUNKS)):
        if place < len(ringed):
            turn_ring(ringed[place])
        if place < CHUNKS:
            finish_chunk(place)
    for step_index in (1, 2, 3):
        gain_step(step_index)
    for index in ringed:
        finish_ring(index)
    gain_step(4)
    for index, cut in sorted(enumerate(cuts), key=lambda pair: not paired[pair[0]]):
        inbox = boxes[index][0]
        sums = totals[index] if paired[index] else boxes[index][-1]
        height = inbox.shape[1]
        slot = base + 10 * index + 6
        taken = sum(len(other) for other in cuts[:index])
        arrived(inbox.at[1], slot + 1)

        @pl.when(jnp.logical_not(stays))
        def _():
            arrived(inbox.at[0], slot)

        def one(step_index, unused, cut=cut, taken=taken, sums=sums, inbox=inbox, height=height):
            row = pl.multiple_of(step_index * 16, 16)
            here = pl.ds(row, 16)
            other = inbox[1, here, :].astype(jnp.float32)

            def store(value):
                first = 0
                for offset, end in enumerate(cut):
                    shard_outs[taken + offset][here, :] = (value + other)[:, first:end]
                    first = end

            @pl.when(stays)
            def _():
                own_row = pl.multiple_of(core * height + row, 16)
                store(sums[pl.ds(own_row, 16), :].astype(jnp.float32))

            @pl.when(jnp.logical_not(stays))
            def _():
                store(inbox[0, here, :].astype(jnp.float32))

            return unused

        lax.fori_loop(0, height // 16, one, 0)
    for chunk in range(CHUNKS):
        for copy in row_copies(chunk)[:3]:
            copy.wait_send()

        @pl.when(stays)
        def _():
            kept_rows(chunk).wait()

        @pl.when(jnp.logical_not(stays))
        def _():
            row_copies(chunk)[3].wait_send()
            arrived(at(rows_out, chunk * step), 4 * chunk + 3)

    for turn_index in range(5):
        gain_copy(turn_index).wait_send()
    for index in ringed:
        for copy in copies(index):
            copy.wait_send()
    for index in range(count):

        @pl.when(stays)
        def _():
            last_copies(index)[0].wait_send()

        @pl.when(jnp.logical_not(stays))
        def _():
            last_copies(index)[1].wait_send()
            last_copies(index)[2].wait_send()


def unstacked(totals):
    flat = []
    for total, parts, alone in totals:
        for matrix in [total] if total.ndim == 2 else [total[k] for k in range(total.shape[0])]:
            flat.append((matrix, parts, alone))
    return flat


def leave(partial, resid, gains, totals):
    if not small_grid():
        summed = finish_scatter_rows(start_scatter([partial.astype(jnp.bfloat16)]), None)
        shards = []
        for total, parts, alone in unstacked(totals):
            shard, first = finish_split(*start_split(total if alone else scatter_pair(total))), 0
            for width in parts:
                shards.append(shard[:, first : first + width])
                first += width
        total_gains = sum_over(gains, DP + TENSOR)
        return [turn((resid + summed).astype(jnp.bfloat16)), total_gains] + shards
    rows, columns = resid.shape
    cuts, scratch = [], []
    outs = [
        jax.ShapeDtypeStruct((rows, columns), jnp.bfloat16),
        jax.ShapeDtypeStruct(gains.shape, jnp.float32),
    ]
    stacks = tuple(1 if total.ndim == 2 else total.shape[0] for total, _, _ in totals)
    arrays = [total.astype(jnp.bfloat16) for total, _, _ in totals]
    for total, parts, alone in unstacked(totals):
        height, width = total.shape[0] // (2 if alone else 8), total.shape[1]
        cuts.append(tuple(sum(parts[: index + 1]) for index in range(len(parts))))
        outs += [jax.ShapeDtypeStruct((height, part_width), jnp.float32) for part_width in parts]
        shapes = [(2, height, width)]
        if not alone:
            shapes += [(height, width)] * 4 + [(2 * height, width)] * 3
        scratch += [pltpu.VMEM(shape, jnp.bfloat16) for shape in shapes]
    paired = tuple(alone for _, _, alone in unstacked(totals))
    slots = 4 * CHUNKS + 10 * len(paired) + 5
    vmem = pl.BlockSpec(memory_space=pltpu.VMEM)
    return pl.pallas_call(
        functools.partial(leave_kernel, tuple(cuts), paired, stacks),
        in_specs=[vmem] * (3 + len(totals)),
        out_specs=[pl.BlockSpec(memory_space=pl.ANY)] + [vmem] * (len(outs) - 1),
        out_shape=outs,
        scratch_shapes=[pltpu.VMEM((rows, columns), jnp.bfloat16)] * 5
        + scratch
        + [
            pltpu.VMEM((9, *gains.shape), jnp.float32),
            pltpu.SemaphoreType.DMA((slots,)),
            pltpu.SemaphoreType.DMA((slots,)),
            pltpu.SemaphoreType.DMA((CHUNKS,)),
        ],
        compiler_params=pltpu.CompilerParams(
            collective_id=1, has_side_effects=True, vmem_limit_bytes=60 * 1024 * 1024
        ),
        cost_estimate=BESIDE,
        name="leave",
    )(partial.astype(jnp.bfloat16), resid, gains, *arrays)


def enter(tokens, matrices):
    if not small_grid():
        own = turn(tokens)
        pairs = [
            (pair_of_weight(jnp.concatenate(shards, axis=1)), whole) for shards, whole in matrices
        ]
        return [lax.all_gather(own, RANK, axis=0, tiled=True)] + [
            gather_weight(pair) if whole else pair for pair, whole in pairs
        ]
    plan, outs = [], [jax.ShapeDtypeStruct((4 * tokens.shape[0], tokens.shape[1]), tokens.dtype)]
    for shards, whole in matrices:
        columns = [0]
        for shard in shards:
            columns.append(columns[-1] + shard.shape[1])
        plan.append((tuple(columns[:-1]), whole))
        height = (8 if whole else 2) * shards[0].shape[0]
        outs.append(jax.ShapeDtypeStruct((height, columns[-1]), tokens.dtype))
    flat = [shard for shards, _ in matrices for shard in shards]
    slots = entry_slots(plan)
    anywhere = pl.BlockSpec(memory_space=pl.ANY)
    return pl.pallas_call(
        functools.partial(entry_kernel, tuple(plan)),
        in_specs=[anywhere] * (1 + len(flat)),
        out_specs=[anywhere] * len(outs),
        out_shape=outs,
        scratch_shapes=[
            pltpu.SemaphoreType.DMA((slots,)),
            pltpu.SemaphoreType.DMA((slots,)),
            pltpu.SemaphoreType.DMA((len(flat) + CHUNKS,)),
        ],
        compiler_params=pltpu.CompilerParams(collective_id=0, has_side_effects=True),
        cost_estimate=BESIDE,
        name="enter",
    )(tokens, *flat)


def row_place(row, own_rows):
    if not small_grid():
        return row
    mask = 2 * lax.axis_index("core") + lax.axis_index("tl")
    block = (row // own_rows) ^ mask
    block = (block // 2) + 2 * (block % 2)
    size = own_rows // PARTS
    place = row % own_rows
    return (place // size) * 4 * size + block * size + place % size


def after(token, value):
    return value if token is None else lax.optimization_barrier((value, token))[0]


def start_gather(value):
    if not small_grid():
        return lax.all_gather(value, RANK, axis=0, tiled=True), None
    return jnp.concatenate([value, swap(value, "core")], axis=0), swap(value, "tl")


def forward_rows(rows, token):
    far = after(token, rows[1])
    return jnp.concatenate([far, swap(far, "core")], axis=0)


def start_scatter(pieces):
    if not small_grid():
        return (lax.psum_scatter(pieces[0], RANK, scatter_dimension=0, tiled=True),)
    near, far = pieces
    rows = near.shape[0] // 2
    far_peer = swap(far[rows:], "core")
    far_sum = (far[:rows].astype(jnp.float32) + far_peer.astype(jnp.float32)).astype(jnp.bfloat16)
    return near[:rows], swap(near[rows:], "core"), swap(far_sum, "tl")


def finish_scatter_rows(terms, token):
    terms = [*terms[:-1], after(token, terms[-1])]
    return sum(term.astype(jnp.float32) for term in terms)


def sum_over(value, axes):
    for axis in axes:
        if lax.axis_size(axis) == 2:
            value = value + swap(value, axis)
        else:
            value = lax.psum(value, axis)
    return value


def layout(length_row, group_rows):
    positions = jnp.arange(group_rows, dtype=jnp.int32)
    start = jnp.int32(0)
    offset = jnp.zeros((group_rows,), jnp.int32)
    starts = positions
    for index in range(length_row.shape[0]):
        end = start + length_row[index]
        inside = (positions >= start) & (positions < end)
        offset = jnp.where(inside, start, offset)
        starts = jnp.where(inside, start, starts)
        start = end
    return (positions - offset, starts)


def rotary_tables(position):
    half_dim = HDIM // 2
    exponents = jnp.arange(half_dim, dtype=jnp.float32) * (2.0 / HDIM)
    frequency = jnp.power(jnp.float32(rope_base), -exponents)
    angles = position.astype(jnp.float32)[:, None] * frequency[None, :]
    cosine, sine = jnp.cos(angles), jnp.sin(angles)
    return (
        jnp.concatenate([cosine, cosine], axis=1),
        jnp.concatenate([-sine, sine], axis=1),
    )


def columns_of(rows, index):
    chosen = (lax.broadcasted_iota(jnp.int32, (rows.shape[0], HDIM), 0) == index).astype(
        jnp.float32
    )
    return lax.dot_general(
        rows,
        chosen,
        (((0,), (0,)), ((), ())),
        precision=lax.Precision.HIGHEST,
        preferred_element_type=jnp.float32,
    )


def row_sums(values):
    ones = jnp.ones((8, HDIM), jnp.float32)
    folded = sum(
        values[:, first : first + HDIM] for first in range(0, values.shape[1], HDIM)
    )
    return lax.dot_general(
        ones,
        folded,
        (((1,), (1,)), ((), ())),
        precision=lax.Precision.HIGHEST,
        preferred_element_type=jnp.float32,
    )[:1]


def rstd_of(squares, index):
    return lax.rsqrt(columns_of(squares, index) * (1.0 / D) + epsilon)


def prepare_kernel(raw, squares, gain_q, gain_k, cosine, sine, q_out, k_out, v_out):
    width = q_out.shape[1]
    table_c, table_s = cosine[...], sine[...]
    both = squares[...]
    for index, (gain, out) in enumerate(((gain_q, q_out), (gain_k, k_out))):
        rstd = rstd_of(both, index)
        for head in range(width // HDIM):
            cols = slice(head * HDIM, (head + 1) * HDIM)
            base = index * width + head * HDIM
            norm = raw[:, base : base + HDIM] * rstd * gain[:, cols]
            turned = norm * table_c + pltpu.roll(norm, HDIM // 2, 1) * table_s
            out[:, cols] = turned.astype(jnp.bfloat16)
    v_out[...] = raw[:, 2 * width :].astype(jnp.bfloat16)


def prepare(raw, squares, gain_q, gain_k, cosine, sine):
    rows, width = raw.shape[0], raw.shape[1] // 3
    whole = pl.BlockSpec((1, width), lambda i: (0, 0))
    table = pl.BlockSpec((BLOCK, HDIM), lambda i: (i, 0))
    out = pl.BlockSpec((BLOCK, width), lambda i: (i, 0))
    return pl.pallas_call(
        prepare_kernel,
        grid=(rows // BLOCK,),
        in_specs=[
            pl.BlockSpec((BLOCK, 3 * width), lambda i: (i, 0)),
            pl.BlockSpec((2, BLOCK), lambda i: (0, i)),
            whole,
            whole,
            table,
            table,
        ],
        out_specs=[out] * 3,
        out_shape=[jax.ShapeDtypeStruct((rows, width), jnp.bfloat16)] * 3,
        cost_estimate=BESIDE,
        name="prepare",
    )(raw, squares, gain_q[None], gain_k[None], cosine, sine)


def allowed_keys(starts, first_key, first_query):
    shape = (BLOCK, BLOCK)
    keys = first_key + lax.broadcasted_iota(jnp.int32, shape, 0)
    queries = first_query + lax.broadcasted_iota(jnp.int32, shape, 1)
    return (keys >= starts) & (keys <= queries)


def head_columns(head):
    return slice(head * HDIM, (head + 1) * HDIM)


def forward_kernel(low_ref, q_ref, k_ref, v_ref, start_ref, attn_ref, full_ref, log_ref):
    block = pl.program_id(0)
    heads = q_ref.shape[1] // HDIM
    starts = start_ref[...]
    scale = 1.0 / math.sqrt(HDIM)

    def step(index, carried):
        rows = pl.ds(pl.multiple_of(index * BLOCK, BLOCK), BLOCK)
        allowed = allowed_keys(starts, index * BLOCK, block * BLOCK)
        after_step = []
        for head, (peak, total, acc) in enumerate(carried):
            cols = head_columns(head)
            scores = contract_cols(k_ref[rows, cols], q_ref[:, cols]) * scale
            scores = jnp.where(allowed, scores, masked_score)
            new_peak = jnp.maximum(peak, jnp.max(scores, axis=0, keepdims=True))
            fade = jnp.exp(peak - new_peak)
            weights = jnp.exp(scores - new_peak)
            total = total * fade + jnp.sum(weights, axis=0, keepdims=True)
            acc = acc * fade + contract_rows(v_ref[rows, cols], weights.astype(jnp.bfloat16))
            after_step.append((new_peak, total, acc))
        return tuple(after_step)

    start = (
        jnp.full((1, BLOCK), masked_score, jnp.float32),
        jnp.zeros((1, BLOCK), jnp.float32),
        jnp.zeros((HDIM, BLOCK), jnp.float32),
    )
    carried = step(block, (start,) * heads)
    carried = lax.fori_loop(low_ref[block], block, step, carried)
    for head, (peak, total, acc) in enumerate(carried):
        out = jnp.transpose(acc / total)
        full_ref[:, head_columns(head)] = out
        attn_ref[:, head_columns(head)] = out.astype(jnp.bfloat16)
        log_ref[head] = peak + jnp.log(total)


def attention_forward(q_b, k_b, v_b, starts, low_block):
    rows, width = q_b.shape
    heads = width // HDIM
    own = pl.BlockSpec((BLOCK, width), lambda i, low: (i, 0))
    whole = pl.BlockSpec((rows, width), lambda i, low: (0, 0))
    return pl.pallas_call(
        forward_kernel,
        grid_spec=pltpu.PrefetchScalarGridSpec(
            num_scalar_prefetch=1,
            grid=(rows // BLOCK,),
            in_specs=[own, whole, whole, pl.BlockSpec((1, BLOCK), lambda i, low: (0, i))],
            out_specs=[own, own, pl.BlockSpec((heads, 1, BLOCK), lambda i, low: (0, 0, i))],
        ),
        out_shape=[
            jax.ShapeDtypeStruct((rows, width), jnp.bfloat16),
            jax.ShapeDtypeStruct((rows, width), jnp.float32),
            jax.ShapeDtypeStruct((heads, 1, rows), jnp.float32),
        ],
        compiler_params=pltpu.CompilerParams(vmem_limit_bytes=VMEM_BYTES),
        cost_estimate=BESIDE,
        name="attention_forward",
    )(low_block, q_b, k_b, v_b, starts)


def backward_kernel(
    high_ref, q_ref, k_ref, v_ref, grad_ref, full_ref, log_ref, start_ref, dq_ref, dk_ref, dv_ref, delta
):
    block = pl.program_id(0)
    blocks = pl.num_programs(0)
    heads = q_ref.shape[1] // HDIM
    scale = 1.0 / math.sqrt(HDIM)

    @pl.when(block == 0)
    def _():
        dq_ref[...] = jnp.zeros_like(dq_ref)

        def one(index, unused):
            rows = pl.ds(pl.multiple_of(index * BLOCK, BLOCK), BLOCK)
            for head in range(heads):
                cols = head_columns(head)
                delta[head, :, rows] = row_sums(
                    grad_ref[rows, cols].astype(jnp.float32) * full_ref[rows, cols]
                )
            return unused

        lax.fori_loop(0, blocks, one, 0)

    here = pl.ds(pl.multiple_of(block * BLOCK, BLOCK), BLOCK)

    def step(index, carried):
        rows = pl.ds(pl.multiple_of(index * BLOCK, BLOCK), BLOCK)
        allowed = allowed_keys(start_ref[:, rows], block * BLOCK, index * BLOCK)
        after_step = []
        for head, (dk, dv) in enumerate(carried):
            cols = head_columns(head)
            keys, values = k_ref[here, cols], v_ref[here, cols]
            queries, grads = q_ref[rows, cols], grad_ref[rows, cols]
            scores = contract_cols(keys, queries) * scale
            probs = jnp.where(allowed, jnp.exp(scores - log_ref[head, :, rows]), 0.0)
            dv = dv + dot(probs.astype(jnp.bfloat16), grads)
            d_probs = contract_cols(values, grads)
            d_scores = (probs * (d_probs - delta[head, :, rows])).astype(jnp.bfloat16)
            dk = dk + dot(d_scores, queries)
            dq_ref[rows, cols] += contract_rows(d_scores, keys)
            after_step.append((dk, dv))
        return tuple(after_step)

    zero = jnp.zeros((BLOCK, HDIM), jnp.float32)
    carried = lax.fori_loop(block, high_ref[block] + 1, step, ((zero, zero),) * heads)
    for head, (dk, dv) in enumerate(carried):
        dk_ref[:, head_columns(head)] = dk * scale
        dv_ref[:, head_columns(head)] = dv.astype(jnp.bfloat16)

    @pl.when(block == blocks - 1)
    def _():
        dq_ref[...] = dq_ref[...] * scale


def attention_backward(q_b, k_b, v_b, grads, full, logs, starts, high_block):
    rows, width = q_b.shape
    heads = width // HDIM
    own = pl.BlockSpec((BLOCK, width), lambda i, high: (i, 0))
    whole = pl.BlockSpec((rows, width), lambda i, high: (0, 0))
    out = jax.ShapeDtypeStruct((rows, width), jnp.float32)
    return pl.pallas_call(
        backward_kernel,
        grid_spec=pltpu.PrefetchScalarGridSpec(
            num_scalar_prefetch=1,
            grid=(rows // BLOCK,),
            in_specs=[whole] * 5
            + [
                pl.BlockSpec((heads, 1, rows), lambda i, high: (0, 0, 0)),
                pl.BlockSpec((1, rows), lambda i, high: (0, 0)),
            ],
            out_specs=[whole, own, own],
            scratch_shapes=[pltpu.VMEM((heads, 1, rows), jnp.float32)],
        ),
        out_shape=[out, out, jax.ShapeDtypeStruct((rows, width), jnp.bfloat16)],
        compiler_params=pltpu.CompilerParams(vmem_limit_bytes=VMEM_BYTES),
        cost_estimate=BESIDE,
        name="attention_backward",
    )(high_block, q_b, k_b, v_b, grads, full, logs, starts)


def norm_grads_kernel(
    dq_ref, dk_ref, raw, squares, gain_q, gain_k, cosine, sine, dq_out, dk_out, dots, q_part, k_part
):
    width = dq_ref.shape[1]
    table_c, table_s = cosine[...], sine[...]
    both = squares[...]

    @pl.when(pl.program_id(0) == 0)
    def _():
        q_part[...] = jnp.zeros_like(q_part)
        k_part[...] = jnp.zeros_like(k_part)

    for index, (grad, gain, out, gain_part) in enumerate(
        ((dq_ref, gain_q, dq_out, q_part), (dk_ref, gain_k, dk_out, k_part))
    ):
        rstd = rstd_of(both, index)
        products = jnp.zeros((BLOCK, HDIM), jnp.float32)
        for head in range(width // HDIM):
            cols = slice(head * HDIM, (head + 1) * HDIM)
            base = index * width + head * HDIM
            turned = grad[:, cols]
            norm = turned * table_c - pltpu.roll(turned, HDIM // 2, 1) * table_s
            out[:, cols] = norm
            product = raw[:, base : base + HDIM] * norm
            gain_part[:, cols] += jnp.sum((product * rstd).reshape(BLOCK // 8, 8, HDIM), axis=0)
            products = products + product * gain[:, cols]
        dots[index : index + 1, :] = row_sums(products)


def norm_grads(d_q_rot, d_k_rot, raw, squares, gain_q, gain_k, cosine, sine):
    rows, width = d_q_rot.shape
    whole = pl.BlockSpec((1, width), lambda i: (0, 0))
    table = pl.BlockSpec((BLOCK, HDIM), lambda i: (i, 0))
    own = pl.BlockSpec((BLOCK, width), lambda i: (i, 0))
    pair = pl.BlockSpec((2, BLOCK), lambda i: (0, i))
    total = pl.BlockSpec((8, width), lambda i: (0, 0))
    grad = jax.ShapeDtypeStruct((rows, width), jnp.float32)
    return pl.pallas_call(
        norm_grads_kernel,
        grid=(rows // BLOCK,),
        in_specs=[
            own,
            own,
            pl.BlockSpec((BLOCK, 2 * width), lambda i: (i, 0)),
            pair,
            whole,
            whole,
            table,
            table,
        ],
        out_specs=[own, own, pair, total, total],
        out_shape=[
            grad,
            grad,
            jax.ShapeDtypeStruct((2, rows), jnp.float32),
            jax.ShapeDtypeStruct((8, width), jnp.float32),
            jax.ShapeDtypeStruct((8, width), jnp.float32),
        ],
        cost_estimate=BESIDE,
        name="norm_grads",
    )(d_q_rot, d_k_rot, raw, squares, gain_q[None], gain_k[None], cosine, sine)


def raw_grads_kernel(dq_ref, dk_ref, dv_ref, raw, squares, dots, gain_q, gain_k, out):
    width = dq_ref.shape[1]
    both, sums = squares[...], dots[...]
    for index, (grad, gain) in enumerate(((dq_ref, gain_q), (dk_ref, gain_k))):
        rstd = rstd_of(both, index)
        share = rstd * rstd * rstd * columns_of(sums, index) * (1.0 / D)
        for head in range(width // HDIM):
            cols = slice(head * HDIM, (head + 1) * HDIM)
            base = index * width + head * HDIM
            value = rstd * gain[:, cols] * grad[:, cols] - raw[:, base : base + HDIM] * share
            out[:, base : base + HDIM] = value.astype(jnp.bfloat16)
    out[:, 2 * width :] = dv_ref[...]


def raw_grads(d_q_norm, d_k_norm, d_v, raw, squares, dots, gain_q, gain_k):
    rows, width = d_q_norm.shape
    whole = pl.BlockSpec((1, width), lambda i: (0, 0))
    own = pl.BlockSpec((BLOCK, width), lambda i: (i, 0))
    wide = pl.BlockSpec((BLOCK, 3 * width), lambda i: (i, 0))
    pair = pl.BlockSpec((2, BLOCK), lambda i: (0, i))
    return pl.pallas_call(
        raw_grads_kernel,
        grid=(rows // BLOCK,),
        in_specs=[
            own,
            own,
            own,
            pl.BlockSpec((BLOCK, 2 * width), lambda i: (i, 0)),
            pair,
            pair,
            whole,
            whole,
        ],
        out_specs=wide,
        out_shape=jax.ShapeDtypeStruct((rows, 3 * width), jnp.bfloat16),
        cost_estimate=BESIDE,
        name="raw_grads",
    )(d_q_norm, d_k_norm, d_v, raw, squares, dots, gain_q[None], gain_k[None])


def dot(left, right):
    return jnp.dot(left, right, preferred_element_type=jnp.float32)


def contract_rows(left, right):
    return lax.dot_general(
        left, right, (((0,), (0,)), ((), ())), preferred_element_type=jnp.float32
    )


def contract_cols(left, right):
    return lax.dot_general(
        left, right, (((1,), (1,)), ((), ())), preferred_element_type=jnp.float32
    )


def column_block(rows, width):
    return min(width, 512 if rows <= 1024 else 256)


def matmul_params():
    return pltpu.CompilerParams(vmem_limit_bytes=56 * 1024 * 1024)


def hidden_kernel(x_ref, gate_w, up_w, gate_out, up_out, hidden_out):
    gate = dot(x_ref[...], gate_w[...])
    up_part = dot(x_ref[...], up_w[...])
    gate_out[...] = gate
    up_out[...] = up_part
    hidden_out[...] = (gate * jax.nn.sigmoid(gate) * up_part).astype(jnp.bfloat16)


def hidden_units(x, gate_full, up_full):
    rows, depth = x.shape
    width = gate_full.shape[1]
    block = column_block(rows, width)
    weight = pl.BlockSpec((depth, block), lambda j: (0, j))
    out = pl.BlockSpec((rows, block), lambda j: (0, j))
    return pl.pallas_call(
        hidden_kernel,
        grid=(width // block,),
        in_specs=[pl.BlockSpec((rows, depth), lambda j: (0, 0)), weight, weight],
        out_specs=[out] * 3,
        out_shape=[
            jax.ShapeDtypeStruct((rows, width), jnp.float32),
            jax.ShapeDtypeStruct((rows, width), jnp.float32),
            jax.ShapeDtypeStruct((rows, width), jnp.bfloat16),
        ],
        compiler_params=matmul_params(),
        cost_estimate=BESIDE,
        name="hidden_units",
    )(x, gate_full, up_full)


def hidden_grads_kernel(grad_ref, weight, gate_ref, up_ref, gate_out, up_out):
    d_hidden = dot(grad_ref[...], weight[...])
    gate = gate_ref[...]
    gate_sigmoid = jax.nn.sigmoid(gate)
    silu = gate * gate_sigmoid
    gate_out[...] = (
        d_hidden * up_ref[...] * (gate_sigmoid * (1.0 + gate * (1.0 - gate_sigmoid)))
    ).astype(jnp.bfloat16)
    up_out[...] = (d_hidden * silu).astype(jnp.bfloat16)


def hidden_grads(grad, down_full, gate, up_part):
    rows, depth = grad.shape
    width = down_full.shape[1]
    block = column_block(rows, width)
    part_spec = pl.BlockSpec((rows, block), lambda j: (0, j))
    out = jax.ShapeDtypeStruct((rows, width), jnp.bfloat16)
    return pl.pallas_call(
        hidden_grads_kernel,
        grid=(width // block,),
        in_specs=[
            pl.BlockSpec((rows, depth), lambda j: (0, 0)),
            pl.BlockSpec((depth, block), lambda j: (0, j)),
            part_spec,
            part_spec,
        ],
        out_specs=[part_spec] * 2,
        out_shape=[out] * 2,
        compiler_params=matmul_params(),
        cost_estimate=BESIDE,
        name="hidden_grads",
    )(grad, down_full, gate, up_part)


def products_kernel(count, *refs):
    total = None
    for left, right in zip(refs[:count], refs[count : 2 * count]):
        term = contract_cols(left[...], right[...])
        total = term if total is None else total + term
    refs[-1][...] = total.astype(jnp.bfloat16)


def sum_products(lefts, rights):
    rows, depth = lefts[0].shape
    width = rights[0].shape[0]
    block = column_block(rows, width)
    return pl.pallas_call(
        functools.partial(products_kernel, len(lefts)),
        grid=(width // block,),
        in_specs=[pl.BlockSpec((rows, depth), lambda j: (0, 0)) for _ in lefts]
        + [pl.BlockSpec((block, depth), lambda j: (j, 0)) for _ in rights],
        out_specs=pl.BlockSpec((rows, block), lambda j: (0, j)),
        out_shape=jax.ShapeDtypeStruct((rows, width), jnp.bfloat16),
        compiler_params=matmul_params(),
        cost_estimate=BESIDE,
        name="sum_products",
    )(*lefts, *rights)


def weight_grad_kernel(count, *refs):
    total = None
    for left, right in zip(refs[:count], refs[count : 2 * count]):
        term = contract_rows(left[...], right[...])
        total = term if total is None else total + term
    refs[-1][...] = total.astype(jnp.bfloat16)


def weight_grad(lefts, rights):
    heights = [left.shape[0] for left in lefts]
    if len(rights) == 1 < len(lefts):
        rights, places = rights * len(lefts), list(range(len(lefts)))
    else:
        places = [0] * len(lefts)
    height, width = lefts[0].shape[1], rights[0].shape[1]
    tall, wide = min(height, 512), min(width, 1024)
    return pl.pallas_call(
        functools.partial(weight_grad_kernel, len(lefts)),
        grid=(width // wide, height // tall),
        in_specs=[pl.BlockSpec((rows, tall), lambda j, i: (0, i)) for rows in heights]
        + [
            pl.BlockSpec((rows, wide), functools.partial(lambda place, j, i: (place, j), place))
            for rows, place in zip(heights, places)
        ],
        out_specs=pl.BlockSpec((tall, wide), lambda j, i: (i, j)),
        out_shape=jax.ShapeDtypeStruct((height, width), jnp.bfloat16),
        compiler_params=matmul_params(),
        cost_estimate=BESIDE,
        name="weight_grad",
    )(*lefts, *rights)


def stacked_weight_grad(left, right, count):
    rows, height = left.shape
    width = right.shape[1] // count
    tall = min(height, 512)
    return pl.pallas_call(
        functools.partial(weight_grad_kernel, 1),
        grid=(count, height // tall),
        in_specs=[
            pl.BlockSpec((rows, tall), lambda j, i: (0, i)),
            pl.BlockSpec((rows, width), lambda j, i: (0, j)),
        ],
        out_specs=pl.BlockSpec((None, tall, width), lambda j, i: (j, i, 0)),
        out_shape=jax.ShapeDtypeStruct((count, height, width), jnp.bfloat16),
        compiler_params=matmul_params(),
        cost_estimate=BESIDE,
        name="stacked_weight_grad",
    )(left, right)


def move_rows(places, wanted_first, count, rows_ref):
    wanted = wanted_first + lax.broadcasted_iota(jnp.int32, (count, places.shape[1]), 0)
    chosen = jnp.where(places == wanted, 1.0, 0.0).astype(jnp.bfloat16)
    return dot(chosen, rows_ref[...]).astype(jnp.bfloat16)


def pick_rows(places, rows_ref):
    columns = lax.broadcasted_iota(jnp.int32, (places.shape[0], rows_ref.shape[0]), 1)
    chosen = jnp.where(places == columns, 1.0, 0.0).astype(jnp.bfloat16)
    return dot(chosen, rows_ref[...]).astype(jnp.bfloat16)


def pack_kernel(places, tokens_ref, weight, packed_out, raw_out, squares_out):
    packed = pick_rows(places[...], tokens_ref)
    packed_out[...] = packed
    raw = dot(packed, weight[...])
    raw_out[...] = raw
    width = raw.shape[1] // 3
    for index in range(2):
        cols = raw[:, index * width : (index + 1) * width]
        squares_out[index : index + 1, :] = row_sums(cols * cols)


def pack(perm_row, tokens_all, qkv_full):
    rows, depth = tokens_all.shape
    width = qkv_full.shape[1]
    return pl.pallas_call(
        pack_kernel,
        grid=(rows // BLOCK,),
        in_specs=[
            pl.BlockSpec((BLOCK, 1), lambda i: (i, 0)),
            pl.BlockSpec((rows, depth), lambda i: (0, 0)),
            pl.BlockSpec((depth, width), lambda i: (0, 0)),
        ],
        out_specs=[
            pl.BlockSpec((BLOCK, depth), lambda i: (i, 0)),
            pl.BlockSpec((BLOCK, width), lambda i: (i, 0)),
            pl.BlockSpec((2, BLOCK), lambda i: (0, i)),
        ],
        out_shape=[
            jax.ShapeDtypeStruct((rows, depth), jnp.bfloat16),
            jax.ShapeDtypeStruct((rows, width), jnp.float32),
            jax.ShapeDtypeStruct((2, rows), jnp.float32),
        ],
        compiler_params=matmul_params(),
        cost_estimate=BESIDE,
        name="pack",
    )(perm_row[:, None], tokens_all, qkv_full)


def given_kernel(count, places, rows_ref, weight, moved_out, product_out):
    moved = move_rows(places[...], pl.program_id(0) * count, count, rows_ref)
    moved_out[...] = moved
    product_out[...] = contract_cols(moved, weight[...]).astype(jnp.bfloat16)


def give_back(place_row, value, weight):
    rows, depth = value.shape
    width = weight.shape[0]
    count = 512
    return pl.pallas_call(
        functools.partial(given_kernel, count),
        grid=(rows // count,),
        in_specs=[
            pl.BlockSpec((1, rows), lambda i: (0, 0)),
            pl.BlockSpec((rows, depth), lambda i: (0, 0)),
            pl.BlockSpec((width, depth), lambda i: (0, 0)),
        ],
        out_specs=[
            pl.BlockSpec((count, depth), lambda i: (i, 0)),
            pl.BlockSpec((count, width), lambda i: (i, 0)),
        ],
        out_shape=[
            jax.ShapeDtypeStruct((rows, depth), jnp.bfloat16),
            jax.ShapeDtypeStruct((rows, width), jnp.bfloat16),
        ],
        compiler_params=matmul_params(),
        cost_estimate=BESIDE,
        name="give_back",
    )(place_row[None], value, weight)


def pick_products_kernel(count, *refs):
    places, pieces, weight = refs[0], refs[1 : 1 + count], refs[1 + count]
    out, products = refs[2 + count], refs[3 + count]
    step, first = BLOCK, 0
    for piece in pieces:
        height = piece.shape[0]

        def one(index, unused, piece=piece, first=first):
            here = pl.ds(pl.multiple_of(index * step, step), step)
            there = pl.ds(pl.multiple_of(first + index * step, step), step)
            products[there, :] = dot(piece[here, :], weight[...]).astype(jnp.bfloat16)
            return unused

        lax.fori_loop(0, height // step, one, 0)
        first += height

    def pick_block(index, unused):
        here = pl.ds(pl.multiple_of(index * step, step), step)
        out[here, :] = pick_rows(places[here, :], products)
        return unused

    lax.fori_loop(0, out.shape[0] // step, pick_block, 0)


def pick_products(place_row, pieces, weight):
    rows, width = place_row.shape[0], weight.shape[1]
    vmem = pl.BlockSpec(memory_space=pltpu.VMEM)
    return pl.pallas_call(
        functools.partial(pick_products_kernel, len(pieces)),
        in_specs=[vmem] * (2 + len(pieces)),
        out_specs=vmem,
        out_shape=jax.ShapeDtypeStruct((rows, width), jnp.bfloat16),
        scratch_shapes=[pltpu.VMEM((rows, width), jnp.bfloat16)],
        compiler_params=matmul_params(),
        cost_estimate=BESIDE,
        name="pick_products",
    )(place_row[:, None], *pieces, weight)


def rms_back(values, rstd, gain_vec, grad):
    scaled = grad * gain_vec
    row_dots = jnp.sum(values * scaled, axis=1, keepdims=True)
    return rstd * scaled - values * (rstd * rstd * rstd) * row_dots / D


def per_device(
    tokens,
    upstream,
    lengths,
    permutation,
    w_query,
    w_key,
    w_value,
    w_out,
    w_gate,
    w_up,
    w_down,
    q_gain,
    k_gain,
    attn_gain,
    ffn_gain,
):
    rank = lax.axis_index("core") * lax.axis_size("tl") + lax.axis_index("tl")
    own_rows = tokens.shape[0]
    group_rows = own_rows * 2 * lax.axis_size("tl")
    local_width = w_query.shape[1]

    own_group = lax.axis_index("core") == lax.axis_index("th")
    layout_row = jnp.concatenate([permutation, lengths], axis=1)
    layout_row = jnp.where(own_group, layout_row, swap(layout_row, "core"))[0]
    perm_row, length_row = layout_row[:group_rows], layout_row[group_rows:]

    tokens_all, qkv_full, out_full, gate_pair = enter(
        tokens,
        [((w_query, w_key, w_value), True), ((w_out.T,), True), ((w_gate,), False)],
    )
    gate_full = gather_weight(gate_pair)
    up_shard, tokens_all = lax.optimization_barrier((w_up, tokens_all))
    up_pair = pair_of_weight(up_shard)
    tokens = lax.dynamic_slice_in_dim(tokens_all, rank * own_rows, own_rows)

    perm_place = row_place(perm_row, own_rows)
    position, starts = layout(length_row, group_rows)
    cosine, sine = rotary_tables(position)
    blocks = group_rows // BLOCK
    low_block = starts[::BLOCK] // BLOCK
    last_keys = (jnp.arange(blocks, dtype=jnp.int32) + 1) * BLOCK - 1
    reached = jnp.sum((starts[None, :] <= last_keys[:, None]).astype(jnp.int32), axis=1)
    high_block = (reached - 1) // BLOCK

    packed, raw, squares = pack(perm_row, tokens_all, qkv_full)
    up_pair, raw = lax.optimization_barrier((up_pair, raw))
    up_full = gather_weight(up_pair)
    squares = sum_over(squares, RANK)
    down_shard, squares = lax.optimization_barrier((w_down.T, squares))
    down_pair = pair_of_weight(down_shard)
    gain_q = lax.dynamic_slice_in_dim(q_gain, rank * local_width, local_width)
    gain_k = lax.dynamic_slice_in_dim(k_gain, rank * local_width, local_width)
    q_b, k_b, v_b = prepare(raw, squares, gain_q, gain_k, cosine, sine)
    attn_b, attn_f, logs = attention_forward(q_b, k_b, v_b, starts[None], low_block)

    parts = PARTS if small_grid() else 1
    part_rows = own_rows // parts

    def part_of(value, index):
        return part(value, 0, index, parts)

    def pieces_of(value, index):
        whole = part_of(value, index)
        return [part(whole, 0, 0, 2), part(whole, 0, 1, 2)] if small_grid() else [whole]

    sides = 2 if small_grid() else 1
    attn_given, attn_parts = give_back(perm_place, attn_b, out_full)
    down_pair, attn_parts = lax.optimization_barrier((down_pair, attn_parts))
    down_full = gather_weight(down_pair)
    order = [(side, index) for side in range(sides) for index in range(parts)]
    token = None

    def pass_through(make_rows, begin, finish, late, between=None):
        nonlocal token
        gathered, far_pieces, begun, sums, scattered = {}, {}, {}, {}, []

        def complete(side, index):
            nonlocal token
            sums[side, index] = finish(*begun[side, index], token)
            if scattered and sides == 2 and not late:
                *others, last = scattered[-1]
                sums[side, index], last = lax.optimization_barrier((sums[side, index], last))
                scattered[-1] = (*others, last)
            token = sums[side, index]

        def scatter(index):
            scattered.append(start_scatter([sums[side, index] for side in range(sides)]))

        for side, index in order:
            if side == 0:
                gathered[index] = start_gather(make_rows(index, token))
                if sides == 2 and index > 0 and not late:
                    far_pieces[index - 1] = forward_rows(gathered[index - 1], token)
                piece = gathered[index][0]
            else:
                if late:
                    far_pieces[index] = forward_rows(gathered[index], token)
                elif index == 0:
                    far_pieces[parts - 1] = forward_rows(gathered[parts - 1], token)
                    if between is not None:
                        near = [gathered[each][0] for each in range(parts)]
                        token = between(near, [far_pieces[each] for each in range(parts)], token)
                piece = far_pieces[index]
            begun[side, index] = begin((index, side), piece, token)
            token = begun[side, index][0]
            if not late:
                complete(side, index)
                if side == sides - 1:
                    scatter(index)
        if late:
            for index in range(parts):
                for side in reversed(range(sides)):
                    complete(side, index)
                scatter(index)
        return scattered

    attn_sums = [start_scatter(pieces_of(attn_parts, index)) for index in range(parts)]
    attn_outs, resids, saved = [], [], {}

    def resid_rows(index, token):
        attn_out = finish_scatter_rows(attn_sums[index], token)
        rstd_a = lax.rsqrt(jnp.mean(attn_out * attn_out, axis=1, keepdims=True) + epsilon)
        attn_outs.append((attn_out, rstd_a))
        resids.append(part_of(tokens, index).astype(jnp.float32) + attn_out * rstd_a * attn_gain)
        return resids[-1].astype(jnp.bfloat16)

    def feed_forward(key, piece, token):
        gate, up_part, hidden_b = hidden_units(after(token, piece), gate_full, up_full)
        saved[key] = (piece, gate, up_part, hidden_b)
        return (hidden_b,)

    def feed_down(hidden_b, token):
        return sum_products([after(token, hidden_b)], [down_full])

    upstream_turn = start_turn(after(attn_parts, upstream))
    mlp_sums = pass_through(resid_rows, feed_forward, feed_down, True)
    token, upstream_turn = lax.optimization_barrier((token, upstream_turn))
    upstream = finish_turn(*upstream_turn)
    layer_outs, gain_parts, grads_f, back = [], [], [], {}

    def d_mlp_rows(index, token):
        mlp_out = finish_scatter_rows(mlp_sums[index], token)
        rstd_m = lax.rsqrt(jnp.mean(mlp_out * mlp_out, axis=1, keepdims=True) + epsilon)
        normed_m = mlp_out * rstd_m
        layer_outs.append((resids[index] + normed_m * ffn_gain).astype(jnp.bfloat16))
        grads_f.append(part_of(upstream, index).astype(jnp.float32))
        gain_parts.append(jnp.sum(grads_f[index] * normed_m, axis=0))
        return rms_back(mlp_out, rstd_m, ffn_gain, grads_f[index]).astype(jnp.bfloat16)

    def feed_back(key, piece, token):
        _, gate, up_part, _ = saved[key]
        d_gate_b, d_up_b = hidden_grads(after(token, piece), down_full, gate, up_part)
        back[key] = (piece, d_gate_b, d_up_b)
        return d_gate_b, d_up_b

    def feed_up(d_gate_b, d_up_b, token):
        return sum_products([after(token, d_gate_b), d_up_b], [gate_full, up_full])

    weight_grads = []

    def first_weight_grad(near, far, token):
        grads = [piece for index in range(parts) for piece in (near[index], far[index])]
        weight_grads.append(weight_grad(after(token, grads), [saved[key][3] for key in sorted(saved)]))
        return weight_grads[0]

    resid_sums = pass_through(d_mlp_rows, feed_back, feed_up, False, first_weight_grad)
    layer_out = jnp.concatenate(layer_outs, axis=0)
    keys = sorted(saved)
    ffn_gain_part = sum(gain_parts)
    attn_gain_part = 0.0
    d_resids, gathered, near_pieces = [], [], []
    operands = [
        ([back[key][0] for key in keys], [saved[key][3] for key in keys]),
        ([saved[key][0] for key in keys], [back[key][1] for key in keys]),
        ([saved[key][0] for key in keys], [back[key][2] for key in keys]),
    ]

    def next_weight_grad(token):
        left, right = operands[len(weight_grads)]
        left, right = after(token, (left, right))
        weight_grads.append(weight_grad(left, right))
        return weight_grads[-1]

    for index in range(parts):
        terms = resid_sums[index]
        if index == 0:
            d_sums = finish_scatter_rows(terms, token)
        else:
            last, weight_grads[-1] = lax.optimization_barrier((terms[-1], weight_grads[-1]))
            d_sums = finish_scatter_rows([*terms[:-1], last], None)
        attn_out, rstd_a = attn_outs[index]
        d_resid = grads_f[index] + d_sums
        d_resids.append(d_resid)
        attn_gain_part = attn_gain_part + jnp.sum(d_resid * attn_out * rstd_a, axis=0)
        d_attn_b = rms_back(attn_out, rstd_a, attn_gain, d_resid).astype(jnp.bfloat16)
        if sides == 2:
            near_pieces.append([d_attn_b, swap(d_attn_b, "core")])
            gathered.append((None, swap(d_attn_b, "tl")))
        else:
            gathered.append(start_gather(d_attn_b))
        token = next_weight_grad((d_attn_b, token))
    far_pieces = []
    for index in range(parts):
        if sides == 2:
            far, weight_grads[-1] = lax.optimization_barrier((gathered[index][1], weight_grads[-1]))
            far_pieces.append([far, swap(far, "core")])
            token = far
        if len(weight_grads) < 3:
            token = next_weight_grad(token)
    while len(weight_grads) < 3:
        token = next_weight_grad(token)
    down_grad, gate_grad, up_grad = weight_grads
    d_attn_pieces = []
    for index in range(parts):
        if sides == 2:
            d_attn_pieces += [*near_pieces[index], *far_pieces[index]]
        else:
            d_attn_pieces.append(gathered[index][0])
    d_resid = jnp.concatenate(d_resids, axis=0)
    out_total = weight_grad(d_attn_pieces, [attn_given])
    d_packed = pick_products(perm_place, d_attn_pieces, out_full)
    down_split = start_split(scatter_pair(down_grad))
    gate_sum, up_sum = scatter_pair(gate_grad), scatter_pair(up_grad)
    layer_turn = start_turn(layer_out)
    d_packed, out_total = lax.optimization_barrier((d_packed, out_total))
    d_q_rot, d_k_rot, d_v = attention_backward(
        q_b, k_b, v_b, d_packed, attn_f, logs, starts[None], high_block
    )
    d_q_rot, down_split, layer_turn = lax.optimization_barrier((d_q_rot, down_split, layer_turn))
    gate_split = start_split(after(d_q_rot, gate_sum))
    d_q_norm, d_k_norm, dots, q_parts, k_parts = norm_grads(
        d_q_rot, d_k_rot, raw, squares, gain_q, gain_k, cosine, sine
    )
    q_gain_part, k_gain_part = jnp.sum(q_parts, axis=0), jnp.sum(k_parts, axis=0)
    dots = sum_over(dots, RANK)
    d_qkv_b = raw_grads(d_q_norm, d_k_norm, d_v, raw, squares, dots, gain_q, gain_k)
    qkv_totals = stacked_weight_grad(packed, d_qkv_b, 3)
    up_split = start_split(after(d_qkv_b, up_sum))
    _, input_parts = give_back(perm_place, d_qkv_b, qkv_full)
    down_shard, layer_out = finish_split(*down_split).T, finish_turn(*layer_turn)
    qkv_totals, down_shard, layer_out = lax.optimization_barrier((qkv_totals, down_shard, layer_out))
    input_parts, gate_split, up_split = lax.optimization_barrier((input_parts, gate_split, up_split))
    gate_shard, up_shard = finish_split(*gate_split), finish_split(*up_split)

    def placed(part_sum):
        return lax.dynamic_update_slice_in_dim(
            jnp.zeros((D,), jnp.float32), part_sum, rank * local_width, 0
        )

    gains = jnp.stack(
        [placed(q_gain_part), placed(k_gain_part), attn_gain_part, ffn_gain_part]
        + [jnp.zeros((D,), jnp.float32)] * 4
    )
    tokens_grad, gain_grads, out_shard, query_shard, key_shard, value_shard = leave(
        input_parts,
        d_resid,
        gains,
        [
            (out_total, [local_width], False),
            (qkv_totals, [local_width], False),
        ],
    )

    return (
        layer_out,
        tokens_grad,
        query_shard,
        key_shard,
        value_shard,
        out_shard.T,
        gate_shard,
        up_shard,
        down_shard,
        gain_grads[0],
        gain_grads[1],
        gain_grads[2],
        gain_grads[3],
    )


def solution(mesh):
    dp, tensor = mesh.shape["dp"], mesh.shape["tensor"]
    fine = Mesh(mesh.devices.reshape(dp // 4, 2, 2, 2, tensor // 2), DP + TENSOR)
    rows, weight, weight_out = P(DP + TENSOR, None), P(DP, TENSOR), P(TENSOR, DP)
    return jax.shard_map(
        per_device,
        mesh=fine,
        in_specs=(rows, rows, P(DP, None), P(DP, None))
        + (weight,) * 3
        + (weight_out, weight, weight, weight_out)
        + (P(),) * 4,
        out_specs=(rows, rows)
        + (weight,) * 3
        + (weight_out, weight, weight, weight_out)
        + (P(),) * 4,
        check_vma=False,
    )
```

```python
import functools
import math

import jax
import jax.numpy as jnp
from jax import lax
from jax.experimental import pallas as pl
from jax.experimental.pallas import tpu as pltpu
from jax.sharding import Mesh, PartitionSpec as P

D = 2048
HDIM = 128

epsilon = 1e-06
rope_base = 500000.0
masked_score = -1e30
BLOCK = 256
VMEM_BYTES = 48 * 1024 * 1024
MESH = pl.DeviceIdType.MESH
BESIDE = pl.CostEstimate(flops=1, bytes_accessed=1, transcendentals=0)
PARTS = 2

SWAP = [(0, 1), (1, 0)]
TURN = [(1, 2), (2, 1)]
CYCLE = [(0, 1), (1, 3), (3, 2), (2, 0)]
CYCLE_BACK = [(d, s) for s, d in CYCLE]
DP = ("a", "b", "core")
TENSOR = ("th", "tl")
RANK = ("core", "tl")


def swap(value, axis):
    return lax.ppermute(value, axis, SWAP)


def start_turn(value):
    return value, lax.ppermute(value, ("core", "th"), TURN)


def finish_turn(kept, arrived):
    stays = lax.axis_index("core") == lax.axis_index("th")
    return jnp.where(stays, kept, arrived)


def turn(value):
    return finish_turn(*start_turn(value))


def small_grid():
    return lax.axis_size("a") == 2 and lax.axis_size("tl") == 2


def part(value, dim, index, count):
    size = value.shape[dim] // count
    return lax.slice_in_dim(value, index * size, (index + 1) * size, axis=dim)


def in_turn(left, right):
    upper = lax.axis_index("th") == 0
    return jnp.where(upper, left, right), jnp.where(upper, right, left)


def pair_of_weight(shard):
    second = lax.ppermute(shard, ("core", "th"), CYCLE)
    return jnp.concatenate(in_turn(turn(shard), second), axis=0)


def gather_weight(pair):
    return lax.all_gather(pair, ("a", "b"), axis=0, tiled=True)


def scatter_pair(total):
    return lax.psum_scatter(
        total.astype(jnp.bfloat16), ("a", "b"), scatter_dimension=0, tiled=True
    )


def start_split(pair):
    first, second = in_turn(part(pair, 0, 0, 2), part(pair, 0, 1, 2))
    return first, start_turn(first)[1], lax.ppermute(second, ("core", "th"), CYCLE_BACK)


def finish_split(first, arrived, other):
    return finish_turn(first, arrived).astype(jnp.float32) + other.astype(jnp.float32)


def greet():
    a, b, core = lax.axis_index("a"), lax.axis_index("b"), lax.axis_index("core")
    th, tl = lax.axis_index("th"), lax.axis_index("tl")
    barrier = pltpu.get_barrier_semaphore()
    others = (
        {"a": 1 - a},
        {"b": 1 - b},
        {"core": 1 - core},
        {"tl": 1 - tl},
        {"th": 1 - th},
        {"core": 1 - core, "th": 1 - th},
    )
    for other in others:
        pl.semaphore_signal(barrier, inc=1, device_id=other, device_id_type=MESH)
    pl.semaphore_wait(barrier, len(others))


CHUNKS = 4


def entry_slots(plan):
    return 4 * CHUNKS + sum(3 * len(units) + 6 for units, _ in plan)


def entry_kernel(plan, *refs):
    shard_count = sum(len(units) for units, _ in plan)
    tokens, shards = refs[0], refs[1 : 1 + shard_count]
    tokens_all, fulls = refs[1 + shard_count], refs[2 + shard_count : -3]
    send, recv, local = refs[-3:]
    a, b, core = lax.axis_index("a"), lax.axis_index("b"), lax.axis_index("core")
    th, tl = lax.axis_index("th"), lax.axis_index("tl")
    stays = core == th
    greet()
    used = [0]

    def slots(count):
        used[0] += count
        return used[0] - count

    def remote(source, target, slot, to):
        return pltpu.make_async_remote_copy(
            src_ref=source,
            dst_ref=target,
            send_sem=send.at[slot],
            recv_sem=recv.at[slot],
            device_id=to,
            device_id_type=MESH,
        )

    def arrived(target, slot):
        remote(target, target, slot, {"core": 1 - core}).wait_recv()

    stages, taken = [], 0
    for full, (units, rings) in zip(fulls, plan):
        stage = []
        for column in units:
            shard = shards[taken]
            base = slots(3)
            height, width = shard.shape

            def place(sub, full=full, column=column, height=height, width=width, rings=rings):
                block = 4 * a + 2 * b if rings else 0
                row = pl.multiple_of((block + sub) * height, height)
                return full.at[pl.ds(row, height), pl.ds(column, width)]

            stage.append((shard, place, base, taken))
            taken += 1
        stages.append(stage)

    def near_copy(shard, place, base):
        return remote(shard, place(core), base + 2, {"core": 1 - core})

    def far_copy(shard, place, base):
        return remote(shard, place(core), base + core, {"core": th, "th": 1 - th})

    def start_stage(stage):
        for shard, place, base, index in stage:
            far_copy(shard, place, base).start()

            @pl.when(stays)
            def _():
                pltpu.make_async_copy(shard, place(core), local.at[index]).start()

            @pl.when(jnp.logical_not(stays))
            def _():
                near_copy(shard, place, base).start()

    def finish_stage(stage):
        for shard, place, base, index in stage:

            @pl.when(stays)
            def _():
                pltpu.make_async_copy(shard, place(core), local.at[index]).wait()
                arrived(place(1 - core), base + 2)

            @pl.when(jnp.logical_not(stays))
            def _():
                arrived(place(0), base)
                arrived(place(1), base + 1)

    def piece(full, block_a, block_b, sub):
        height = full.shape[0] // 8
        row = pl.multiple_of((4 * block_a + 2 * block_b + sub) * height, height)
        return full.at[pl.ds(row, height), :]

    def ring(full, base):
        to_a, to_b = {"a": 1 - a}, {"b": 1 - b}
        return (
            [remote(piece(full, a, b, sub), piece(full, a, b, sub), base + sub, to_b) for sub in (0, 1)],
            [remote(piece(full, a, b, sub), piece(full, a, b, sub), base + 2 + sub, to_a) for sub in (0, 1)],
            remote(piece(full, a, 1 - b, 0), piece(full, a, 1 - b, 0), base + 4, to_a),
            remote(piece(full, 1 - a, b, 1), piece(full, 1 - a, b, 1), base + 5, to_b),
        )

    ring_base = [slots(6) for _ in fulls]

    def start_ring(index):
        over_b, over_a, _, _ = ring(fulls[index], ring_base[index])
        for copy in (over_b[0], over_a[1], over_b[1], over_a[0]):
            copy.start()

    def forward_ring(index):
        full, base = fulls[index], ring_base[index]
        arrived(piece(full, a, 1 - b, 0), base)
        ring(full, base)[2].start()
        arrived(piece(full, 1 - a, b, 1), base + 3)
        ring(full, base)[3].start()

    def finish_ring(index):
        full, base = fulls[index], ring_base[index]
        arrived(piece(full, a, 1 - b, 1), base + 1)
        arrived(piece(full, 1 - a, b, 0), base + 2)
        arrived(piece(full, 1 - a, 1 - b, 0), base + 4)
        arrived(piece(full, 1 - a, 1 - b, 1), base + 5)
        over_b, over_a, first, second = ring(full, base)
        for copy in (*over_b, *over_a, first, second):
            copy.wait_send()

    rows = tokens.shape[0]
    step = rows // CHUNKS
    row_base = slots(4 * CHUNKS)

    def rows_of(block_core, block_tl, chunk):
        row = pl.multiple_of((2 * block_core + block_tl) * rows + chunk * step, step)
        return tokens_all.at[pl.ds(row, step), :]

    def row_copies(chunk):
        slot = row_base + 4 * chunk
        own, other = rows_of(core, tl, chunk), rows_of(core, 1 - tl, chunk)
        return (
            remote(
                tokens.at[pl.ds(chunk * step, step), :],
                rows_of(th, tl, chunk),
                slot,
                {"core": th, "th": core},
            ),
            remote(own, own, slot + 1, {"tl": 1 - tl}),
            remote(own, own, slot + 2, {"core": 1 - core}),
            remote(other, other, slot + 3, {"core": 1 - core}),
        )

    def own_rows(chunk):
        return pltpu.make_async_copy(
            tokens.at[pl.ds(chunk * step, step), :],
            rows_of(core, tl, chunk),
            local.at[shard_count + chunk],
        )

    for chunk in range(CHUNKS):

        @pl.when(stays)
        def _():
            own_rows(chunk).start()

    ringed = [index for index, (_, rings) in enumerate(plan) if rings]
    for index in ringed:
        start_stage(stages[index])
    for chunk in range(CHUNKS):

        @pl.when(jnp.logical_not(stays))
        def _():
            row_copies(chunk)[0].start()

        @pl.when(stays)
        def _():
            own_rows(chunk).wait()
            row_copies(chunk)[1].start()
            row_copies(chunk)[2].start()

    for index in ringed:
        finish_stage(stages[index])
        start_ring(index)
    for index in range(len(plan)):
        if index not in ringed:
            start_stage(stages[index])
    for chunk in range(CHUNKS):

        @pl.when(jnp.logical_not(stays))
        def _():
            arrived(rows_of(core, tl, chunk), row_base + 4 * chunk)
            row_copies(chunk)[1].start()
            row_copies(chunk)[2].start()

    for index in ringed:
        forward_ring(index)
    for chunk in range(CHUNKS):
        arrived(rows_of(core, 1 - tl, chunk), row_base + 4 * chunk + 1)
        row_copies(chunk)[3].start()
    for index in ringed:
        finish_ring(index)
    for index in range(len(plan)):
        if index not in ringed:
            finish_stage(stages[index])
    for chunk in range(CHUNKS):
        arrived(rows_of(1 - core, tl, chunk), row_base + 4 * chunk + 2)
        arrived(rows_of(1 - core, 1 - tl, chunk), row_base + 4 * chunk + 3)

        @pl.when(jnp.logical_not(stays))
        def _():
            row_copies(chunk)[0].wait_send()

        for copy in row_copies(chunk)[1:]:
            copy.wait_send()
    for stage in stages:
        for shard, place, base, _ in stage:
            far_copy(shard, place, base).wait_send()

            @pl.when(jnp.logical_not(stays))
            def _():
                near_copy(shard, place, base).wait_send()


def leave_kernel(cuts, paired, stacks, *refs):
    count = len(cuts)
    ringed = [index for index in range(count) if not paired[index]]
    partial, resid, gains, given = refs[0], refs[1], refs[2], refs[3 : 3 + len(stacks)]
    totals = []
    for ref, stack in zip(given, stacks):
        totals += [ref] if stack == 1 else [ref.at[k] for k in range(stack)]
    taken = 3 + len(stacks)
    outs = refs[taken : taken + 2 + sum(len(cut) for cut in cuts)]
    rows_out, gains_out, shard_outs = outs[0], outs[1], outs[2:]
    scratch = refs[taken + len(outs) :]
    peer_far, peer_near, far_sum, from_far, done_rows = scratch[:5]
    boxes, taken = [], 5
    for alone in paired:
        boxes.append(scratch[taken : taken + (1 if alone else 8)])
        taken += 1 if alone else 8
    gain_box, send, recv, local = scratch[-4:]
    a, b, core = lax.axis_index("a"), lax.axis_index("b"), lax.axis_index("core")
    th, tl = lax.axis_index("th"), lax.axis_index("tl")
    stays = core == th
    to_a, to_b, to_core, to_tl = {"a": 1 - a}, {"b": 1 - b}, {"core": 1 - core}, {"tl": 1 - tl}
    greet()

    def remote(source, target, slot, to, send_slot=None):
        return pltpu.make_async_remote_copy(
            src_ref=source,
            dst_ref=target,
            send_sem=send.at[slot if send_slot is None else send_slot],
            recv_sem=recv.at[slot],
            device_id=to,
            device_id_type=MESH,
        )

    def arrived(target, slot):
        remote(target, target, slot, to_core).wait_recv()

    def add(target, target_row, height, *sources):
        step = 16

        def one(index, unused):
            value = None
            for source, first in sources:
                here = pl.ds(pl.multiple_of(first + index * step, step), step)
                term = source[here, :].astype(jnp.float32)
                value = term if value is None else value + term
            there = pl.ds(pl.multiple_of(target_row + index * step, step), step)
            target[there, :] = value.astype(target.dtype)
            return unused

        lax.fori_loop(0, height // step, one, 0)

    rows = resid.shape[0]
    step = rows // CHUNKS

    own, peer, far, peer_of_far = range(4)

    size = rows // PARTS

    def row_of(block, chunk):
        place = chunk * step
        return (place // size) * 4 * size + block * size + place % size

    def at(ref, row):
        return ref.at[pl.ds(row, step), :]

    def row_copies(chunk):
        here = chunk * step
        return (
            remote(at(partial, row_of(peer_of_far, chunk)), at(peer_far, here), 4 * chunk, to_core),
            remote(at(partial, row_of(peer, chunk)), at(peer_near, here), 4 * chunk + 1, to_core),
            remote(at(far_sum, here), at(from_far, here), 4 * chunk + 2, to_tl),
            remote(at(done_rows, here), at(rows_out, here), 4 * chunk + 3, {"core": th, "th": core}),
        )

    def kept_rows(chunk):
        here = chunk * step
        return pltpu.make_async_copy(at(done_rows, here), at(rows_out, here), local.at[chunk])

    base = 4 * CHUNKS

    def piece(ref, block_a, block_b, sub):
        height = ref.shape[0] // 8
        return pl.multiple_of((4 * block_a + 2 * block_b + sub) * height, height), height

    def slice_of(ref, block_a, block_b, sub):
        row, height = piece(ref, block_a, block_b, sub)
        return ref.at[pl.ds(row, height), :]

    def copies(index):
        total = totals[index]
        _, over_a, over_b, send_b, send_a, from_b, from_a, _ = boxes[index]
        slot = base + 10 * index
        height = total.shape[0] // 8

        def half(ref, sub):
            return ref.at[pl.ds(sub * height, height), :]

        return (
            remote(slice_of(total, 1 - a, 1 - b, 0), over_a, slot, to_a),
            remote(slice_of(total, 1 - a, 1 - b, 1), over_b, slot + 1, to_b),
            remote(slice_of(total, a, 1 - b, 1), half(from_b, 1), slot + 2, to_b),
            remote(slice_of(total, 1 - a, b, 0), half(from_a, 0), slot + 3, to_a),
            remote(send_b, half(from_b, 0), slot + 4, to_b),
            remote(send_a, half(from_a, 1), slot + 5, to_a),
        )

    def own_sum(index, sub):
        sums = totals[index] if paired[index] else boxes[index][7]
        height = sums.shape[0] // 2
        return sums.at[pl.ds(pl.multiple_of(sub * height, height), height), :]

    def last_copies(index):
        inbox = boxes[index][0]
        slot = base + 10 * index + 6
        return (
            remote(own_sum(index, 1 - core), inbox.at[0], slot, to_core),
            remote(own_sum(index, 0), inbox.at[1], slot + 1, {"core": 0, "th": core}),
            remote(own_sum(index, 1), inbox.at[1], slot + 1, {"core": 1, "th": core}, slot + 2),
        )

    def start_last(index):
        @pl.when(stays)
        def _():
            last_copies(index)[0].start()

        @pl.when(jnp.logical_not(stays))
        def _():
            last_copies(index)[1].start()
            last_copies(index)[2].start()

    gain_axes = ({"core": 1 - core}, {"tl": 1 - tl}, {"b": 1 - b}, {"a": 1 - a}, {"th": 1 - th})

    def gain_copy(turn_index):
        source = gains if turn_index == 0 else gain_box.at[4 + turn_index]
        return remote(
            source,
            gain_box.at[turn_index],
            base + 10 * count + turn_index,
            gain_axes[turn_index],
        )

    def gain_step(turn_index):
        arrived(gain_box.at[turn_index], base + 10 * count + turn_index)
        mine = gains[...] if turn_index == 0 else gain_box[4 + turn_index]
        total = mine + gain_box[turn_index]
        if turn_index == 4:
            gains_out[...] = total
        else:
            gain_box[5 + turn_index] = total
            gain_copy(turn_index + 1).start()

    def start_ring(index):
        for copy in copies(index)[:4]:
            copy.start()

    def turn_ring(index):
        total = totals[index]
        _, over_a, over_b, send_b, send_a, _, _, _ = boxes[index]
        height = total.shape[0] // 8
        arrived(over_a, base + 10 * index)
        add(send_b, 0, height, (total, piece(total, a, 1 - b, 0)[0]), (over_a, 0))
        copies(index)[4].start()
        arrived(over_b, base + 10 * index + 1)
        add(send_a, 0, height, (total, piece(total, 1 - a, b, 1)[0]), (over_b, 0))
        copies(index)[5].start()

    def finish_ring(index):
        total = totals[index]
        _, _, _, _, _, from_b, from_a, sums = boxes[index]
        height = total.shape[0] // 8
        slot = base + 10 * index
        for sub in (0, 1):
            arrived(from_b.at[pl.ds(sub * height, height), :], slot + (4 if sub == 0 else 2))
            arrived(from_a.at[pl.ds(sub * height, height), :], slot + (3 if sub == 0 else 5))
            add(
                sums,
                sub * height,
                height,
                (total, piece(total, a, b, sub)[0]),
                (from_b, sub * height),
                (from_a, sub * height),
            )
        start_last(index)

    def finish_chunk(chunk):
        here = chunk * step
        arrived(at(peer_near, here), 4 * chunk + 1)
        arrived(at(from_far, here), 4 * chunk + 2)
        add(
            done_rows,
            here,
            step,
            (partial, row_of(own, chunk)),
            (peer_near, here),
            (from_far, here),
            (resid, here),
        )

        @pl.when(stays)
        def _():
            kept_rows(chunk).start()

        @pl.when(jnp.logical_not(stays))
        def _():
            row_copies(chunk)[3].start()

    for chunk in range(CHUNKS):
        row_copies(chunk)[0].start()
    for chunk in range(CHUNKS):
        row_copies(chunk)[1].start()
    for index in range(count):
        if paired[index]:
            start_last(index)
    for chunk in range(CHUNKS):
        arrived(at(peer_far, chunk * step), 4 * chunk)
        add(
            far_sum,
            chunk * step,
            step,
            (partial, row_of(far, chunk)),
            (peer_far, chunk * step),
        )
        row_copies(chunk)[2].start()
    for index in ringed:
        start_ring(index)
    gain_copy(0).start()
    gain_step(0)
    for place in range(max(len(ringed), CHUNKS)):
        if place < len(ringed):
            turn_ring(ringed[place])
        if place < CHUNKS:
            finish_chunk(place)
    for step_index in (1, 2, 3):
        gain_step(step_index)
    for index in ringed:
        finish_ring(index)
    gain_step(4)
    for index, cut in sorted(enumerate(cuts), key=lambda pair: not paired[pair[0]]):
        inbox = boxes[index][0]
        sums = totals[index] if paired[index] else boxes[index][-1]
        height = inbox.shape[1]
        slot = base + 10 * index + 6
        taken = sum(len(other) for other in cuts[:index])
        arrived(inbox.at[1], slot + 1)

        @pl.when(jnp.logical_not(stays))
        def _():
            arrived(inbox.at[0], slot)

        def one(step_index, unused, cut=cut, taken=taken, sums=sums, inbox=inbox, height=height):
            row = pl.multiple_of(step_index * 16, 16)
            here = pl.ds(row, 16)
            other = inbox[1, here, :].astype(jnp.float32)

            def store(value):
                first = 0
                for offset, end in enumerate(cut):
                    shard_outs[taken + offset][here, :] = (value + other)[:, first:end]
                    first = end

            @pl.when(stays)
            def _():
                own_row = pl.multiple_of(core * height + row, 16)
                store(sums[pl.ds(own_row, 16), :].astype(jnp.float32))

            @pl.when(jnp.logical_not(stays))
            def _():
                store(inbox[0, here, :].astype(jnp.float32))

            return unused

        lax.fori_loop(0, height // 16, one, 0)
    for chunk in range(CHUNKS):
        for copy in row_copies(chunk)[:3]:
            copy.wait_send()

        @pl.when(stays)
        def _():
            kept_rows(chunk).wait()

        @pl.when(jnp.logical_not(stays))
        def _():
            row_copies(chunk)[3].wait_send()
            arrived(at(rows_out, chunk * step), 4 * chunk + 3)

    for turn_index in range(5):
        gain_copy(turn_index).wait_send()
    for index in ringed:
        for copy in copies(index):
            copy.wait_send()
    for index in range(count):

        @pl.when(stays)
        def _():
            last_copies(index)[0].wait_send()

        @pl.when(jnp.logical_not(stays))
        def _():
            last_copies(index)[1].wait_send()
            last_copies(index)[2].wait_send()


def unstacked(totals):
    flat = []
    for total, parts, alone in totals:
        for matrix in [total] if total.ndim == 2 else [total[k] for k in range(total.shape[0])]:
            flat.append((matrix, parts, alone))
    return flat


def leave(partial, resid, gains, totals):
    if not small_grid():
        summed = finish_scatter_rows(start_scatter([partial.astype(jnp.bfloat16)]), None)
        shards = []
        for total, parts, alone in unstacked(totals):
            shard, first = finish_split(*start_split(total if alone else scatter_pair(total))), 0
            for width in parts:
                shards.append(shard[:, first : first + width])
                first += width
        total_gains = sum_over(gains, DP + TENSOR)
        return [turn((resid + summed).astype(jnp.bfloat16)), total_gains] + shards
    rows, columns = resid.shape
    cuts, scratch = [], []
    outs = [
        jax.ShapeDtypeStruct((rows, columns), jnp.bfloat16),
        jax.ShapeDtypeStruct(gains.shape, jnp.float32),
    ]
    stacks = tuple(1 if total.ndim == 2 else total.shape[0] for total, _, _ in totals)
    arrays = [total.astype(jnp.bfloat16) for total, _, _ in totals]
    for total, parts, alone in unstacked(totals):
        height, width = total.shape[0] // (2 if alone else 8), total.shape[1]
        cuts.append(tuple(sum(parts[: index + 1]) for index in range(len(parts))))
        outs += [jax.ShapeDtypeStruct((height, part_width), jnp.float32) for part_width in parts]
        shapes = [(2, height, width)]
        if not alone:
            shapes += [(height, width)] * 4 + [(2 * height, width)] * 3
        scratch += [pltpu.VMEM(shape, jnp.bfloat16) for shape in shapes]
    paired = tuple(alone for _, _, alone in unstacked(totals))
    slots = 4 * CHUNKS + 10 * len(paired) + 5
    vmem = pl.BlockSpec(memory_space=pltpu.VMEM)
    return pl.pallas_call(
        functools.partial(leave_kernel, tuple(cuts), paired, stacks),
        in_specs=[vmem] * (3 + len(totals)),
        out_specs=[pl.BlockSpec(memory_space=pl.ANY)] + [vmem] * (len(outs) - 1),
        out_shape=outs,
        scratch_shapes=[pltpu.VMEM((rows, columns), jnp.bfloat16)] * 5
        + scratch
        + [
            pltpu.VMEM((9, *gains.shape), jnp.float32),
            pltpu.SemaphoreType.DMA((slots,)),
            pltpu.SemaphoreType.DMA((slots,)),
            pltpu.SemaphoreType.DMA((CHUNKS,)),
        ],
        compiler_params=pltpu.CompilerParams(
            collective_id=1, has_side_effects=True, vmem_limit_bytes=60 * 1024 * 1024
        ),
        cost_estimate=BESIDE,
        name="leave",
    )(partial.astype(jnp.bfloat16), resid, gains, *arrays)


def enter(tokens, matrices):
    if not small_grid():
        own = turn(tokens)
        pairs = [
            (pair_of_weight(jnp.concatenate(shards, axis=1)), whole) for shards, whole in matrices
        ]
        return [lax.all_gather(own, RANK, axis=0, tiled=True)] + [
            gather_weight(pair) if whole else pair for pair, whole in pairs
        ]
    plan, outs = [], [jax.ShapeDtypeStruct((4 * tokens.shape[0], tokens.shape[1]), tokens.dtype)]
    for shards, whole in matrices:
        columns = [0]
        for shard in shards:
            columns.append(columns[-1] + shard.shape[1])
        plan.append((tuple(columns[:-1]), whole))
        height = (8 if whole else 2) * shards[0].shape[0]
        outs.append(jax.ShapeDtypeStruct((height, columns[-1]), tokens.dtype))
    flat = [shard for shards, _ in matrices for shard in shards]
    slots = entry_slots(plan)
    anywhere = pl.BlockSpec(memory_space=pl.ANY)
    return pl.pallas_call(
        functools.partial(entry_kernel, tuple(plan)),
        in_specs=[anywhere] * (1 + len(flat)),
        out_specs=[anywhere] * len(outs),
        out_shape=outs,
        scratch_shapes=[
            pltpu.SemaphoreType.DMA((slots,)),
            pltpu.SemaphoreType.DMA((slots,)),
            pltpu.SemaphoreType.DMA((len(flat) + CHUNKS,)),
        ],
        compiler_params=pltpu.CompilerParams(collective_id=0, has_side_effects=True),
        cost_estimate=BESIDE,
        name="enter",
    )(tokens, *flat)


def row_place(row, own_rows):
    if not small_grid():
        return row
    mask = 2 * lax.axis_index("core") + lax.axis_index("tl")
    block = (row // own_rows) ^ mask
    block = (block // 2) + 2 * (block % 2)
    size = own_rows // PARTS
    place = row % own_rows
    return (place // size) * 4 * size + block * size + place % size


def after(token, value):
    return value if token is None else lax.optimization_barrier((value, token))[0]


def start_gather(value):
    if not small_grid():
        return lax.all_gather(value, RANK, axis=0, tiled=True), None
    return jnp.concatenate([value, swap(value, "core")], axis=0), swap(value, "tl")


def forward_rows(rows, token):
    far = after(token, rows[1])
    return jnp.concatenate([far, swap(far, "core")], axis=0)


def start_scatter(pieces):
    if not small_grid():
        return (lax.psum_scatter(pieces[0], RANK, scatter_dimension=0, tiled=True),)
    near, far = pieces
    rows = near.shape[0] // 2
    far_peer = swap(far[rows:], "core")
    far_sum = (far[:rows].astype(jnp.float32) + far_peer.astype(jnp.float32)).astype(jnp.bfloat16)
    return near[:rows], swap(near[rows:], "core"), swap(far_sum, "tl")


def finish_scatter_rows(terms, token):
    terms = [*terms[:-1], after(token, terms[-1])]
    return sum(term.astype(jnp.float32) for term in terms)


def sum_over(value, axes):
    for axis in axes:
        if lax.axis_size(axis) == 2:
            value = value + swap(value, axis)
        else:
            value = lax.psum(value, axis)
    return value


def layout(length_row, group_rows):
    positions = jnp.arange(group_rows, dtype=jnp.int32)
    start = jnp.int32(0)
    offset = jnp.zeros((group_rows,), jnp.int32)
    starts = positions
    for index in range(length_row.shape[0]):
        end = start + length_row[index]
        inside = (positions >= start) & (positions < end)
        offset = jnp.where(inside, start, offset)
        starts = jnp.where(inside, start, starts)
        start = end
    return (positions - offset, starts)


def rotary_tables(position):
    half_dim = HDIM // 2
    exponents = jnp.arange(half_dim, dtype=jnp.float32) * (2.0 / HDIM)
    frequency = jnp.power(jnp.float32(rope_base), -exponents)
    angles = position.astype(jnp.float32)[:, None] * frequency[None, :]
    cosine, sine = jnp.cos(angles), jnp.sin(angles)
    return (
        jnp.concatenate([cosine, cosine], axis=1),
        jnp.concatenate([-sine, sine], axis=1),
    )


def columns_of(rows, index):
    chosen = (lax.broadcasted_iota(jnp.int32, (rows.shape[0], HDIM), 0) == index).astype(
        jnp.float32
    )
    return lax.dot_general(
        rows,
        chosen,
        (((0,), (0,)), ((), ())),
        precision=lax.Precision.HIGHEST,
        preferred_element_type=jnp.float32,
    )


def row_sums(values):
    ones = jnp.ones((8, HDIM), jnp.float32)
    folded = sum(
        values[:, first : first + HDIM] for first in range(0, values.shape[1], HDIM)
    )
    return lax.dot_general(
        ones,
        folded,
        (((1,), (1,)), ((), ())),
        precision=lax.Precision.HIGHEST,
        preferred_element_type=jnp.float32,
    )[:1]


def rstd_of(squares, index):
    return lax.rsqrt(columns_of(squares, index) * (1.0 / D) + epsilon)


def prepare_kernel(raw, squares, gain_q, gain_k, cosine, sine, q_out, k_out, v_out):
    width = q_out.shape[1]
    table_c, table_s = cosine[...], sine[...]
    both = squares[...]
    for index, (gain, out) in enumerate(((gain_q, q_out), (gain_k, k_out))):
        rstd = rstd_of(both, index)
        for head in range(width // HDIM):
            cols = slice(head * HDIM, (head + 1) * HDIM)
            base = index * width + head * HDIM
            norm = raw[:, base : base + HDIM] * rstd * gain[:, cols]
            turned = norm * table_c + pltpu.roll(norm, HDIM // 2, 1) * table_s
            out[:, cols] = turned.astype(jnp.bfloat16)
    v_out[...] = raw[:, 2 * width :].astype(jnp.bfloat16)


def prepare(raw, squares, gain_q, gain_k, cosine, sine):
    rows, width = raw.shape[0], raw.shape[1] // 3
    whole = pl.BlockSpec((1, width), lambda i: (0, 0))
    table = pl.BlockSpec((BLOCK, HDIM), lambda i: (i, 0))
    out = pl.BlockSpec((BLOCK, width), lambda i: (i, 0))
    return pl.pallas_call(
        prepare_kernel,
        grid=(rows // BLOCK,),
        in_specs=[
            pl.BlockSpec((BLOCK, 3 * width), lambda i: (i, 0)),
            pl.BlockSpec((2, BLOCK), lambda i: (0, i)),
            whole,
            whole,
            table,
            table,
        ],
        out_specs=[out] * 3,
        out_shape=[jax.ShapeDtypeStruct((rows, width), jnp.bfloat16)] * 3,
        cost_estimate=BESIDE,
        name="prepare",
    )(raw, squares, gain_q[None], gain_k[None], cosine, sine)


def allowed_keys(starts, first_key, first_query):
    shape = (BLOCK, BLOCK)
    keys = first_key + lax.broadcasted_iota(jnp.int32, shape, 0)
    queries = first_query + lax.broadcasted_iota(jnp.int32, shape, 1)
    return (keys >= starts) & (keys <= queries)


def head_columns(head):
    return slice(head * HDIM, (head + 1) * HDIM)


def forward_kernel(low_ref, q_ref, k_ref, v_ref, start_ref, attn_ref, full_ref, log_ref):
    block = pl.program_id(0)
    heads = q_ref.shape[1] // HDIM
    starts = start_ref[...]
    scale = 1.0 / math.sqrt(HDIM)

    def step(index, carried):
        rows = pl.ds(pl.multiple_of(index * BLOCK, BLOCK), BLOCK)
        allowed = allowed_keys(starts, index * BLOCK, block * BLOCK)
        after_step = []
        for head, (peak, total, acc) in enumerate(carried):
            cols = head_columns(head)
            scores = contract_cols(k_ref[rows, cols], q_ref[:, cols]) * scale
            scores = jnp.where(allowed, scores, masked_score)
            new_peak = jnp.maximum(peak, jnp.max(scores, axis=0, keepdims=True))
            fade = jnp.exp(peak - new_peak)
            weights = jnp.exp(scores - new_peak)
            total = total * fade + jnp.sum(weights, axis=0, keepdims=True)
            acc = acc * fade + contract_rows(v_ref[rows, cols], weights.astype(jnp.bfloat16))
            after_step.append((new_peak, total, acc))
        return tuple(after_step)

    start = (
        jnp.full((1, BLOCK), masked_score, jnp.float32),
        jnp.zeros((1, BLOCK), jnp.float32),
        jnp.zeros((HDIM, BLOCK), jnp.float32),
    )
    carried = step(block, (start,) * heads)
    carried = lax.fori_loop(low_ref[block], block, step, carried)
    for head, (peak, total, acc) in enumerate(carried):
        out = jnp.transpose(acc / total)
        full_ref[:, head_columns(head)] = out
        attn_ref[:, head_columns(head)] = out.astype(jnp.bfloat16)
        log_ref[head] = peak + jnp.log(total)


def attention_forward(q_b, k_b, v_b, starts, low_block):
    rows, width = q_b.shape
    heads = width // HDIM
    own = pl.BlockSpec((BLOCK, width), lambda i, low: (i, 0))
    whole = pl.BlockSpec((rows, width), lambda i, low: (0, 0))
    return pl.pallas_call(
        forward_kernel,
        grid_spec=pltpu.PrefetchScalarGridSpec(
            num_scalar_prefetch=1,
            grid=(rows // BLOCK,),
            in_specs=[own, whole, whole, pl.BlockSpec((1, BLOCK), lambda i, low: (0, i))],
            out_specs=[own, own, pl.BlockSpec((heads, 1, BLOCK), lambda i, low: (0, 0, i))],
        ),
        out_shape=[
            jax.ShapeDtypeStruct((rows, width), jnp.bfloat16),
            jax.ShapeDtypeStruct((rows, width), jnp.float32),
            jax.ShapeDtypeStruct((heads, 1, rows), jnp.float32),
        ],
        compiler_params=pltpu.CompilerParams(vmem_limit_bytes=VMEM_BYTES),
        cost_estimate=BESIDE,
        name="attention_forward",
    )(low_block, q_b, k_b, v_b, starts)


def backward_kernel(
    high_ref, q_ref, k_ref, v_ref, grad_ref, full_ref, log_ref, start_ref, dq_ref, dk_ref, dv_ref, delta
):
    block = pl.program_id(0)
    blocks = pl.num_programs(0)
    heads = q_ref.shape[1] // HDIM
    scale = 1.0 / math.sqrt(HDIM)

    @pl.when(block == 0)
    def _():
        dq_ref[...] = jnp.zeros_like(dq_ref)

        def one(index, unused):
            rows = pl.ds(pl.multiple_of(index * BLOCK, BLOCK), BLOCK)
            for head in range(heads):
                cols = head_columns(head)
                delta[head, :, rows] = row_sums(
                    grad_ref[rows, cols].astype(jnp.float32) * full_ref[rows, cols]
                )
            return unused

        lax.fori_loop(0, blocks, one, 0)

    here = pl.ds(pl.multiple_of(block * BLOCK, BLOCK), BLOCK)

    def step(index, carried):
        rows = pl.ds(pl.multiple_of(index * BLOCK, BLOCK), BLOCK)
        allowed = allowed_keys(start_ref[:, rows], block * BLOCK, index * BLOCK)
        after_step = []
        for head, (dk, dv) in enumerate(carried):
            cols = head_columns(head)
            keys, values = k_ref[here, cols], v_ref[here, cols]
            queries, grads = q_ref[rows, cols], grad_ref[rows, cols]
            scores = contract_cols(keys, queries) * scale
            probs = jnp.where(allowed, jnp.exp(scores - log_ref[head, :, rows]), 0.0)
            dv = dv + dot(probs.astype(jnp.bfloat16), grads)
            d_probs = contract_cols(values, grads)
            d_scores = (probs * (d_probs - delta[head, :, rows])).astype(jnp.bfloat16)
            dk = dk + dot(d_scores, queries)
            dq_ref[rows, cols] += contract_rows(d_scores, keys)
            after_step.append((dk, dv))
        return tuple(after_step)

    zero = jnp.zeros((BLOCK, HDIM), jnp.float32)
    carried = lax.fori_loop(block, high_ref[block] + 1, step, ((zero, zero),) * heads)
    for head, (dk, dv) in enumerate(carried):
        dk_ref[:, head_columns(head)] = dk * scale
        dv_ref[:, head_columns(head)] = dv.astype(jnp.bfloat16)

    @pl.when(block == blocks - 1)
    def _():
        dq_ref[...] = dq_ref[...] * scale


def attention_backward(q_b, k_b, v_b, grads, full, logs, starts, high_block):
    rows, width = q_b.shape
    heads = width // HDIM
    own = pl.BlockSpec((BLOCK, width), lambda i, high: (i, 0))
    whole = pl.BlockSpec((rows, width), lambda i, high: (0, 0))
    out = jax.ShapeDtypeStruct((rows, width), jnp.float32)
    return pl.pallas_call(
        backward_kernel,
        grid_spec=pltpu.PrefetchScalarGridSpec(
            num_scalar_prefetch=1,
            grid=(rows // BLOCK,),
            in_specs=[whole] * 5
            + [
                pl.BlockSpec((heads, 1, rows), lambda i, high: (0, 0, 0)),
                pl.BlockSpec((1, rows), lambda i, high: (0, 0)),
            ],
            out_specs=[whole, own, own],
            scratch_shapes=[pltpu.VMEM((heads, 1, rows), jnp.float32)],
        ),
        out_shape=[out, out, jax.ShapeDtypeStruct((rows, width), jnp.bfloat16)],
        compiler_params=pltpu.CompilerParams(vmem_limit_bytes=VMEM_BYTES),
        cost_estimate=BESIDE,
        name="attention_backward",
    )(high_block, q_b, k_b, v_b, grads, full, logs, starts)


def norm_grads_kernel(
    dq_ref, dk_ref, raw, squares, gain_q, gain_k, cosine, sine, dq_out, dk_out, dots, q_part, k_part
):
    width = dq_ref.shape[1]
    table_c, table_s = cosine[...], sine[...]
    both = squares[...]

    @pl.when(pl.program_id(0) == 0)
    def _():
        q_part[...] = jnp.zeros_like(q_part)
        k_part[...] = jnp.zeros_like(k_part)

    for index, (grad, gain, out, gain_part) in enumerate(
        ((dq_ref, gain_q, dq_out, q_part), (dk_ref, gain_k, dk_out, k_part))
    ):
        rstd = rstd_of(both, index)
        products = jnp.zeros((BLOCK, HDIM), jnp.float32)
        for head in range(width // HDIM):
            cols = slice(head * HDIM, (head + 1) * HDIM)
            base = index * width + head * HDIM
            turned = grad[:, cols]
            norm = turned * table_c - pltpu.roll(turned, HDIM // 2, 1) * table_s
            out[:, cols] = norm
            product = raw[:, base : base + HDIM] * norm
            gain_part[:, cols] += jnp.sum((product * rstd).reshape(BLOCK // 8, 8, HDIM), axis=0)
            products = products + product * gain[:, cols]
        dots[index : index + 1, :] = row_sums(products)


def norm_grads(d_q_rot, d_k_rot, raw, squares, gain_q, gain_k, cosine, sine):
    rows, width = d_q_rot.shape
    whole = pl.BlockSpec((1, width), lambda i: (0, 0))
    table = pl.BlockSpec((BLOCK, HDIM), lambda i: (i, 0))
    own = pl.BlockSpec((BLOCK, width), lambda i: (i, 0))
    pair = pl.BlockSpec((2, BLOCK), lambda i: (0, i))
    total = pl.BlockSpec((8, width), lambda i: (0, 0))
    grad = jax.ShapeDtypeStruct((rows, width), jnp.float32)
    return pl.pallas_call(
        norm_grads_kernel,
        grid=(rows // BLOCK,),
        in_specs=[
            own,
            own,
            pl.BlockSpec((BLOCK, 2 * width), lambda i: (i, 0)),
            pair,
            whole,
            whole,
            table,
            table,
        ],
        out_specs=[own, own, pair, total, total],
        out_shape=[
            grad,
            grad,
            jax.ShapeDtypeStruct((2, rows), jnp.float32),
            jax.ShapeDtypeStruct((8, width), jnp.float32),
            jax.ShapeDtypeStruct((8, width), jnp.float32),
        ],
        cost_estimate=BESIDE,
        name="norm_grads",
    )(d_q_rot, d_k_rot, raw, squares, gain_q[None], gain_k[None], cosine, sine)


def raw_grads_kernel(dq_ref, dk_ref, dv_ref, raw, squares, dots, gain_q, gain_k, out):
    width = dq_ref.shape[1]
    both, sums = squares[...], dots[...]
    for index, (grad, gain) in enumerate(((dq_ref, gain_q), (dk_ref, gain_k))):
        rstd = rstd_of(both, index)
        share = rstd * rstd * rstd * columns_of(sums, index) * (1.0 / D)
        for head in range(width // HDIM):
            cols = slice(head * HDIM, (head + 1) * HDIM)
            base = index * width + head * HDIM
            value = rstd * gain[:, cols] * grad[:, cols] - raw[:, base : base + HDIM] * share
            out[:, base : base + HDIM] = value.astype(jnp.bfloat16)
    out[:, 2 * width :] = dv_ref[...]


def raw_grads(d_q_norm, d_k_norm, d_v, raw, squares, dots, gain_q, gain_k):
    rows, width = d_q_norm.shape
    whole = pl.BlockSpec((1, width), lambda i: (0, 0))
    own = pl.BlockSpec((BLOCK, width), lambda i: (i, 0))
    wide = pl.BlockSpec((BLOCK, 3 * width), lambda i: (i, 0))
    pair = pl.BlockSpec((2, BLOCK), lambda i: (0, i))
    return pl.pallas_call(
        raw_grads_kernel,
        grid=(rows // BLOCK,),
        in_specs=[
            own,
            own,
            own,
            pl.BlockSpec((BLOCK, 2 * width), lambda i: (i, 0)),
            pair,
            pair,
            whole,
            whole,
        ],
        out_specs=wide,
        out_shape=jax.ShapeDtypeStruct((rows, 3 * width), jnp.bfloat16),
        cost_estimate=BESIDE,
        name="raw_grads",
    )(d_q_norm, d_k_norm, d_v, raw, squares, dots, gain_q[None], gain_k[None])


def dot(left, right):
    return jnp.dot(left, right, preferred_element_type=jnp.float32)


def contract_rows(left, right):
    return lax.dot_general(
        left, right, (((0,), (0,)), ((), ())), preferred_element_type=jnp.float32
    )


def contract_cols(left, right):
    return lax.dot_general(
        left, right, (((1,), (1,)), ((), ())), preferred_element_type=jnp.float32
    )


def column_block(rows, width):
    return min(width, 512 if rows <= 1024 else 256)


def matmul_params():
    return pltpu.CompilerParams(vmem_limit_bytes=56 * 1024 * 1024)


def hidden_kernel(x_ref, gate_w, up_w, gate_out, up_out, hidden_out):
    gate = dot(x_ref[...], gate_w[...])
    up_part = dot(x_ref[...], up_w[...])
    gate_out[...] = gate
    up_out[...] = up_part
    hidden_out[...] = (gate * jax.nn.sigmoid(gate) * up_part).astype(jnp.bfloat16)


def hidden_units(x, gate_full, up_full):
    rows, depth = x.shape
    width = gate_full.shape[1]
    block = column_block(rows, width)
    weight = pl.BlockSpec((depth, block), lambda j: (0, j))
    out = pl.BlockSpec((rows, block), lambda j: (0, j))
    return pl.pallas_call(
        hidden_kernel,
        grid=(width // block,),
        in_specs=[pl.BlockSpec((rows, depth), lambda j: (0, 0)), weight, weight],
        out_specs=[out] * 3,
        out_shape=[
            jax.ShapeDtypeStruct((rows, width), jnp.float32),
            jax.ShapeDtypeStruct((rows, width), jnp.float32),
            jax.ShapeDtypeStruct((rows, width), jnp.bfloat16),
        ],
        compiler_params=matmul_params(),
        cost_estimate=BESIDE,
        name="hidden_units",
    )(x, gate_full, up_full)


def hidden_grads_kernel(grad_ref, weight, gate_ref, up_ref, gate_out, up_out):
    d_hidden = dot(grad_ref[...], weight[...])
    gate = gate_ref[...]
    gate_sigmoid = jax.nn.sigmoid(gate)
    silu = gate * gate_sigmoid
    gate_out[...] = (
        d_hidden * up_ref[...] * (gate_sigmoid * (1.0 + gate * (1.0 - gate_sigmoid)))
    ).astype(jnp.bfloat16)
    up_out[...] = (d_hidden * silu).astype(jnp.bfloat16)


def hidden_grads(grad, down_full, gate, up_part):
    rows, depth = grad.shape
    width = down_full.shape[1]
    block = column_block(rows, width)
    part_spec = pl.BlockSpec((rows, block), lambda j: (0, j))
    out = jax.ShapeDtypeStruct((rows, width), jnp.bfloat16)
    return pl.pallas_call(
        hidden_grads_kernel,
        grid=(width // block,),
        in_specs=[
            pl.BlockSpec((rows, depth), lambda j: (0, 0)),
            pl.BlockSpec((depth, block), lambda j: (0, j)),
            part_spec,
            part_spec,
        ],
        out_specs=[part_spec] * 2,
        out_shape=[out] * 2,
        compiler_params=matmul_params(),
        cost_estimate=BESIDE,
        name="hidden_grads",
    )(grad, down_full, gate, up_part)


def products_kernel(count, *refs):
    total = None
    for left, right in zip(refs[:count], refs[count : 2 * count]):
        term = contract_cols(left[...], right[...])
        total = term if total is None else total + term
    refs[-1][...] = total.astype(jnp.bfloat16)


def sum_products(lefts, rights):
    rows, depth = lefts[0].shape
    width = rights[0].shape[0]
    block = column_block(rows, width)
    return pl.pallas_call(
        functools.partial(products_kernel, len(lefts)),
        grid=(width // block,),
        in_specs=[pl.BlockSpec((rows, depth), lambda j: (0, 0)) for _ in lefts]
        + [pl.BlockSpec((block, depth), lambda j: (j, 0)) for _ in rights],
        out_specs=pl.BlockSpec((rows, block), lambda j: (0, j)),
        out_shape=jax.ShapeDtypeStruct((rows, width), jnp.bfloat16),
        compiler_params=matmul_params(),
        cost_estimate=BESIDE,
        name="sum_products",
    )(*lefts, *rights)


def weight_grad_kernel(count, *refs):
    total = None
    for left, right in zip(refs[:count], refs[count : 2 * count]):
        term = contract_rows(left[...], right[...])
        total = term if total is None else total + term
    refs[-1][...] = total.astype(jnp.bfloat16)


def weight_grad(lefts, rights):
    heights = [left.shape[0] for left in lefts]
    if len(rights) == 1 < len(lefts):
        rights, places = rights * len(lefts), list(range(len(lefts)))
    else:
        places = [0] * len(lefts)
    height, width = lefts[0].shape[1], rights[0].shape[1]
    tall, wide = min(height, 512), min(width, 1024)
    return pl.pallas_call(
        functools.partial(weight_grad_kernel, len(lefts)),
        grid=(width // wide, height // tall),
        in_specs=[pl.BlockSpec((rows, tall), lambda j, i: (0, i)) for rows in heights]
        + [
            pl.BlockSpec((rows, wide), functools.partial(lambda place, j, i: (place, j), place))
            for rows, place in zip(heights, places)
        ],
        out_specs=pl.BlockSpec((tall, wide), lambda j, i: (i, j)),
        out_shape=jax.ShapeDtypeStruct((height, width), jnp.bfloat16),
        compiler_params=matmul_params(),
        cost_estimate=BESIDE,
        name="weight_grad",
    )(*lefts, *rights)


def stacked_weight_grad(left, right, count):
    rows, height = left.shape
    width = right.shape[1] // count
    tall = min(height, 512)
    return pl.pallas_call(
        functools.partial(weight_grad_kernel, 1),
        grid=(count, height // tall),
        in_specs=[
            pl.BlockSpec((rows, tall), lambda j, i: (0, i)),
            pl.BlockSpec((rows, width), lambda j, i: (0, j)),
        ],
        out_specs=pl.BlockSpec((None, tall, width), lambda j, i: (j, i, 0)),
        out_shape=jax.ShapeDtypeStruct((count, height, width), jnp.bfloat16),
        compiler_params=matmul_params(),
        cost_estimate=BESIDE,
        name="stacked_weight_grad",
    )(left, right)


def move_rows(places, wanted_first, count, rows_ref):
    wanted = wanted_first + lax.broadcasted_iota(jnp.int32, (count, places.shape[1]), 0)
    chosen = jnp.where(places == wanted, 1.0, 0.0).astype(jnp.bfloat16)
    return dot(chosen, rows_ref[...]).astype(jnp.bfloat16)


def pick_rows(places, rows_ref):
    columns = lax.broadcasted_iota(jnp.int32, (places.shape[0], rows_ref.shape[0]), 1)
    chosen = jnp.where(places == columns, 1.0, 0.0).astype(jnp.bfloat16)
    return dot(chosen, rows_ref[...]).astype(jnp.bfloat16)


def pack_kernel(places, tokens_ref, weight, packed_out, raw_out, squares_out):
    packed = pick_rows(places[...], tokens_ref)
    packed_out[...] = packed
    raw = dot(packed, weight[...])
    raw_out[...] = raw
    width = raw.shape[1] // 3
    for index in range(2):
        cols = raw[:, index * width : (index + 1) * width]
        squares_out[index : index + 1, :] = row_sums(cols * cols)


def pack(perm_row, tokens_all, qkv_full):
    rows, depth = tokens_all.shape
    width = qkv_full.shape[1]
    return pl.pallas_call(
        pack_kernel,
        grid=(rows // BLOCK,),
        in_specs=[
            pl.BlockSpec((BLOCK, 1), lambda i: (i, 0)),
            pl.BlockSpec((rows, depth), lambda i: (0, 0)),
            pl.BlockSpec((depth, width), lambda i: (0, 0)),
        ],
        out_specs=[
            pl.BlockSpec((BLOCK, depth), lambda i: (i, 0)),
            pl.BlockSpec((BLOCK, width), lambda i: (i, 0)),
            pl.BlockSpec((2, BLOCK), lambda i: (0, i)),
        ],
        out_shape=[
            jax.ShapeDtypeStruct((rows, depth), jnp.bfloat16),
            jax.ShapeDtypeStruct((rows, width), jnp.float32),
            jax.ShapeDtypeStruct((2, rows), jnp.float32),
        ],
        compiler_params=matmul_params(),
        cost_estimate=BESIDE,
        name="pack",
    )(perm_row[:, None], tokens_all, qkv_full)


def given_kernel(count, places, rows_ref, weight, moved_out, product_out):
    moved = move_rows(places[...], pl.program_id(0) * count, count, rows_ref)
    moved_out[...] = moved
    product_out[...] = contract_cols(moved, weight[...]).astype(jnp.bfloat16)


def give_back(place_row, value, weight):
    rows, depth = value.shape
    width = weight.shape[0]
    count = 512
    return pl.pallas_call(
        functools.partial(given_kernel, count),
        grid=(rows // count,),
        in_specs=[
            pl.BlockSpec((1, rows), lambda i: (0, 0)),
            pl.BlockSpec((rows, depth), lambda i: (0, 0)),
            pl.BlockSpec((width, depth), lambda i: (0, 0)),
        ],
        out_specs=[
            pl.BlockSpec((count, depth), lambda i: (i, 0)),
            pl.BlockSpec((count, width), lambda i: (i, 0)),
        ],
        out_shape=[
            jax.ShapeDtypeStruct((rows, depth), jnp.bfloat16),
            jax.ShapeDtypeStruct((rows, width), jnp.bfloat16),
        ],
        compiler_params=matmul_params(),
        cost_estimate=BESIDE,
        name="give_back",
    )(place_row[None], value, weight)


def pick_products_kernel(count, *refs):
    places, pieces, weight = refs[0], refs[1 : 1 + count], refs[1 + count]
    out, products = refs[2 + count], refs[3 + count]
    step, first = BLOCK, 0
    for piece in pieces:
        height = piece.shape[0]

        def one(index, unused, piece=piece, first=first):
            here = pl.ds(pl.multiple_of(index * step, step), step)
            there = pl.ds(pl.multiple_of(first + index * step, step), step)
            products[there, :] = dot(piece[here, :], weight[...]).astype(jnp.bfloat16)
            return unused

        lax.fori_loop(0, height // step, one, 0)
        first += height

    def pick_block(index, unused):
        here = pl.ds(pl.multiple_of(index * step, step), step)
        out[here, :] = pick_rows(places[here, :], products)
        return unused

    lax.fori_loop(0, out.shape[0] // step, pick_block, 0)


def pick_products(place_row, pieces, weight):
    rows, width = place_row.shape[0], weight.shape[1]
    vmem = pl.BlockSpec(memory_space=pltpu.VMEM)
    return pl.pallas_call(
        functools.partial(pick_products_kernel, len(pieces)),
        in_specs=[vmem] * (2 + len(pieces)),
        out_specs=vmem,
        out_shape=jax.ShapeDtypeStruct((rows, width), jnp.bfloat16),
        scratch_shapes=[pltpu.VMEM((rows, width), jnp.bfloat16)],
        compiler_params=matmul_params(),
        cost_estimate=BESIDE,
        name="pick_products",
    )(place_row[:, None], *pieces, weight)


def rms_back(values, rstd, gain_vec, grad):
    scaled = grad * gain_vec
    row_dots = jnp.sum(values * scaled, axis=1, keepdims=True)
    return rstd * scaled - values * (rstd * rstd * rstd) * row_dots / D


def per_device(
    tokens,
    upstream,
    lengths,
    permutation,
    w_query,
    w_key,
    w_value,
    w_out,
    w_gate,
    w_up,
    w_down,
    q_gain,
    k_gain,
    attn_gain,
    ffn_gain,
):
    rank = lax.axis_index("core") * lax.axis_size("tl") + lax.axis_index("tl")
    own_rows = tokens.shape[0]
    group_rows = own_rows * 2 * lax.axis_size("tl")
    local_width = w_query.shape[1]

    own_group = lax.axis_index("core") == lax.axis_index("th")
    layout_row = jnp.concatenate([permutation, lengths], axis=1)
    layout_row = jnp.where(own_group, layout_row, swap(layout_row, "core"))[0]
    perm_row, length_row = layout_row[:group_rows], layout_row[group_rows:]

    tokens_all, qkv_full, out_full, gate_pair = enter(
        tokens,
        [((w_query, w_key, w_value), True), ((w_out.T,), True), ((w_gate,), False)],
    )
    gate_full = gather_weight(gate_pair)
    up_shard, tokens_all = lax.optimization_barrier((w_up, tokens_all))
    up_pair = pair_of_weight(up_shard)
    tokens = lax.dynamic_slice_in_dim(tokens_all, rank * own_rows, own_rows)

    perm_place = row_place(perm_row, own_rows)
    position, starts = layout(length_row, group_rows)
    cosine, sine = rotary_tables(position)
    blocks = group_rows // BLOCK
    low_block = starts[::BLOCK] // BLOCK
    last_keys = (jnp.arange(blocks, dtype=jnp.int32) + 1) * BLOCK - 1
    reached = jnp.sum((starts[None, :] <= last_keys[:, None]).astype(jnp.int32), axis=1)
    high_block = (reached - 1) // BLOCK

    packed, raw, squares = pack(perm_row, tokens_all, qkv_full)
    up_pair, raw = lax.optimization_barrier((up_pair, raw))
    up_full = gather_weight(up_pair)
    squares = sum_over(squares, RANK)
    down_shard, squares = lax.optimization_barrier((w_down.T, squares))
    down_pair = pair_of_weight(down_shard)
    gain_q = lax.dynamic_slice_in_dim(q_gain, rank * local_width, local_width)
    gain_k = lax.dynamic_slice_in_dim(k_gain, rank * local_width, local_width)
    q_b, k_b, v_b = prepare(raw, squares, gain_q, gain_k, cosine, sine)
    attn_b, attn_f, logs = attention_forward(q_b, k_b, v_b, starts[None], low_block)

    parts = PARTS if small_grid() else 1
    part_rows = own_rows // parts

    def part_of(value, index):
        return part(value, 0, index, parts)

    def pieces_of(value, index):
        whole = part_of(value, index)
        return [part(whole, 0, 0, 2), part(whole, 0, 1, 2)] if small_grid() else [whole]

    sides = 2 if small_grid() else 1
    attn_given, attn_parts = give_back(perm_place, attn_b, out_full)
    down_pair, attn_parts = lax.optimization_barrier((down_pair, attn_parts))
    down_full = gather_weight(down_pair)
    order = [(side, index) for side in range(sides) for index in range(parts)]
    token = None

    def pass_through(make_rows, begin, finish, late, between=None):
        nonlocal token
        gathered, far_pieces, begun, sums, scattered = {}, {}, {}, {}, []

        def complete(side, index):
            nonlocal token
            sums[side, index] = finish(*begun[side, index], token)
            if scattered and sides == 2 and not late:
                *others, last = scattered[-1]
                sums[side, index], last = lax.optimization_barrier((sums[side, index], last))
                scattered[-1] = (*others, last)
            token = sums[side, index]

        def scatter(index):
            scattered.append(start_scatter([sums[side, index] for side in range(sides)]))

        for side, index in order:
            if side == 0:
                gathered[index] = start_gather(make_rows(index, token))
                if sides == 2 and index > 0 and not late:
                    far_pieces[index - 1] = forward_rows(gathered[index - 1], token)
                piece = gathered[index][0]
            else:
                if late:
                    far_pieces[index] = forward_rows(gathered[index], token)
                elif index == 0:
                    far_pieces[parts - 1] = forward_rows(gathered[parts - 1], token)
                    if between is not None:
                        near = [gathered[each][0] for each in range(parts)]
                        token = between(near, [far_pieces[each] for each in range(parts)], token)
                piece = far_pieces[index]
            begun[side, index] = begin((index, side), piece, token)
            token = begun[side, index][0]
            if not late:
                complete(side, index)
                if side == sides - 1:
                    scatter(index)
        if late:
            for index in range(parts):
                for side in reversed(range(sides)):
                    complete(side, index)
                scatter(index)
        return scattered

    attn_sums = [start_scatter(pieces_of(attn_parts, index)) for index in range(parts)]
    attn_outs, resids, saved = [], [], {}

    def resid_rows(index, token):
        attn_out = finish_scatter_rows(attn_sums[index], token)
        rstd_a = lax.rsqrt(jnp.mean(attn_out * attn_out, axis=1, keepdims=True) + epsilon)
        attn_outs.append((attn_out, rstd_a))
        resids.append(part_of(tokens, index).astype(jnp.float32) + attn_out * rstd_a * attn_gain)
        return resids[-1].astype(jnp.bfloat16)

    def feed_forward(key, piece, token):
        gate, up_part, hidden_b = hidden_units(after(token, piece), gate_full, up_full)
        saved[key] = (piece, gate, up_part, hidden_b)
        return (hidden_b,)

    def feed_down(hidden_b, token):
        return sum_products([after(token, hidden_b)], [down_full])

    upstream_turn = start_turn(after(attn_parts, upstream))
    mlp_sums = pass_through(resid_rows, feed_forward, feed_down, True)
    token, upstream_turn = lax.optimization_barrier((token, upstream_turn))
    upstream = finish_turn(*upstream_turn)
    layer_outs, gain_parts, grads_f, back = [], [], [], {}

    def d_mlp_rows(index, token):
        mlp_out = finish_scatter_rows(mlp_sums[index], token)
        rstd_m = lax.rsqrt(jnp.mean(mlp_out * mlp_out, axis=1, keepdims=True) + epsilon)
        normed_m = mlp_out * rstd_m
        layer_outs.append((resids[index] + normed_m * ffn_gain).astype(jnp.bfloat16))
        grads_f.append(part_of(upstream, index).astype(jnp.float32))
        gain_parts.append(jnp.sum(grads_f[index] * normed_m, axis=0))
        return rms_back(mlp_out, rstd_m, ffn_gain, grads_f[index]).astype(jnp.bfloat16)

    def feed_back(key, piece, token):
        _, gate, up_part, _ = saved[key]
        d_gate_b, d_up_b = hidden_grads(after(token, piece), down_full, gate, up_part)
        back[key] = (piece, d_gate_b, d_up_b)
        return d_gate_b, d_up_b

    def feed_up(d_gate_b, d_up_b, token):
        return sum_products([after(token, d_gate_b), d_up_b], [gate_full, up_full])

    weight_grads = []

    def first_weight_grad(near, far, token):
        grads = [piece for index in range(parts) for piece in (near[index], far[index])]
        weight_grads.append(weight_grad(after(token, grads), [saved[key][3] for key in sorted(saved)]))
        return weight_grads[0]

    resid_sums = pass_through(d_mlp_rows, feed_back, feed_up, False, first_weight_grad)
    layer_out = jnp.concatenate(layer_outs, axis=0)
    keys = sorted(saved)
    ffn_gain_part = sum(gain_parts)
    attn_gain_part = 0.0
    d_resids, gathered, near_pieces = [], [], []
    operands = [
        ([back[key][0] for key in keys], [saved[key][3] for key in keys]),
        ([saved[key][0] for key in keys], [back[key][1] for key in keys]),
        ([saved[key][0] for key in keys], [back[key][2] for key in keys]),
    ]

    def next_weight_grad(token):
        left, right = operands[len(weight_grads)]
        left, right = after(token, (left, right))
        weight_grads.append(weight_grad(left, right))
        return weight_grads[-1]

    for index in range(parts):
        terms = resid_sums[index]
        if index == 0:
            d_sums = finish_scatter_rows(terms, token)
        else:
            last, weight_grads[-1] = lax.optimization_barrier((terms[-1], weight_grads[-1]))
            d_sums = finish_scatter_rows([*terms[:-1], last], None)
        attn_out, rstd_a = attn_outs[index]
        d_resid = grads_f[index] + d_sums
        d_resids.append(d_resid)
        attn_gain_part = attn_gain_part + jnp.sum(d_resid * attn_out * rstd_a, axis=0)
        d_attn_b = rms_back(attn_out, rstd_a, attn_gain, d_resid).astype(jnp.bfloat16)
        if sides == 2:
            near_pieces.append([d_attn_b, swap(d_attn_b, "core")])
            gathered.append((None, swap(d_attn_b, "tl")))
        else:
            gathered.append(start_gather(d_attn_b))
        token = next_weight_grad((d_attn_b, token))
    far_pieces = []
    for index in range(parts):
        if sides == 2:
            far, weight_grads[-1] = lax.optimization_barrier((gathered[index][1], weight_grads[-1]))
            far_pieces.append([far, swap(far, "core")])
            token = far
        if len(weight_grads) < 3:
            token = next_weight_grad(token)
    while len(weight_grads) < 3:
        token = next_weight_grad(token)
    down_grad, gate_grad, up_grad = weight_grads
    d_attn_pieces = []
    for index in range(parts):
        if sides == 2:
            d_attn_pieces += [*near_pieces[index], *far_pieces[index]]
        else:
            d_attn_pieces.append(gathered[index][0])
    d_resid = jnp.concatenate(d_resids, axis=0)
    out_total = weight_grad(d_attn_pieces, [attn_given])
    d_packed = pick_products(perm_place, d_attn_pieces, out_full)
    down_split = start_split(scatter_pair(down_grad))
    gate_sum, up_sum = scatter_pair(gate_grad), scatter_pair(up_grad)
    layer_turn = start_turn(layer_out)
    d_packed, out_total = lax.optimization_barrier((d_packed, out_total))
    d_q_rot, d_k_rot, d_v = attention_backward(
        q_b, k_b, v_b, d_packed, attn_f, logs, starts[None], high_block
    )
    d_q_rot, down_split, layer_turn = lax.optimization_barrier((d_q_rot, down_split, layer_turn))
    gate_split = start_split(after(d_q_rot, gate_sum))
    d_q_norm, d_k_norm, dots, q_parts, k_parts = norm_grads(
        d_q_rot, d_k_rot, raw, squares, gain_q, gain_k, cosine, sine
    )
    q_gain_part, k_gain_part = jnp.sum(q_parts, axis=0), jnp.sum(k_parts, axis=0)
    dots = sum_over(dots, RANK)
    d_qkv_b = raw_grads(d_q_norm, d_k_norm, d_v, raw, squares, dots, gain_q, gain_k)
    qkv_totals = stacked_weight_grad(packed, d_qkv_b, 3)
    gate_last, _ = lax.optimization_barrier((gate_split[1:], d_qkv_b))
    gate_split = (gate_split[0], *gate_last)
    up_split = start_split(after((d_qkv_b, gate_last), up_sum))
    _, input_parts = give_back(perm_place, d_qkv_b, qkv_full)
    down_shard, layer_out = finish_split(*down_split).T, finish_turn(*layer_turn)
    qkv_totals, down_shard, layer_out = lax.optimization_barrier((qkv_totals, down_shard, layer_out))
    input_parts, gate_split, up_split = lax.optimization_barrier((input_parts, gate_split, up_split))
    gate_shard, up_shard = finish_split(*gate_split), finish_split(*up_split)

    def placed(part_sum):
        return lax.dynamic_update_slice_in_dim(
            jnp.zeros((D,), jnp.float32), part_sum, rank * local_width, 0
        )

    gains = jnp.stack(
        [placed(q_gain_part), placed(k_gain_part), attn_gain_part, ffn_gain_part]
        + [jnp.zeros((D,), jnp.float32)] * 4
    )
    tokens_grad, gain_grads, out_shard, query_shard, key_shard, value_shard = leave(
        input_parts,
        d_resid,
        gains,
        [
            (out_total, [local_width], False),
            (qkv_totals, [local_width], False),
        ],
    )

    return (
        layer_out,
        tokens_grad,
        query_shard,
        key_shard,
        value_shard,
        out_shard.T,
        gate_shard,
        up_shard,
        down_shard,
        gain_grads[0],
        gain_grads[1],
        gain_grads[2],
        gain_grads[3],
    )


def solution(mesh):
    dp, tensor = mesh.shape["dp"], mesh.shape["tensor"]
    fine = Mesh(mesh.devices.reshape(dp // 4, 2, 2, 2, tensor // 2), DP + TENSOR)
    rows, weight, weight_out = P(DP + TENSOR, None), P(DP, TENSOR), P(TENSOR, DP)
    return jax.shard_map(
        per_device,
        mesh=fine,
        in_specs=(rows, rows, P(DP, None), P(DP, None))
        + (weight,) * 3
        + (weight_out, weight, weight, weight_out)
        + (P(),) * 4,
        out_specs=(rows, rows)
        + (weight,) * 3
        + (weight_out, weight, weight, weight_out)
        + (P(),) * 4,
        check_vma=False,
    )
```
